32 devices in a mesh: rel: 4 (over y, x), ent: 8 (over z, core).
Axes of the slice: x: 2, y: 2, z: 4, core: 2. Of those that a mesh axis runs over, the one named last changes fastest.
Arguments:
- ent_table: float32 [16384, 400], P('ent'), may hold values from -0.3 to 0.3
- entity_first_moment: float32 [16384, 400], P('ent'), may hold values from -2.037372e-09 to 2.037372e-09
- ent_v: float32 [16384, 400], P('ent'), may hold values from 2.144052e-20 to 8.576208e-20
- rel_table: float32 [3, 6400, 400], P(None, ('rel', 'ent')), may hold values from -0.3 to 0.3
- relation_first_moment: float32 [3, 6400, 400], P(None, ('rel', 'ent')), may hold values from -2.037372e-09 to 2.037372e-09
- rel_v: float32 [3, 6400, 400], P(None, ('rel', 'ent')), may hold values from 2.144052e-20 to 8.576208e-20
- src_ids: int32 [4, 8, 8, 1280], P('rel', 'ent'), may hold values from 0 to 2047
- rel_ids: int32 [4, 8, 8, 1280], P('rel', 'ent'), may hold values from 0 to 1599
- dst_ids: int32 [4, 8, 8, 1280], P('rel', 'ent'), may hold values from 0 to 2047
- neg_ids: int32 [4, 8, 8, 1000], P('rel', 'ent'), may hold values from 0 to 2047
- bucket_counts: int32 [4, 8, 8], P('rel', 'ent'), may hold values from 256 to 1280, as said below
Outputs:
- loss_sum: float32 [], replicated
- edge_count: float32 [], replicated
- grad_norm: float32 [], replicated
- new_ent: float32 [16384, 400], P('ent')
- new_ent_m: float32 [16384, 400], P('ent')
- new_ent_v: float32 [16384, 400], P('ent')
- ent_copy: bfloat16 [16384, 400], P('ent')
- new_rel: float32 [3, 6400, 400], P(None, ('rel', 'ent'))
- new_rel_m: float32 [3, 6400, 400], P(None, ('rel', 'ent'))
- new_rel_v: float32 [3, 6400, 400], P(None, ('rel', 'ent'))
- rel_copy: bfloat16 [3, 6400, 400], P(None, ('rel', 'ent'))
The draws below stay inside these ranges and needn't reach their ends.
Inputs may be any that keep to these rules, and one draw needn't show every extreme that they name: `bucket_counts`: each sender's row of 8 buckets holds one bucket filled to 1280.
All inputs are finite; a program needn't handle non-finite values.
Results may differ from the reference program's by a relative error of at most 0.0034.
Values may be sent and summed in bfloat16 or wider, within the bound.
A program may use at most 512 MiB of HBM per device.

```python
import math
import jax
import jax.numpy as jnp
from jax import lax

EMBED_WIDTH = 400
ENT_DEV = 2048
REL_DEV = 200
CAP = 1280
NEG = 1000
STEP = 10
ENTITY_TOTAL = 16384
RELATION_TOTAL = 6400
EDGE_SLOTS = 327680
PARAMETER_TOTAL = 14233600
N_REL = 4
N_ENT = 8


def draw_bucket_counts(key, part):
    key = jax.random.fold_in(key, 7)
    first, second = jax.random.split(key)
    base = jax.random.randint(first, (N_REL, N_ENT, N_ENT), CAP // 5, CAP + 1)
    filled = jax.random.randint(second, (N_REL, N_ENT, 1), 0, N_ENT)
    return jnp.where(jnp.arange(N_ENT)[None, None, :] == filled, CAP, base).astype(jnp.int32)


def touch_ends(values, key, low, top_value):
    longest = values.shape.index(max(values.shape))
    spots = []
    for shift in (0, 1):
        where = [jax.random.randint(jax.random.fold_in(key, axis), (), 0, length) for axis, length in enumerate(values.shape)]
        where[longest] = (where[longest] + shift) % values.shape[longest]
        spots.append(tuple(where))
    return values.at[spots[0]].set(low).at[spots[1]].set(top_value)


def steps_of(own_key, dims, cuts, smallest, largest):
    level = 1.0
    for position, blocks in cuts:
        heights = jax.random.uniform(jax.random.fold_in(jax.random.fold_in(own_key, 6), position), (blocks,), jnp.float32, smallest / len(cuts), largest / len(cuts))
        level = level * jnp.repeat(jnp.exp(heights), dims[position] // blocks).reshape((-1,) + (1,) * (len(dims) - 1 - position))
    return level


def noise(rng, shape, deviation, bound, shards=(), kind=jnp.bfloat16):
    entries = deviation * jax.random.normal(rng, shape, jnp.float32)
    if shards:
        entries = entries * steps_of(rng, shape, shards, -0.22, 0.18)
    return jnp.clip(entries, -bound, bound).astype(kind)


def setup_inputs(seed: int = 0) -> dict:
    arg_keys = jax.random.split(jax.random.key(seed), 12)
    ent_table = noise(arg_keys[0], (ENTITY_TOTAL, EMBED_WIDTH), 0.05, 0.3, ((0, 8),), jnp.float32)
    entity_first_moment = noise(arg_keys[1], (ENTITY_TOTAL, EMBED_WIDTH), (0.0011 * (EDGE_SLOTS * PARAMETER_TOTAL) ** -0.5), 2.037372048846464e-09, ((0, 8),), jnp.float32)
    ent_v = jnp.clip(jnp.exp(math.log(8.576207944714937e-20) - 1.3862944 * jax.random.uniform(arg_keys[2], (ENTITY_TOTAL, EMBED_WIDTH), jnp.float32) ** steps_of(arg_keys[2], (ENTITY_TOTAL, EMBED_WIDTH), ((0, 8),), -0.2, 0.2)), 2.1440519861787343e-20, 8.576207944714937e-20)
    rel_table = noise(arg_keys[3], (3, RELATION_TOTAL, EMBED_WIDTH), 0.05, 0.3, ((1, 32),), jnp.float32)
    relation_first_moment = noise(arg_keys[4], (3, RELATION_TOTAL, EMBED_WIDTH), (0.0011 * (EDGE_SLOTS * PARAMETER_TOTAL) ** -0.5), 2.037372048846464e-09, ((1, 32),), jnp.float32)
    rel_v = jnp.clip(jnp.exp(math.log(8.576207944714937e-20) - 1.3862944 * jax.random.uniform(arg_keys[5], (3, RELATION_TOTAL, EMBED_WIDTH), jnp.float32) ** steps_of(arg_keys[5], (3, RELATION_TOTAL, EMBED_WIDTH), ((1, 32),), -0.2, 0.2)), 2.1440519861787343e-20, 8.576207944714937e-20)
    src_ids = touch_ends(jax.random.randint(arg_keys[6], (N_REL, N_ENT, N_ENT, CAP), 0, ENT_DEV), jax.random.fold_in(arg_keys[6], 1), 0, ENT_DEV - 1).astype(jnp.int32)
    rel_ids = touch_ends(jax.random.randint(arg_keys[7], (N_REL, N_ENT, N_ENT, CAP), 0, REL_DEV * N_ENT), jax.random.fold_in(arg_keys[7], 1), 0, (REL_DEV * N_ENT) - 1).astype(jnp.int32)
    dst_ids = touch_ends(jax.random.randint(arg_keys[8], (N_REL, N_ENT, N_ENT, CAP), 0, ENT_DEV), jax.random.fold_in(arg_keys[8], 1), 0, ENT_DEV - 1).astype(jnp.int32)
    neg_ids = touch_ends(jax.random.randint(arg_keys[9], (N_REL, N_ENT, N_ENT, NEG), 0, ENT_DEV), jax.random.fold_in(arg_keys[9], 1), 0, ENT_DEV - 1).astype(jnp.int32)
    bucket_counts = draw_bucket_counts(jax.random.fold_in(arg_keys[11], 71), 0)
    return dict(ent_table=ent_table, entity_first_moment=entity_first_moment, ent_v=ent_v, rel_table=rel_table, relation_first_moment=relation_first_moment, rel_v=rel_v, src_ids=src_ids, rel_ids=rel_ids, dst_ids=dst_ids, neg_ids=neg_ids, bucket_counts=bucket_counts)


@jax.custom_vjp
def low(v):
    return lax.optimization_barrier(v.astype(jnp.bfloat16)).astype(jnp.float32)

@jax.custom_vjp
def low_back(v):
    return v

def low_keep(v):
    return (low(v), None)

def low_pass(kept, grad):
    return (grad,)

def back_keep(v):
    return (v, None)

def back_low(kept, grad):
    return (low(grad),)
low.defvjp(low_keep, low_pass)
low_back.defvjp(back_keep, back_low)
margin = 2.5
beta_one = 0.9
beta_two = 0.999
learn_rate = 0.05
decay_rate = 0.01
epsilon = 1e-16

def score_block(hidden, target, negative, live):
    diff = hidden - target
    pos_dist = jnp.sqrt(lax.optimization_barrier(jnp.sum(diff * diff, -1)) + 1.0)
    prod = low_back(jnp.einsum('ekd,end->ekn', hidden, negative, precision=lax.Precision.HIGHEST))
    sq = lax.optimization_barrier(jnp.sum(hidden * hidden, -1))[..., None] + lax.optimization_barrier(jnp.sum(negative * negative, -1))[:, None, :] - 2.0 * prod
    neg_dist = jnp.sqrt(sq + 1.0)
    per_edge = jax.nn.softplus(pos_dist - margin) + lax.optimization_barrier(jnp.mean(jax.nn.softplus(margin - neg_dist), -1))
    return jnp.sum(live * per_edge)

def adamw(weight, moment, second, grad):
    moment = beta_one * moment + (1.0 - beta_one) * grad
    second = beta_two * second + (1.0 - beta_two) * grad * grad
    m_hat = moment / (1.0 - beta_one ** STEP)
    v_hat = second / (1.0 - beta_two ** STEP)
    weight = weight - learn_rate * (m_hat / (jnp.sqrt(v_hat) + epsilon) + decay_rate * weight)
    return (weight, moment, second)

def reference(ent_table, entity_first_moment, ent_v, rel_table, relation_first_moment, rel_v, src_ids, rel_ids, dst_ids, neg_ids, bucket_counts):
    nrel, nent, _, cap = src_ids.shape
    entd = ent_table.shape[0] // nent
    group = rel_table.shape[1] // nrel
    width = ent_table.shape[1]
    mask = (jnp.arange(cap, dtype=jnp.int32)[None, None, None, :] < bucket_counts[..., None]).astype(jnp.float32)
    count = jnp.sum(mask)
    src_glob = src_ids + (jnp.arange(nent, dtype=jnp.int32) * entd)[None, :, None, None]
    rel_glob = rel_ids + (jnp.arange(nrel, dtype=jnp.int32) * group)[:, None, None, None]
    mask_in = mask.transpose(0, 2, 1, 3).reshape(nrel * nent, nent, cap)
    dst_in = dst_ids.transpose(0, 2, 1, 3).reshape(nrel * nent, nent, cap)
    neg_in = neg_ids.reshape(nrel * nent, nent, neg_ids.shape[3])
    owner = jnp.tile(jnp.arange(nent, dtype=jnp.int32), nrel)

    def forward(ent, rel):
        ent_low = low(ent)
        rel_low = low(rel)
        hidden = ent_low[src_glob] + rel_low[0][rel_glob] + rel_low[1][rel_glob] + rel_low[2][rel_glob]
        hidden = low_back(low(hidden))
        hidden = hidden.transpose(0, 2, 1, 3, 4).reshape(nrel * nent, nent, cap, width)

        def block(args):
            hid, dst, neg, live, index = args
            part = lax.dynamic_slice_in_dim(ent_low, index * entd, entd, 0)
            return score_block(hid, part[dst], part[neg], live)
        per_block = lax.map(jax.checkpoint(block), (hidden, dst_in, neg_in, mask_in, owner))
        return jnp.sum(per_block)
    loss_sum, pull = jax.vjp(forward, ent_table, rel_table)
    g_ent, g_rel = pull(1.0 / count)
    grad_norm = jnp.sqrt(jnp.sum(g_ent * g_ent) + jnp.sum(g_rel * g_rel))
    clip = 0.01 * lax.rsqrt(jnp.float32(nrel * nent * nent * cap))
    scale = jnp.minimum(1.0, clip / grad_norm)
    new_ent, new_ent_m, new_ent_v = adamw(ent_table, entity_first_moment, ent_v, scale * g_ent)
    new_rel, new_rel_m, new_rel_v = adamw(rel_table, relation_first_moment, rel_v, scale * g_rel)
    return (loss_sum, count, grad_norm, new_ent, new_ent_m, new_ent_v, new_ent.astype(jnp.bfloat16), new_rel, new_rel_m, new_rel_v, new_rel.astype(jnp.bfloat16))
```

```python
import functools
import math

import jax
import jax.numpy as jnp
from jax import lax
from jax.experimental import pallas as pl
from jax.experimental.pallas import tpu as pltpu
from jax.sharding import PartitionSpec as P

STEP = 10
f32 = jnp.float32
bf16 = jnp.bfloat16
i32 = jnp.int32
MESH = pl.DeviceIdType.MESH


margin = 2.5
beta_one = 0.9
beta_two = 0.999
learn_rate = 0.05
decay_rate = 0.01
epsilon = 1e-16


def shortened(array):
    return jax.tree.map(lambda a: a.astype(jnp.bfloat16) if a.dtype == jnp.float32 else a, array)


def adamw(weight, moment, second, grad):
    moment = beta_one * moment + (1.0 - beta_one) * grad
    second = beta_two * second + (1.0 - beta_two) * grad * grad
    m_hat = moment / (1.0 - beta_one**STEP)
    v_hat = second / (1.0 - beta_two**STEP)
    weight = weight - learn_rate * (m_hat / (jnp.sqrt(v_hat) + epsilon) + decay_rate * weight)
    return (weight, moment, second)


def general_body(
    ent_table,
    entity_first_moment,
    ent_v,
    rel_table,
    relation_first_moment,
    rel_v,
    src_ids,
    rel_ids,
    dst_ids,
    neg_ids,
    bucket_counts,
):
    parts = src_ids.shape[2]
    slots = src_ids.shape[3]
    width = ent_table.shape[1]
    negcount = neg_ids.shape[3]
    clip_level = 0.01 / math.sqrt(lax.axis_size("rel") * lax.axis_size("ent") * parts * slots)
    ent_low = ent_table.astype(jnp.bfloat16)
    layers = lax.all_gather(rel_table.astype(jnp.bfloat16), "ent", axis=1, tiled=True)
    rel_sum = (
        layers[0].astype(jnp.float32)
        + layers[1].astype(jnp.float32)
        + layers[2].astype(jnp.float32)
    )
    sources = src_ids[0, 0]
    relation = rel_ids[0, 0]
    counts = bucket_counts[0, 0]
    hidden = ent_low[sources].astype(jnp.float32) + rel_sum[relation]
    total = lax.psum(jnp.sum(counts).astype(jnp.float32), ("rel", "ent"))
    arrived, dst_in, count_in = (
        lax.all_to_all(hidden.astype(jnp.bfloat16), "ent", split_axis=0, concat_axis=0, tiled=True),
        lax.all_to_all(dst_ids[0, 0], "ent", split_axis=0, concat_axis=0, tiled=True),
        lax.all_to_all(counts[:, None], "ent", split_axis=0, concat_axis=0, tiled=True),
    )
    live = (jnp.arange(slots, dtype=jnp.int32)[None, :] < count_in).astype(jnp.float32)
    negatives = neg_ids[0, 0]

    def block(args):
        hid, dst, neg, alive = args
        weight = alive / total
        hid_f = hid.astype(jnp.float32)
        diff = hid_f - ent_low[dst].astype(jnp.float32)
        pos_dist = jnp.sqrt(jnp.sum(diff * diff, -1) + 1.0)
        rows = ent_low[neg]
        rows_f = rows.astype(jnp.float32)
        prod = lax.dot_general(
            hid, rows, (((1,), (1,)), ((), ())), preferred_element_type=jnp.float32
        )
        sq = (
            jnp.sum(hid_f * hid_f, -1)[:, None] + jnp.sum(rows_f * rows_f, -1)[None, :] - 2.0 * prod
        )
        neg_dist = jnp.sqrt(sq + 1.0)
        per_edge = jax.nn.softplus(pos_dist - margin) + jnp.mean(
            jax.nn.softplus(margin - neg_dist), -1
        )
        loss = jnp.sum(alive * per_edge)
        g_pos = weight * jax.nn.sigmoid(pos_dist - margin)
        g_diff = (g_pos / pos_dist)[:, None] * diff
        g_sq = -(weight[:, None] / negcount) * jax.nn.sigmoid(margin - neg_dist) / (2.0 * neg_dist)
        g_prod = (-2.0 * g_sq).astype(jnp.bfloat16)
        g_hid = (
            g_diff
            + 2.0 * hid_f * jnp.sum(g_sq, 1)[:, None]
            + jnp.dot(g_prod, rows, preferred_element_type=jnp.float32)
        )
        g_rows = 2.0 * rows_f * jnp.sum(g_sq, 0)[:, None] + lax.dot_general(
            g_prod, hid, (((0,), (0,)), ((), ())), preferred_element_type=jnp.float32
        )
        return (loss, g_hid.astype(jnp.bfloat16), -g_diff, g_rows)

    losses, back, g_target, g_negative = lax.map(
        block, (arrived, dst_in, negatives, live), batch_size=min(4, parts)
    )
    returned = (
        jax.tree.map(
            lambda part, own: part.astype(own.dtype),
            lax.all_to_all(shortened(back), "ent", split_axis=0, concat_axis=0, tiled=True),
            back,
        )
        .reshape(-1, width)
        .astype(jnp.float32)
    )
    ent_grad = jnp.zeros(ent_table.shape, jnp.float32)
    ent_grad = ent_grad.at[dst_in.reshape(-1)].add(g_target.reshape(-1, width))
    ent_grad = ent_grad.at[negatives.reshape(-1)].add(g_negative.reshape(-1, width))
    ent_grad = ent_grad.at[sources.reshape(-1)].add(returned)
    ent_grad = lax.psum(ent_grad, "rel")
    rel_local = jnp.zeros(rel_sum.shape, jnp.float32).at[relation.reshape(-1)].add(returned)
    rel_grad = lax.psum_scatter(rel_local, "ent", scatter_dimension=0, tiled=True)
    own_squares = jnp.where(
        lax.axis_index("rel") == 0, jnp.sum(ent_grad * ent_grad), 0.0
    ) + 3.0 * jnp.sum(rel_grad * rel_grad)
    squares, loss_sum = lax.psum((own_squares, jnp.sum(losses)), ("rel", "ent"))
    grad_norm = jnp.sqrt(squares)
    scale = jnp.minimum(1.0, clip_level / grad_norm)
    new_ent, new_ent_m, new_ent_v = adamw(ent_table, entity_first_moment, ent_v, scale * ent_grad)
    new_rel, new_rel_m, new_rel_v = adamw(
        rel_table, relation_first_moment, rel_v, scale * rel_grad[None]
    )
    return (
        loss_sum,
        total,
        grad_norm,
        new_ent,
        new_ent_m,
        new_ent_v,
        new_ent.astype(jnp.bfloat16),
        new_rel,
        new_rel_m,
        new_rel_v,
        new_rel.astype(jnp.bfloat16),
    )


KT1=256
RP=256

def split3(x):
    hi=x.astype(bf16).astype(f32); r=x-hi
    mid=r.astype(bf16).astype(f32); lo=r-mid
    return hi,mid,lo

def place():
    r=lax.axis_index("rel"); e=lax.axis_index("ent")
    z=lax.div(e,2); k=lax.rem(e,2)
    xn=r+1-2*lax.rem(r,2)
    yn=lax.rem(r+2,4)
    return r,z,k,xn,yn

def gather_kernel(et_ref, rt_ref, src_ref, rid_ref, neg_ref,
                  tab_ref, h_ref, negout_ref,
                  tb, rall, eh, hb, lsem, hsem, zs, zr, xs, xr, ys, yr, dxs, dxr, dys, dyr, cs, cr, rs, rr, rcs, rcr, ns, nr):
    width,ents=et_ref.shape
    nz=4; parts=8
    CK=ents//4
    cap=src_ref.shape[1]
    c,z,k,xn,yn=place()
    e=2*z+k
    half=208
    sib=2*z+1-k
    def dev(rel,ent): return (rel,ent)
    bar=pltpu.get_barrier_semaphore()
    for d in range(1,parts):
        pl.semaphore_signal(bar,inc=1,device_id=dev(c,lax.rem(e+d,parts)),device_id_type=MESH)
    pl.semaphore_signal(bar,inc=1,device_id=dev(xn,e),device_id_type=MESH)
    pl.semaphore_signal(bar,inc=1,device_id=dev(yn,e),device_id_type=MESH)
    tb[...]=et_ref[...].astype(bf16)
    rsum=(rt_ref[0]+rt_ref[1])+rt_ref[2] if False else (rt_ref[0].astype(bf16).astype(f32)+rt_ref[1].astype(bf16).astype(f32)+rt_ref[2].astype(bf16).astype(f32))
    rsum=jnp.concatenate([rsum,jnp.zeros((RP-rsum.shape[0],width),f32)],0)
    rall[e]=rsum.T.astype(bf16)
    pl.semaphore_wait(bar,parts+1)
    def rc(src,dst,s,r,to):
        return pltpu.make_async_remote_copy(src_ref=src,dst_ref=dst,send_sem=s,recv_sem=r,device_id=to,device_id_type=MESH)
    lanes=pl.ds(pl.multiple_of(c*CK,CK),CK)
    lanes_x=pl.ds(pl.multiple_of(xn*CK,CK),CK)
    lanes_y=pl.ds(pl.multiple_of(yn*CK,CK),CK)
    def rel_copy(zz,o):
        return rc(rall.at[2*o+k],rall.at[2*o+k],rs.at[zz],rr.at[o],dev(c,2*zz+k))
    def rel_sib(o,kk):
        return rc(rall.at[2*o+kk],rall.at[2*o+kk],rcs.at[o],rcr.at[o],dev(c,sib))
    for dz in range(1,nz):
        rel_copy(lax.rem(z+dz,nz),z).start()
    rel_sib(z,k).start()
    def neg_copy(to,own):
        return rc(neg_ref.at[to],negout_ref.at[own],ns.at[to],nr.at[own],dev(c,to))
    for d in range(1,parts):
        neg_copy(lax.rem(e+d,parts),e).start()
    own_neg=pltpu.make_async_copy(neg_ref.at[e],negout_ref.at[e],lsem.at[1])
    own_neg.start()
    def up(o,own):
        src=tb.at[:,lanes] if own else tab_ref.at[2*o+k,:,lanes]
        return rc(src,tab_ref.at[2*o+k,:,lanes],zs.at[0,o],zr.at[o],dev(c,2*(z+1)+k))
    def down(o,own):
        src=tb.at[:,lanes] if own else tab_ref.at[2*o+k,:,lanes]
        return rc(src,tab_ref.at[2*o+k,:,lanes],zs.at[1,o],zr.at[o],dev(c,2*(z-1)+k))
    @pl.when(z<nz-1)
    def _(): up(z,True).start()
    @pl.when(z>0)
    def _(): down(z,True).start()
    own_tab=pltpu.make_async_copy(tb,tab_ref.at[e],lsem.at[0])
    own_tab.start()
    def core_copy(o,kk,own):
        src=tb if own else tab_ref.at[2*o+kk]
        return rc(src,tab_ref.at[2*o+kk],cs.at[o],cr.at[o],dev(c,sib))
    core_copy(z,k,True).start()
    def xcopy(o,l): return rc(tab_ref.at[2*o+k,:,l],tab_ref.at[2*o+k,:,l],xs.at[o],xr.at[o],dev(xn,e))
    def ycopy(o,l): return rc(tab_ref.at[2*o+k,:,l],tab_ref.at[2*o+k,:,l],ys.at[o],yr.at[o],dev(yn,e))
    def dycopy(o,l):
        v=tab_ref.at[2*o+k,0:half,l]
        return rc(v,v,dys.at[o],dyr.at[o],dev(yn,e))
    def dxcopy(o,l):
        v=tab_ref.at[2*o+k,half:width,l]
        return rc(v,v,dxs.at[o],dxr.at[o],dev(xn,e))
    def sides(dist,fn):
        @pl.when(z>=dist)
        def _(): fn(z-dist,True)
        @pl.when(z+dist<nz)
        def _(): fn(z+dist,False)
    def arrive(dist):
        def fn(o,below):
            rc(tb.at[:,lanes],tab_ref.at[2*o+k,:,lanes],zs.at[0,o],zr.at[o],dev(c,e)).wait_recv()
            if below:
                @pl.when(z<nz-1)
                def _(): up(o,False).start()
            else:
                @pl.when(z>0)
                def _(): down(o,False).start()
            xcopy(o,lanes).start()
            ycopy(o,lanes).start()
        sides(dist,fn)
    def cross(dist):
        def fn(o,below):
            xcopy(o,lanes_x).wait_recv()
            dycopy(o,lanes_x).start()
            ycopy(o,lanes_y).wait_recv()
            dxcopy(o,lanes_y).start()
        sides(dist,fn)
    def whole(dist):
        def fn(o,below):
            l_d=pl.ds(pl.multiple_of((3-c)*CK,CK),CK)
            dycopy(o,l_d).wait_recv()
            dxcopy(o,l_d).wait_recv()
            core_copy(o,k,False).start()
        sides(dist,fn)
    def onehot(ids):
        return jnp.where(lax.broadcasted_iota(i32,(ents,KT1),0)==ids,1.0,0.0).astype(bf16)
    nt=cap//KT1
    def src_slot(b):
        def tile(t,_):
            l=pl.ds(pl.multiple_of(t*KT1,KT1),KT1)
            eh[b,:,l]=jnp.dot(tb[...],onehot(src_ref[b:b+1,l]),preferred_element_type=f32).astype(bf16)
            return 0
        lax.fori_loop(0,nt,tile,0)
    def out_copy(b):
        return pltpu.make_async_copy(hb.at[b%2],h_ref.at[pl.ds(b*cap,cap),:],hsem.at[b%2])
    nrel=rt_ref.shape[1]
    def rel_slot(b):
        if b>=2: out_copy(b-2).wait()
        def tile(t,_):
            l=pl.ds(pl.multiple_of(t*KT1,KT1),KT1)
            q=rid_ref[b:b+1,l]
            g=jnp.floor((q.astype(f32)+0.5)*(1.0/nrel)).astype(i32)
            q=q+(RP-nrel)*g
            acc=eh[b,:,l].astype(f32)
            for g0 in range(0,parts):
                oh=jnp.where(lax.broadcasted_iota(i32,(RP,KT1),0)+RP*g0==q,1.0,0.0).astype(bf16)
                acc=acc+jnp.dot(rall[g0],oh,preferred_element_type=f32)
            hid=acc.astype(bf16)
            hf=hid.astype(f32)
            hi,mid,lo=split3(jnp.sum(hf*hf,0,keepdims=True))
            row=lax.broadcasted_iota(i32,(hb.shape[2]-width,KT1),0)
            ex=jnp.where(row==0,hi,jnp.where(row==1,mid,jnp.where(row==2,lo,jnp.where(row<6,1.0,0.0))))
            hb[b%2,pl.ds(pl.multiple_of(t*KT1,KT1),KT1),:]=jnp.concatenate([hf,ex],0).T.astype(bf16)
            return 0
        lax.fori_loop(0,nt,tile,0)
        out_copy(b).start()
    for b in range(4): src_slot(b)
    arrive(1)
    for b in range(4,6): src_slot(b)
    for dz in range(1,nz):
        o=lax.rem(z+dz,nz)
        rel_copy(z,o).wait_recv()
        rel_sib(o,k).start()
    arrive(2)
    cross(1)
    for b in range(6,8): src_slot(b)
    whole(1)
    for o in range(nz): rel_sib(o,1-k).wait_recv()
    arrive(3)
    rel_slot(0); rel_slot(1)
    cross(2)
    rel_slot(2); rel_slot(3)
    whole(2); cross(3)
    for b in range(4,8): rel_slot(b)
    whole(3)
    for o in range(nz): core_copy(o,1-k,False).wait_recv()
    core_copy(z,k,True).wait_send()
    for dist in range(1,nz):
        def fn(o,below):
            core_copy(o,k,False).wait_send()
            xcopy(o,lanes).wait_send(); ycopy(o,lanes).wait_send()
            dycopy(o,lanes_x).wait_send(); dxcopy(o,lanes_y).wait_send()
            if below:
                @pl.when(z<nz-1)
                def _(): up(o,False).wait_send()
            else:
                @pl.when(z>0)
                def _(): down(o,False).wait_send()
        sides(dist,fn)
    @pl.when(z<nz-1)
    def _(): up(z,True).wait_send()
    @pl.when(z>0)
    def _(): down(z,True).wait_send()
    for dz in range(1,nz):
        o=lax.rem(z+dz,nz)
        rel_copy(o,z).wait_send()
    for o in range(nz): rel_sib(o,k).wait_send()
    for d in range(1,parts):
        o=lax.rem(e+d,parts)
        neg_copy(o,e).wait_send()
        neg_copy(e,o).wait_recv()
    own_tab.wait(); own_neg.wait()
    out_copy(6).wait(); out_copy(7).wait()

def gather_call(et,rt,src,rid,negs):
    width,ents=et.shape
    parts,cap=src.shape
    D=pltpu.SemaphoreType.DMA
    V=pl.BlockSpec(memory_space=pltpu.VMEM); A=pl.BlockSpec(memory_space=pl.ANY)
    return pl.pallas_call(gather_kernel,name="k1_gather",
        in_specs=[V]*5,out_specs=[A,A,V],
        out_shape=[jax.ShapeDtypeStruct((parts,width,ents),bf16),jax.ShapeDtypeStruct((parts*cap,512),bf16),jax.ShapeDtypeStruct(negs.shape,i32)],
        scratch_shapes=[pltpu.VMEM((width,ents),bf16),pltpu.VMEM((parts,width,RP),bf16),pltpu.VMEM((parts,width,cap),bf16),pltpu.VMEM((2,cap,512),bf16),
            D((2,)),D((2,)),D((2,4)),D((4,)),D((4,)),D((4,)),D((4,)),D((4,)),D((4,)),D((4,)),D((4,)),D((4,)),D((4,)),D((4,)),D((4,)),D((4,)),D((4,)),D((4,)),D((8,)),D((8,))],
        compiler_params=pltpu.CompilerParams(collective_id=1,has_side_effects=True,vmem_limit_bytes=60<<20))(et,rt,src,rid,negs)


KT = 256
WA=416
def block_kernel(width, ents, negcount, CH,
                 counts_ref, h_ref, t_ref, dst_ref, neg_ref, gh_ref, g_ref, loss_ref,
                 ta_ref, tr_ref, acc_ref, crow_ref, s_ref):
    j=pl.program_id(0)
    wa=ta_ref.shape[0]
    count=counts_ref[j]
    tiles=lax.div(count+(KT-1),KT)
    t=t_ref[0]
    tf=t.astype(f32)
    norm=(jnp.sum(tf*tf,0,keepdims=True)+1.0)*0.25
    hi,mid,lo=split3(norm)
    ta_ref[0:width,:]=t*bf16(-0.5)
    sub=lax.broadcasted_iota(jnp.int32,(wa-width,ents),0)
    pad=jnp.where(sub<3,0.25,0.0)
    pad=jnp.where(sub==3,hi,pad)
    pad=jnp.where(sub==4,mid,pad)
    pad=jnp.where(sub==5,lo,pad)
    ta_ref[width:,:]=pad.astype(bf16)
    tcat=jnp.concatenate([t, jnp.where(sub==0,1.0,0.0).astype(bf16)],0)
    tr_ref[...]=tcat.T
    ids=neg_ref[0]
    nn=ids.shape[1]
    ohi=jnp.where(lax.broadcasted_iota(jnp.int32,(ents//128,nn),0)==lax.shift_right_arithmetic(ids,7),1.0,0.0).astype(bf16)
    olo=jnp.where(lax.broadcasted_iota(jnp.int32,(128,nn),0)==(ids&127),1.0,0.0).astype(bf16)
    c=lax.dot_general(ohi,olo,(((1,),(1,)),((),())),preferred_element_type=f32)*(1.0/negcount)
    for i in range(ents//128):
        crow_ref[0:1,128*i:128*(i+1)]=c[i:i+1,:]
    acc_ref[...]=jnp.zeros_like(acc_ref)
    gh_ref[...]=jnp.zeros_like(gh_ref)
    @pl.when(j==0)
    def _(): loss_ref[...]=jnp.zeros_like(loss_ref)
    first=jnp.logical_and(lax.broadcasted_iota(jnp.int32,(8,128),0)==0,lax.broadcasted_iota(jnp.int32,(8,128),1)==0)
    loss_ref[8:16,:]+=jnp.where(first,count.astype(f32),0.0)
    eye=lax.broadcasted_iota(jnp.int32,(KT,KT),0)==lax.broadcasted_iota(jnp.int32,(KT,KT),1)
    lanes=lax.broadcasted_iota(jnp.int32,(1,CH),1)
    nch=ents//CH
    def rows_of(kt): return pl.ds(pl.multiple_of(kt*KT,KT),KT)
    def live_of(kt): return (lax.broadcasted_iota(jnp.int32,(KT,1),0)+kt*KT)<count
    def idcol(kt):
        idr=dst_ref[0,pl.ds(kt,1),:].astype(f32)
        return jnp.sum(jnp.where(eye,idr,0.0),1,keepdims=True).astype(jnp.int32)
    def aug(kt):
        hb=h_ref[rows_of(kt),:]
        last=hb[:,width//128*128:wa].astype(f32)
        lane=lax.broadcasted_iota(jnp.int32,last.shape,1)+width//128*128
        last=jnp.where(jnp.logical_and(lane==width,jnp.logical_not(live_of(kt))),4e6,last)
        return jnp.concatenate([hb[:,:width//128*128],last.astype(bf16)],1)
    def sdot(ha,ci): return jnp.dot(ha,ta_ref[:,ci*CH:(ci+1)*CH],preferred_element_type=f32)
    def post(s,idc,ci,sp):
        es=jnp.where((idc-ci*CH)==lanes,s,0.0)
        for a in range(CH//128): sp=sp+es[:,128*a:128*(a+1)]
        s_ref[:,ci*CH:(ci+1)*CH]=s
        return sp
    def column(sp,kt):
        live=live_of(kt)
        sq=jnp.sum(sp,1,keepdims=True)*4.0
        rr=lax.rsqrt(sq)
        x=sq*rr-margin
        a=jnp.where(live,jax.nn.sigmoid(x)*rr,0.0)
        inva=jnp.where(live,1.0/a,0.0)
        pos=jnp.where(live,jnp.maximum(x,0.0)+jnp.log(1.0+jnp.exp(-jnp.abs(x))),0.0)
        p8=pos[0:8]
        for b in range(1,KT//8): p8+=pos[8*b:8*b+8]
        loss_ref[0:8,:]+=jnp.where(lax.broadcasted_iota(jnp.int32,(8,128),1)==0,p8,0.0)
        return a,inva
    ha=aug(0); idc=idcol(0); sp=jnp.zeros((KT,128),f32)
    for ci in range(nch): sp=post(sdot(ha,ci),idc,ci,sp)
    a0,i0=column(sp,0)
    def tile(kt,carry):
        rho,inva,idc=carry
        nk=jnp.minimum(kt+1,tiles-1)
        hb=h_ref[rows_of(kt),:]
        hf=hb[:,:width].astype(f32)
        hi,mid,lo=split3(rho)
        ex=lax.broadcasted_iota(jnp.int32,(KT,wa-width),1)
        pad=jnp.where(ex==0,hi,jnp.where(ex==1,mid,jnp.where(ex==2,lo,0.0)))
        hat=jnp.concatenate([(hf*rho),pad],1).astype(bf16).T
        ha=aug(nk); nidc=idcol(nk)
        gh=jnp.zeros((KT,wa),f32)
        sp=jnp.zeros((KT,128),f32)
        lsum=jnp.zeros((8,CH),f32)
        ss=[None]*nch; ms=[None]*nch
        ss[0]=sdot(ha,0)
        for ci in range(nch+1):
            if ci+1<nch: ss[ci+1]=sdot(ha,ci+1)
            if ci>=1:
                pc=slice((ci-1)*CH,ci*CH)
                gh+=jnp.dot(ms[ci-1],tr_ref[pc,:],preferred_element_type=f32)
                acc_ref[:,pc]+=jnp.dot(hat,ms[ci-1],preferred_element_type=f32)
            if ci<nch:
                cols=slice(ci*CH,(ci+1)*CH)
                s=s_ref[:,cols]
                r=lax.rsqrt(s)
                th=jnp.tanh(margin*0.5-s*r)
                mask=(idc-ci*CH)==lanes
                cr=crow_ref[0:1,cols]
                x=(cr*0.25*(1.0+th))*(r*inva)
                ms[ci]=(jnp.where(mask,1.0,0.0)-x).astype(bf16)
                o=1.0-th
                p=o[0:8]
                for b in range(1,KT//8): p=p*o[8*b:8*b+8]
                lsum+=(math.log(2.0)*(KT//8)-jnp.log(p))*cr
                sp=post(ss[ci],nidc,ci,sp)
        l8=lsum[:,0:128]
        for b in range(1,CH//128): l8+=lsum[:,128*b:128*(b+1)]
        loss_ref[0:8,:]+=l8
        out=(hf*gh[:,width:width+1]-gh[:,:width])*rho
        gh_ref[rows_of(kt),:width]=out.astype(bf16)
        live=kt+1<tiles
        na,ni=column(jnp.where(live,sp,1.0),jnp.where(live,nk,tiles))
        return na,ni,nidc
    lax.fori_loop(0,tiles,tile,(a0,i0,idc))
    g_ref[0]=tf*acc_ref[width:width+1,:]+tf*acc_ref[width+1:width+2,:]+tf*acc_ref[width+2:width+3,:]-acc_ref[0:width,:]

def run_blocks(h,tables,dst,neg,counts,negcount,CH=512,approx=True):
    parts,width,ents=tables.shape
    cap=h.shape[0]//parts
    wa=WA
    nn=neg.shape[-1]
    gs=pltpu.PrefetchScalarGridSpec(num_scalar_prefetch=1,grid=(parts,),
      in_specs=[pl.BlockSpec((cap,h.shape[1]),lambda j,c:(j,0)),
                pl.BlockSpec((1,width,ents),lambda j,c:(j,0,0)),
                pl.BlockSpec((1,cap//KT,KT),lambda j,c:(j,0,0)),
                pl.BlockSpec((1,1,nn),lambda j,c:(j,0,0))],
      out_specs=[pl.BlockSpec((cap,width),lambda j,c:(j,0)),
                 pl.BlockSpec((1,width,ents),lambda j,c:(j,0,0)),
                 pl.BlockSpec((16,128),lambda j,c:(0,0))],
      scratch_shapes=[pltpu.VMEM((wa,ents),bf16),pltpu.VMEM((ents,wa),bf16),
                      pltpu.VMEM((wa,ents),f32),pltpu.VMEM((8,ents),f32),pltpu.VMEM((KT,ents),f32)])
    return pl.pallas_call(functools.partial(block_kernel,width,ents,negcount,CH),grid_spec=gs,name="k2_blocks",
      out_shape=[jax.ShapeDtypeStruct((h.shape[0],width),bf16),jax.ShapeDtypeStruct(tables.shape,f32),jax.ShapeDtypeStruct((16,128),f32)],
      compiler_params=pltpu.CompilerParams(vmem_limit_bytes=60<<20,dimension_semantics=("arbitrary",)))(counts,h,tables,dst,neg)


HALF=208
BT=bf16
ZT=bf16
RT=f32

def reduce_kernel(g_ref, gh_ref, src_ref, rid_ref, sc_ref,
                  ge_ref, gr_ref, sco_ref,
                  pr, own, sacc, racc, sax, say, rax, ray, sbx, sby, rbx, rby, sz, rz, ghb, ght, rp, rsz, rzr, scb,
                  ps, prr, osem, gsem, axs, axr, ays, ayr, bxs, bxr, bys, byr, zs, zr, rps, rpr, rzs, rzrr, gxs, gxr, gys, gyr, gdxs, gdxr, gdys, gdyr, css, csr, czs, czr):
    parts,width,ents=g_ref.shape
    nz=4; CK=ents//4
    cap=src_ref.shape[1]
    nrel=gr_ref.shape[0]
    c,z,k,xn,yn=place()
    e=2*z+k; sib=2*z+1-k
    x=lax.rem(c,2); y=lax.div(c,2)
    bar=pltpu.get_barrier_semaphore()
    for to in ((c,sib),(xn,e),(yn,e))+tuple((c,lax.rem(e+2*d,parts)) for d in range(1,nz)):
        pl.semaphore_signal(bar,inc=1,device_id=to,device_id_type=MESH)
    pl.semaphore_wait(bar,nz+2)
    def rc(src,dst,s,r,to):
        return pltpu.make_async_remote_copy(src_ref=src,dst_ref=dst,send_sem=s,recv_sem=r,device_id=to,device_id_type=MESH)
    order=[lax.rem(z+1+i,nz) for i in range(nz)]
    def pair(i): return rc(g_ref.at[2*order[i]+1-k],pr.at[i],ps.at[i],prr.at[i],(c,sib))
    def load(i): return pltpu.make_async_copy(g_ref.at[2*order[i]+k],own.at[i%2],osem.at[i%2])
    for i in range(nz): pair(i).start()
    load(0).start(); load(1).start()
    def gload(b): return pltpu.make_async_copy(gh_ref.at[pl.ds(b*cap,cap),:],ghb.at[b%2],gsem.at[b%2])
    gload(0).start()
    def lane(ck,n=1): return pl.ds(pl.multiple_of(ck*CK,CK),n*CK)
    def ax(i): return rc(sax.at[i],rax.at[i],axs.at[i],axr.at[i],(xn,e))
    def ay(i): return rc(say.at[i],ray.at[i],ays.at[i],ayr.at[i],(yn,e))
    def bx(i): return rc(sbx.at[i],rbx.at[i],bxs.at[i],bxr.at[i],(xn,e))
    def by(i): return rc(sby.at[i],rby.at[i],bys.at[i],byr.at[i],(yn,e))
    def zc(i): return rc(sz.at[i],rz.at[i],zs.at[i],zr.at[i],(c,2*order[i]+k))
    RB=16
    def strips(lo,hi,fn):
        def it(t,_):
            fn(pl.ds(pl.multiple_of(lo+t*RB,RB),RB),pl.ds(pl.multiple_of(t*RB,RB),RB)); return 0
        lax.fori_loop(0,(hi-lo)//RB,it,0)
    xo=1-x; yo=1-y
    def stage0(i):
        pair(i).wait_recv()
        load(i).wait()
        def one(rows,rel,xfirst):
            v=pr[i,rows,:]+own[i%2,rows,:]
            if i==nz-1: v=v+sacc[rows,:]
            pr[i,rows,:]=v
        strips(0,HALF,lambda rows,rel: one(rows,rel,True))
        strips(HALF,width,lambda rows,rel: one(rows,rel,False))
        def sx(rows,rel):
            sax[i,rel,0:CK]=pr[i,rows,lane(xo)].astype(bf16)
            sax[i,rel,CK:]=pr[i,rows,lane(xo+2)].astype(bf16)
        strips(0,HALF,sx)
        ax(i).start()
        def sy(rows,rel):
            say[i,rel,:]=pr[i,rows,lane(2*yo,2)].astype(bf16)
        strips(HALF,width,sy)
        ay(i).start()
        if i+2<nz: load(i+2).start()
    def stageB(i):
        ax(i).wait_recv()
        def px(rows,rel):
            sby[i,rel,:]=(pr[i,rows,lane(x+2*yo)]+rax[i,rel,lane(yo)].astype(f32)).astype(BT)
            pr[i,rows,lane(c)]=pr[i,rows,lane(c)]+rax[i,rel,lane(y)].astype(f32)
        strips(0,HALF,px)
        by(i).start()
        ay(i).wait_recv()
        def py(rows,rel):
            sbx[i,rel,:]=(pr[i,rows,lane(2*y+xo)]+ray[i,rel,lane(xo)].astype(f32)).astype(BT)
            pr[i,rows,lane(c)]=pr[i,rows,lane(c)]+ray[i,rel,lane(x)].astype(f32)
        strips(HALF,width,py)
        bx(i).start()
    def stageZ(i):
        by(i).wait_recv(); bx(i).wait_recv()
        last=i==nz-1
        def one(buf):
            def f(rows,rel):
                v=pr[i,rows,lane(c)]+buf[i,rel,:].astype(f32)
                if last: ge_ref[rows,lane(c)]=v
                else: sz[i,rows,:]=v.astype(ZT)
            return f
        strips(0,HALF,one(rby)); strips(HALF,width,one(rbx))
        if not last: zc(i).start()
    def getblock(b):
        gload(b).wait()
        if b+1<parts: gload(b+1).start()
    EC=512
    def src_slot(b):
        ght[...]=ghb[b%2].T
        KT=256
        eye=lax.broadcasted_iota(i32,(KT,KT),0)==lax.broadcasted_iota(i32,(KT,KT),1)
        cols=[]
        for t in range(cap//KT):
            idr=src_ref[b:b+1,t*KT:(t+1)*KT].astype(f32)
            cols.append(jnp.sum(jnp.where(eye,idr,0.0),1,keepdims=True).astype(i32))
        idc=jnp.concatenate(cols,0)
        def chunk(t,_):
            l=pl.ds(pl.multiple_of(t*EC,EC),EC)
            oh=jnp.where(idc==lax.broadcasted_iota(i32,(1,EC),1)+t*EC,1.0,0.0).astype(bf16)
            d=jnp.dot(ght[...],oh,preferred_element_type=f32)
            if b==0: sacc[:,l]=d
            else: sacc[:,l]=sacc[:,l]+d
            return 0
        lax.fori_loop(0,ents//EC,chunk,0)
    QC=nrel*2
    def rel_slot(b):
        ids=rid_ref[b:b+1,:]
        def chunk(t,_):
            rows=pl.ds(pl.multiple_of(t*QC,8),QC)
            oh=jnp.where(lax.broadcasted_iota(i32,(QC,cap),0)+t*QC==ids,1.0,0.0).astype(bf16)
            d=jnp.dot(oh,ghb[b%2],preferred_element_type=f32)
            if b==0: racc[rows,:]=d
            else: racc[rows,:]=racc[rows,:]+d
            return 0
        lax.fori_loop(0,parts*nrel//QC,chunk,0)
    def grp(g): return pl.ds(pl.multiple_of(g*nrel,8),nrel)
    def relpair(i): return rc(racc.at[grp(2*order[i]+1-k),:],rp.at[i],rps.at[i],rpr.at[i],(c,sib))
    def relz(i): return rc(rsz.at[i],rzr.at[i],rzs.at[i],rzrr.at[i],(c,2*order[i]+k))
    def slot(b):
        getblock(b); src_slot(b); rel_slot(b)
    slot(0)
    stage0(0)
    slot(1)
    stage0(1)
    stageB(0)
    slot(2)
    stage0(2)
    stageB(1)
    stageZ(0)
    slot(3)
    stageB(2)
    stageZ(1)
    slot(4)
    stageZ(2)
    for b in range(5,parts): slot(b)
    stage0(3)
    for i in range(nz): relpair(i).start()
    for i in range(nz-1):
        relpair(i).wait_recv()
        rsz[i]=(racc[grp(2*order[i]+k),:]+rp[i]).astype(RT)
        relz(i).start()
    stageB(3)
    stageZ(3)
    for i in range(nz-1):
        zc(i).wait_recv()
    def fin(rows,rel):
        v=ge_ref[rows,lane(c)]
        for i in range(nz-1): v=v+rz[i,rows,:].astype(f32)
        ge_ref[rows,lane(c)]=v
        return v
    def fit(t,acc):
        v=fin(pl.ds(pl.multiple_of(t*RB,RB),RB),None)
        return acc+v*v
    sq=lax.fori_loop(0,width//RB,fit,jnp.zeros((RB,CK),f32))
    def gx(l): return rc(ge_ref.at[:,l],ge_ref.at[:,l],gxs,gxr,(xn,e))
    def gy(l): return rc(ge_ref.at[:,l],ge_ref.at[:,l],gys,gyr,(yn,e))
    def gdy(l): return rc(ge_ref.at[0:HALF,l],ge_ref.at[0:HALF,l],gdys,gdyr,(yn,e))
    def gdx(l): return rc(ge_ref.at[HALF:width,l],ge_ref.at[HALF:width,l],gdxs,gdxr,(xn,e))
    gx(lane(c)).start(); gy(lane(c)).start()
    relpair(nz-1).wait_recv()
    rv=racc[grp(e),:]+rp[nz-1]
    for i in range(nz-1):
        relz(i).wait_recv()
        rv=rv+rzr[i].astype(f32)
    gr_ref[...]=rv
    one=jnp.sum(sq)+3.0*jnp.sum(rv*rv)
    row=lax.broadcasted_iota(i32,(8,128),0)
    v=jnp.where(row==0,one,jnp.where(row==1,jnp.sum(sc_ref[0:8,:]),jnp.where(row==2,jnp.sum(sc_ref[8:16,:]),0.0)))
    for s,to in enumerate(((c,sib),(xn,e),(yn,e))):
        scb[s]=v
        cp=rc(scb.at[s],scb.at[3+s],css.at[s],csr.at[s],to)
        cp.start(); cp.wait()
        v=v+scb[3+s]
        if s==1:
            gx(lane(xn)).wait_recv(); gdy(lane(xn)).start()
            gy(lane(yn)).wait_recv(); gdx(lane(yn)).start()
    scb[6+z]=v
    def cz(d): return rc(scb.at[6+z],scb.at[6+z],czs.at[d],czr.at[d],(c,lax.rem(e+2*d,parts)))
    for d in range(1,nz): cz(d).start()
    for d in range(1,nz): cz(d).wait()
    sco_ref[...]=(scb[6]+scb[7])+(scb[8]+scb[9])
    gdy(lane(3-c)).wait_recv(); gdx(lane(3-c)).wait_recv()
    gx(lane(c)).wait_send(); gy(lane(c)).wait_send(); gdy(lane(xn)).wait_send(); gdx(lane(yn)).wait_send()
    for i in range(nz):
        pair(i).wait_send(); ax(i).wait_send(); ay(i).wait_send(); bx(i).wait_send(); by(i).wait_send(); relpair(i).wait_send()
        if i<nz-1: zc(i).wait_send(); relz(i).wait_send()

def reduce_call(g,gh,src,rid,sc,nrel):
    parts,width,ents=g.shape
    cap=src.shape[1]; nz=4; CK=ents//4
    D=pltpu.SemaphoreType.DMA
    V=pl.BlockSpec(memory_space=pltpu.VMEM); A=pl.BlockSpec(memory_space=pl.ANY)
    VM=pltpu.VMEM
    return pl.pallas_call(reduce_kernel,name="k3_reduce",
        in_specs=[A,A,V,V,V],out_specs=[V,V,V],
        out_shape=[jax.ShapeDtypeStruct((width,ents),f32),jax.ShapeDtypeStruct((nrel,width),f32),jax.ShapeDtypeStruct((8,128),f32)],
        scratch_shapes=[VM((nz,width,ents),f32),VM((2,width,ents),f32),VM((width,ents),f32),VM((parts*nrel,width),f32),
            VM((nz,HALF,2*CK),bf16),VM((nz,width-HALF,2*CK),bf16),VM((nz,HALF,2*CK),bf16),VM((nz,width-HALF,2*CK),bf16),
            VM((nz,width-HALF,CK),BT),VM((nz,HALF,CK),BT),VM((nz,width-HALF,CK),BT),VM((nz,HALF,CK),BT),
            VM((nz-1,width,CK),ZT),VM((nz-1,width,CK),ZT),
            VM((2,cap,width),bf16),VM((width,cap),bf16),VM((nz,nrel,width),f32),VM((nz-1,nrel,width),RT),VM((nz-1,nrel,width),RT),VM((10,8,128),f32),
            D((4,)),D((4,)),D((2,)),D((2,)),D((4,)),D((4,)),D((4,)),D((4,)),D((4,)),D((4,)),D((4,)),D((4,)),D((3,)),D((3,)),D((4,)),D((4,)),D((3,)),D((3,)),
            D,D,D,D,D,D,D,D,D((3,)),D((3,)),D((4,)),D((4,))],
        compiler_params=pltpu.CompilerParams(collective_id=2,has_side_effects=True,vmem_limit_bytes=62<<20))(g,gh,src,rid,sc)


def cube_body(
    ent_table,
    entity_first_moment,
    ent_v,
    rel_table,
    relation_first_moment,
    rel_v,
    src_ids,
    rel_ids,
    dst_ids,
    neg_ids,
    bucket_counts,
):
    parts, slots = src_ids.shape[2:]
    negcount = neg_ids.shape[3]
    nrel = rel_table.shape[1]
    clip_level = 0.01 / math.sqrt(lax.axis_size("rel") * lax.axis_size("ent") * parts * slots)
    padded = -(-negcount // 1024) * 1024
    negs = jnp.pad(neg_ids[0, 0], ((0, 0), (0, padded - negcount)), constant_values=-1)
    tables, hidden, arrived = gather_call(
        ent_table.T, rel_table, src_ids[0, 0], rel_ids[0, 0], negs.reshape(parts, -1, 128)
    )
    back, partial, sums = run_blocks(
        hidden,
        tables,
        dst_ids[0, 0].reshape(parts, -1, KT),
        arrived.reshape(parts, 1, padded),
        bucket_counts[0, 0],
        negcount,
    )
    ent_grad, rel_grad, totals = reduce_call(
        partial, back, src_ids[0, 0], rel_ids[0, 0], sums, nrel
    )
    squares, loss_sum, total = totals[0, 0], totals[1, 0], totals[2, 0]
    grad_norm = jnp.sqrt(squares) / total
    scale = jnp.minimum(1.0, clip_level / grad_norm) / total
    new_ent, new_ent_m, new_ent_v = adamw(ent_table, entity_first_moment, ent_v, scale * ent_grad.T)
    new_rel, new_rel_m, new_rel_v = adamw(
        rel_table, relation_first_moment, rel_v, scale * rel_grad[None]
    )
    return (
        loss_sum,
        total,
        grad_norm,
        new_ent,
        new_ent_m,
        new_ent_v,
        new_ent.astype(jnp.bfloat16),
        new_rel,
        new_rel_m,
        new_rel_v,
        new_rel.astype(jnp.bfloat16),
    )


def solution(mesh):
    body = cube_body if mesh.shape["rel"] == 4 and mesh.shape["ent"] == 8 else general_body
    return jax.shard_map(
        body,
        mesh=mesh,
        in_specs=(
            P("ent", None),
            P("ent", None),
            P("ent", None),
            P(None, ("rel", "ent"), None),
            P(None, ("rel", "ent"), None),
            P(None, ("rel", "ent"), None),
            P("rel", "ent", None, None),
            P("rel", "ent", None, None),
            P("rel", "ent", None, None),
            P("rel", "ent", None, None),
            P("rel", "ent", None),
        ),
        out_specs=(
            P(),
            P(),
            P(),
            P("ent", None),
            P("ent", None),
            P("ent", None),
            P("ent", None),
            P(None, ("rel", "ent"), None),
            P(None, ("rel", "ent"), None),
            P(None, ("rel", "ent"), None),
            P(None, ("rel", "ent"), None),
        ),
        check_vma=False,
    )
```

```python
import functools
import math

import jax
import jax.numpy as jnp
from jax import lax
from jax.experimental import pallas as pl
from jax.experimental.pallas import tpu as pltpu
from jax.sharding import PartitionSpec as P

STEP = 10
f32 = jnp.float32
bf16 = jnp.bfloat16
i32 = jnp.int32
MESH = pl.DeviceIdType.MESH


margin = 2.5
beta_one = 0.9
beta_two = 0.999
learn_rate = 0.05
decay_rate = 0.01
epsilon = 1e-16


def shortened(array):
    return jax.tree.map(lambda a: a.astype(jnp.bfloat16) if a.dtype == jnp.float32 else a, array)


def adamw(weight, moment, second, grad):
    moment = beta_one * moment + (1.0 - beta_one) * grad
    second = beta_two * second + (1.0 - beta_two) * grad * grad
    m_hat = moment / (1.0 - beta_one**STEP)
    v_hat = second / (1.0 - beta_two**STEP)
    weight = weight - learn_rate * (m_hat / (jnp.sqrt(v_hat) + epsilon) + decay_rate * weight)
    return (weight, moment, second)


def general_body(
    ent_table,
    entity_first_moment,
    ent_v,
    rel_table,
    relation_first_moment,
    rel_v,
    src_ids,
    rel_ids,
    dst_ids,
    neg_ids,
    bucket_counts,
):
    parts = src_ids.shape[2]
    slots = src_ids.shape[3]
    width = ent_table.shape[1]
    negcount = neg_ids.shape[3]
    clip_level = 0.01 / math.sqrt(lax.axis_size("rel") * lax.axis_size("ent") * parts * slots)
    ent_low = ent_table.astype(jnp.bfloat16)
    layers = lax.all_gather(rel_table.astype(jnp.bfloat16), "ent", axis=1, tiled=True)
    rel_sum = (
        layers[0].astype(jnp.float32)
        + layers[1].astype(jnp.float32)
        + layers[2].astype(jnp.float32)
    )
    sources = src_ids[0, 0]
    relation = rel_ids[0, 0]
    counts = bucket_counts[0, 0]
    hidden = ent_low[sources].astype(jnp.float32) + rel_sum[relation]
    total = lax.psum(jnp.sum(counts).astype(jnp.float32), ("rel", "ent"))
    arrived, dst_in, count_in = (
        lax.all_to_all(hidden.astype(jnp.bfloat16), "ent", split_axis=0, concat_axis=0, tiled=True),
        lax.all_to_all(dst_ids[0, 0], "ent", split_axis=0, concat_axis=0, tiled=True),
        lax.all_to_all(counts[:, None], "ent", split_axis=0, concat_axis=0, tiled=True),
    )
    live = (jnp.arange(slots, dtype=jnp.int32)[None, :] < count_in).astype(jnp.float32)
    negatives = neg_ids[0, 0]

    def block(args):
        hid, dst, neg, alive = args
        weight = alive / total
        hid_f = hid.astype(jnp.float32)
        diff = hid_f - ent_low[dst].astype(jnp.float32)
        pos_dist = jnp.sqrt(jnp.sum(diff * diff, -1) + 1.0)
        rows = ent_low[neg]
        rows_f = rows.astype(jnp.float32)
        prod = lax.dot_general(
            hid, rows, (((1,), (1,)), ((), ())), preferred_element_type=jnp.float32
        )
        sq = (
            jnp.sum(hid_f * hid_f, -1)[:, None] + jnp.sum(rows_f * rows_f, -1)[None, :] - 2.0 * prod
        )
        neg_dist = jnp.sqrt(sq + 1.0)
        per_edge = jax.nn.softplus(pos_dist - margin) + jnp.mean(
            jax.nn.softplus(margin - neg_dist), -1
        )
        loss = jnp.sum(alive * per_edge)
        g_pos = weight * jax.nn.sigmoid(pos_dist - margin)
        g_diff = (g_pos / pos_dist)[:, None] * diff
        g_sq = -(weight[:, None] / negcount) * jax.nn.sigmoid(margin - neg_dist) / (2.0 * neg_dist)
        g_prod = (-2.0 * g_sq).astype(jnp.bfloat16)
        g_hid = (
            g_diff
            + 2.0 * hid_f * jnp.sum(g_sq, 1)[:, None]
            + jnp.dot(g_prod, rows, preferred_element_type=jnp.float32)
        )
        g_rows = 2.0 * rows_f * jnp.sum(g_sq, 0)[:, None] + lax.dot_general(
            g_prod, hid, (((0,), (0,)), ((), ())), preferred_element_type=jnp.float32
        )
        return (loss, g_hid.astype(jnp.bfloat16), -g_diff, g_rows)

    losses, back, g_target, g_negative = lax.map(
        block, (arrived, dst_in, negatives, live), batch_size=min(4, parts)
    )
    returned = (
        jax.tree.map(
            lambda part, own: part.astype(own.dtype),
            lax.all_to_all(shortened(back), "ent", split_axis=0, concat_axis=0, tiled=True),
            back,
        )
        .reshape(-1, width)
        .astype(jnp.float32)
    )
    ent_grad = jnp.zeros(ent_table.shape, jnp.float32)
    ent_grad = ent_grad.at[dst_in.reshape(-1)].add(g_target.reshape(-1, width))
    ent_grad = ent_grad.at[negatives.reshape(-1)].add(g_negative.reshape(-1, width))
    ent_grad = ent_grad.at[sources.reshape(-1)].add(returned)
    ent_grad = lax.psum(ent_grad, "rel")
    rel_local = jnp.zeros(rel_sum.shape, jnp.float32).at[relation.reshape(-1)].add(returned)
    rel_grad = lax.psum_scatter(rel_local, "ent", scatter_dimension=0, tiled=True)
    own_squares = jnp.where(
        lax.axis_index("rel") == 0, jnp.sum(ent_grad * ent_grad), 0.0
    ) + 3.0 * jnp.sum(rel_grad * rel_grad)
    squares, loss_sum = lax.psum((own_squares, jnp.sum(losses)), ("rel", "ent"))
    grad_norm = jnp.sqrt(squares)
    scale = jnp.minimum(1.0, clip_level / grad_norm)
    new_ent, new_ent_m, new_ent_v = adamw(ent_table, entity_first_moment, ent_v, scale * ent_grad)
    new_rel, new_rel_m, new_rel_v = adamw(
        rel_table, relation_first_moment, rel_v, scale * rel_grad[None]
    )
    return (
        loss_sum,
        total,
        grad_norm,
        new_ent,
        new_ent_m,
        new_ent_v,
        new_ent.astype(jnp.bfloat16),
        new_rel,
        new_rel_m,
        new_rel_v,
        new_rel.astype(jnp.bfloat16),
    )


KT1=256
RP=256

def split3(x):
    hi=x.astype(bf16).astype(f32); r=x-hi
    mid=r.astype(bf16).astype(f32); lo=r-mid
    return hi,mid,lo

def place():
    r=lax.axis_index("rel"); e=lax.axis_index("ent")
    z=lax.div(e,2); k=lax.rem(e,2)
    xn=r+1-2*lax.rem(r,2)
    yn=lax.rem(r+2,4)
    return r,z,k,xn,yn

def gather_kernel(et_ref, rt_ref, src_ref, rid_ref, neg_ref,
                  tab_ref, h_ref, negout_ref,
                  tb, rall, eh, hb, lsem, hsem, us, ds, zr, xs, xr, ys, yr, fs, fr, cs, cr, rcs, rcr, ns, nr):
    width,ents=et_ref.shape
    nz=4; parts=8
    CK=ents//4
    cap=src_ref.shape[1]
    c,z,k,xn,yn=place()
    e=2*z+k
    half=208
    sib=2*z+1-k
    bar=pltpu.get_barrier_semaphore()
    for d in range(1,parts):
        pl.semaphore_signal(bar,inc=1,device_id=(c,lax.rem(e+d,parts)),device_id_type=MESH)
    pl.semaphore_signal(bar,inc=1,device_id=(xn,e),device_id_type=MESH)
    pl.semaphore_signal(bar,inc=1,device_id=(yn,e),device_id_type=MESH)
    tb[...]=et_ref[...].astype(bf16)
    low=[rt_ref[l].astype(bf16).astype(f32) for l in range(3)]
    rsum=jnp.concatenate([low[0]+low[1]+low[2],jnp.zeros((RP-rt_ref.shape[1],width),f32)],0)
    rall[e]=rsum.T.astype(bf16)
    pl.semaphore_wait(bar,parts+1)
    def rc(src,dst,s,r,to):
        return pltpu.make_async_remote_copy(src_ref=src,dst_ref=dst,send_sem=s,recv_sem=r,device_id=to,device_id_type=MESH)
    rows_of=(pl.ds(0,half),pl.ds(half,width-half))
    def lane(ck): return pl.ds(pl.multiple_of(ck*CK,CK),CK)
    SEQ=((2,1),(0,1),(2,2),(1,1),(2,3),(0,2),(1,2),(0,3),(1,3))
    def part(o,u,own=False):
        if u==2: return rall.at[2*o+k]
        return tb.at[rows_of[u],lane(c)] if own else tab_ref.at[2*o+k,rows_of[u],lane(c)]
    def up(o,u,own): return rc(part(o,u,own),part(o,u),us.at[u,o],zr.at[u,o],(c,2*(z+1)+k))
    def down(o,u,own): return rc(part(o,u,own),part(o,u),ds.at[u,o],zr.at[u,o],(c,2*(z-1)+k))
    def sides(dist,fn):
        @pl.when(z>=dist)
        def _(): fn(z-dist)
        @pl.when(z+dist<nz)
        def _(): fn(z+dist)
    def along(n,act):
        u,dist=SEQ[n]
        f=dist-1
        @pl.when(jnp.logical_and(z<nz-1,z>=f))
        def _(): act(up(z-f,u,f==0))
        @pl.when(jnp.logical_and(z>0,z+f<nz))
        def _(): act(down(z+f,u,f==0))
    def xc(o,h,l): return rc(tab_ref.at[2*o+k,rows_of[h],l],tab_ref.at[2*o+k,rows_of[h],l],xs.at[o,h],xr.at[o,h],(xn,e))
    def yc(o,h,l): return rc(tab_ref.at[2*o+k,rows_of[h],l],tab_ref.at[2*o+k,rows_of[h],l],ys.at[o,h],yr.at[o,h],(yn,e))
    def fc(o,h,l):
        v=tab_ref.at[2*o+k,rows_of[h],l]
        return rc(v,v,fs.at[o,h],fr.at[o,h],((yn,e),(xn,e))[h])
    def cc(o,h,kk,own=False):
        v=tab_ref.at[2*o+kk,rows_of[h],:]
        return rc(tb.at[rows_of[h],:] if own else v,v,cs.at[o,h],cr.at[o,h],(c,sib))
    def rel_sib(o,kk):
        return rc(rall.at[2*o+kk],rall.at[2*o+kk],rcs.at[o],rcr.at[o],(c,sib))
    along(0,lambda cp: cp.start())
    along(1,lambda cp: cp.start())
    rel_sib(z,k).start()
    def neg_copy(to,own):
        return rc(neg_ref.at[to],negout_ref.at[own],ns.at[to],nr.at[own],(c,to))
    for d in range(1,parts):
        neg_copy(lax.rem(e+d,parts),e).start()
    own_neg=pltpu.make_async_copy(neg_ref.at[e],negout_ref.at[e],lsem.at[1])
    own_neg.start()
    own_tab=pltpu.make_async_copy(tb,tab_ref.at[e],lsem.at[0])
    own_tab.start()
    for h in range(2): cc(z,h,k,True).start()
    def Z(n):
        u,dist=SEQ[n]
        def fn(o):
            up(o,u,False).wait_recv()
            if u==2: rel_sib(o,k).start()
            else:
                xc(o,u,lane(c)).start(); yc(o,u,lane(c)).start()
        sides(dist,fn)
        if n+2<len(SEQ): along(n+2,lambda cp: cp.start())
    def C(dist,h):
        def fn(o):
            if h==0: xc(o,0,lane(xn)).wait_recv(); fc(o,0,lane(xn)).start()
            else: yc(o,1,lane(yn)).wait_recv(); fc(o,1,lane(yn)).start()
        sides(dist,fn)
    def W(dist,h):
        def fn(o):
            if h==0: yc(o,0,lane(yn)).wait_recv()
            else: xc(o,1,lane(xn)).wait_recv()
            fc(o,h,lane(3-c)).wait_recv()
            cc(o,h,k).start()
        sides(dist,fn)
    def onehot(ids):
        return jnp.where(lax.broadcasted_iota(i32,(ents,KT1),0)==ids,1.0,0.0).astype(bf16)
    nt=cap//KT1
    def src_slot(b):
        def tile(t,_):
            l=pl.ds(pl.multiple_of(t*KT1,KT1),KT1)
            eh[b,:,l]=jnp.dot(tb[...],onehot(src_ref[b:b+1,l]),preferred_element_type=f32).astype(bf16)
            return 0
        lax.fori_loop(0,nt,tile,0)
    def out_copy(b):
        return pltpu.make_async_copy(hb.at[b%2],h_ref.at[pl.ds(b*cap,cap),:],hsem.at[b%2])
    nrel=rt_ref.shape[1]
    def rel_slot(b):
        if b>=2: out_copy(b-2).wait()
        def tile(t,_):
            l=pl.ds(pl.multiple_of(t*KT1,KT1),KT1)
            q=rid_ref[b:b+1,l]
            g=jnp.floor((q.astype(f32)+0.5)*(1.0/nrel)).astype(i32)
            q=q+(RP-nrel)*g
            acc=eh[b,:,l].astype(f32)
            for g0 in range(0,parts):
                oh=jnp.where(lax.broadcasted_iota(i32,(RP,KT1),0)+RP*g0==q,1.0,0.0).astype(bf16)
                acc=acc+jnp.dot(rall[g0],oh,preferred_element_type=f32)
            hid=acc.astype(bf16)
            hf=hid.astype(f32)
            hi,mid,lo=split3(jnp.sum(hf*hf,0,keepdims=True))
            row=lax.broadcasted_iota(i32,(hb.shape[2]-width,KT1),0)
            ex=jnp.where(row==0,hi,jnp.where(row==1,mid,jnp.where(row==2,lo,jnp.where(row<6,1.0,0.0))))
            hb[b%2,pl.ds(pl.multiple_of(t*KT1,KT1),KT1),:]=jnp.concatenate([hf,ex],0).T.astype(bf16)
            return 0
        lax.fori_loop(0,nt,tile,0)
        out_copy(b).start()
    def allrel():
        for o in range(nz): rel_sib(o,1-k).wait_recv()
    src_slot(0)
    src_slot(1)
    Z(0)
    src_slot(2)
    Z(1)
    src_slot(3)
    Z(2)
    src_slot(4)
    C(1,0)
    src_slot(5)
    Z(3)
    src_slot(6)
    Z(4)
    W(1,0)
    src_slot(7)
    C(1,1)
    Z(5)
    allrel()
    rel_slot(0)
    W(1,1)
    Z(6)
    rel_slot(1)
    C(2,0)
    Z(7)
    rel_slot(2)
    W(2,0)
    C(2,1)
    Z(8)
    rel_slot(3)
    W(2,1)
    C(3,0)
    rel_slot(4)
    C(3,1)
    W(3,0)
    rel_slot(5)
    W(3,1)
    rel_slot(6)
    rel_slot(7)
    for n in range(len(SEQ)): along(n,lambda cp: cp.wait_send())
    for h in range(2):
        for o in range(nz): cc(o,h,1-k).wait_recv()
        cc(z,h,k,True).wait_send()
        for dist in range(1,nz):
            def fn(o):
                cc(o,h,k).wait_send()
                xc(o,h,lane(c)).wait_send(); yc(o,h,lane(c)).wait_send()
                fc(o,h,(lane(xn),lane(yn))[h]).wait_send()
            sides(dist,fn)
    for o in range(nz): rel_sib(o,k).wait_send()
    for d in range(1,parts):
        o=lax.rem(e+d,parts)
        neg_copy(o,e).wait_send()
        neg_copy(e,o).wait_recv()
    own_tab.wait(); own_neg.wait()
    out_copy(6).wait(); out_copy(7).wait()

def gather_call(et,rt,src,rid,negs):
    width,ents=et.shape
    parts,cap=src.shape
    D=pltpu.SemaphoreType.DMA
    V=pl.BlockSpec(memory_space=pltpu.VMEM); A=pl.BlockSpec(memory_space=pl.ANY)
    return pl.pallas_call(gather_kernel,name="k1_gather",
        in_specs=[V]*5,out_specs=[A,A,V],
        out_shape=[jax.ShapeDtypeStruct((parts,width,ents),bf16),jax.ShapeDtypeStruct((parts*cap,512),bf16),jax.ShapeDtypeStruct(negs.shape,i32)],
        scratch_shapes=[pltpu.VMEM((width,ents),bf16),pltpu.VMEM((parts,width,RP),bf16),pltpu.VMEM((parts,width,cap),bf16),pltpu.VMEM((2,cap,512),bf16),
            D((2,)),D((2,)),D((3,4)),D((3,4)),D((3,4)),D((4,2)),D((4,2)),D((4,2)),D((4,2)),D((4,2)),D((4,2)),D((4,2)),D((4,2)),D((4,)),D((4,)),D((8,)),D((8,))],
        compiler_params=pltpu.CompilerParams(collective_id=1,has_side_effects=True,vmem_limit_bytes=60<<20))(et,rt,src,rid,negs)


KT = 256
WA=416
def block_kernel(width, ents, negcount, CH,
                 counts_ref, h_ref, t_ref, dst_ref, neg_ref, gh_ref, g_ref, loss_ref,
                 ta_ref, tr_ref, acc_ref, crow_ref, s_ref):
    j=pl.program_id(0)
    wa=ta_ref.shape[0]
    count=counts_ref[j]
    tiles=lax.div(count+(KT-1),KT)
    t=t_ref[0]
    tf=t.astype(f32)
    norm=(jnp.sum(tf*tf,0,keepdims=True)+1.0)*0.25
    hi,mid,lo=split3(norm)
    ta_ref[0:width,:]=t*bf16(-0.5)
    sub=lax.broadcasted_iota(jnp.int32,(wa-width,ents),0)
    pad=jnp.where(sub<3,0.25,0.0)
    pad=jnp.where(sub==3,hi,pad)
    pad=jnp.where(sub==4,mid,pad)
    pad=jnp.where(sub==5,lo,pad)
    ta_ref[width:,:]=pad.astype(bf16)
    tcat=jnp.concatenate([t, jnp.where(sub==0,1.0,0.0).astype(bf16)],0)
    tr_ref[...]=tcat.T
    ids=neg_ref[0]
    nn=ids.shape[1]
    ohi=jnp.where(lax.broadcasted_iota(jnp.int32,(ents//128,nn),0)==lax.shift_right_arithmetic(ids,7),1.0,0.0).astype(bf16)
    olo=jnp.where(lax.broadcasted_iota(jnp.int32,(128,nn),0)==(ids&127),1.0,0.0).astype(bf16)
    c=lax.dot_general(ohi,olo,(((1,),(1,)),((),())),preferred_element_type=f32)
    for i in range(ents//128):
        crow_ref[0:1,128*i:128*(i+1)]=c[i:i+1,:]
    acc_ref[...]=jnp.zeros_like(acc_ref)
    gh_ref[...]=jnp.zeros_like(gh_ref)
    @pl.when(j==0)
    def _(): loss_ref[...]=jnp.zeros_like(loss_ref)
    first=jnp.logical_and(lax.broadcasted_iota(jnp.int32,(8,128),0)==0,lax.broadcasted_iota(jnp.int32,(8,128),1)==0)
    loss_ref[8:16,:]+=jnp.where(first,count.astype(f32),0.0)
    eye=lax.broadcasted_iota(jnp.int32,(KT,KT),0)==lax.broadcasted_iota(jnp.int32,(KT,KT),1)
    lanes=lax.broadcasted_iota(jnp.int32,(1,CH),1)
    nch=ents//CH
    def rows_of(kt): return pl.ds(pl.multiple_of(kt*KT,KT),KT)
    def live_of(kt): return (lax.broadcasted_iota(jnp.int32,(KT,1),0)+kt*KT)<count
    def idcol(kt):
        idr=dst_ref[0,pl.ds(kt,1),:].astype(f32)
        return jnp.sum(jnp.where(eye,idr,0.0),1,keepdims=True).astype(jnp.int32)
    def aug(kt):
        hb=h_ref[rows_of(kt),:]
        last=hb[:,width//128*128:wa].astype(f32)
        lane=lax.broadcasted_iota(jnp.int32,last.shape,1)+width//128*128
        last=jnp.where(jnp.logical_and(lane==width,jnp.logical_not(live_of(kt))),4e6,last)
        return jnp.concatenate([hb[:,:width//128*128],last.astype(bf16)],1)
    def sdot(ha,ci): return jnp.dot(ha,ta_ref[:,ci*CH:(ci+1)*CH],preferred_element_type=f32)
    def post(s,idc,ci,sp):
        es=jnp.where(idc==lanes+ci*CH,s,0.0)
        for a in range(CH//128): sp=sp+es[:,128*a:128*(a+1)]
        s_ref[:,ci*CH:(ci+1)*CH]=s
        return sp
    def column(sp,kt):
        live=live_of(kt)
        sq=jnp.sum(sp,1,keepdims=True)*4.0
        rr=lax.rsqrt(sq)
        x=sq*rr-margin
        a=jnp.where(live,jax.nn.sigmoid(x)*rr,0.0)
        inva=jnp.where(live,1.0/a,0.0)
        pos=jnp.where(live,jnp.maximum(x,0.0)+jnp.log(1.0+jnp.exp(-jnp.abs(x))),0.0)
        p8=pos[0:8]
        for b in range(1,KT//8): p8+=pos[8*b:8*b+8]
        loss_ref[0:8,:]+=jnp.where(lax.broadcasted_iota(jnp.int32,(8,128),1)==0,p8,0.0)
        return a,inva
    ha=aug(0); idc=idcol(0); sp=jnp.zeros((KT,128),f32)
    for ci in range(nch): sp=post(sdot(ha,ci),idc,ci,sp)
    a0,i0=column(sp,0)
    def tile(kt,carry):
        rho,inva,idc=carry
        nk=jnp.minimum(kt+1,tiles-1)
        hb=h_ref[rows_of(kt),:]
        hf=hb[:,:width].astype(f32)
        hi,mid,lo=split3(rho)
        ex=lax.broadcasted_iota(jnp.int32,(KT,wa-width),1)
        pad=jnp.where(ex==0,hi,jnp.where(ex==1,mid,jnp.where(ex==2,lo,0.0)))
        hat=jnp.concatenate([(hf*rho),pad],1).astype(bf16).T
        ha=aug(nk); nidc=idcol(nk)
        gh=jnp.zeros((KT,wa),f32)
        sp=jnp.zeros((KT,128),f32)
        lsum=jnp.zeros((8,CH),f32)
        ms=[None]*nch
        invn=inva*(0.25/negcount)
        pend=None
        for ci in range(nch+1):
            if ci<nch:
                cols=slice(ci*CH,(ci+1)*CH)
                s=s_ref[:,cols]
                r=lax.rsqrt(s)
                th=jnp.tanh(margin*0.5-s*r)
                sp=post(sdot(ha,ci),nidc,ci,sp)
                cr=crow_ref[0:1,cols]
                mask=idc==lanes+ci*CH
                u=(1.0+th).astype(bf16)
                x=(u*cr.astype(bf16))*(r*invn).astype(bf16)
                ms[ci]=jnp.where(mask,1.0,0.0).astype(bf16)-x
                o=1.0-th
                p=o[0:8]
                for b in range(1,KT//8): p=p*o[8*b:8*b+8]
                lsum+=(math.log(2.0)*(KT//8)-jnp.log(p))*cr
            if ci>=1:
                pc=slice((ci-1)*CH,ci*CH)
                gh+=jnp.dot(ms[ci-1],tr_ref[pc,:],preferred_element_type=f32)
                acc_ref[:,pc]+=jnp.dot(hat,ms[ci-1],preferred_element_type=f32)
        l8=lsum[:,0:128]
        for b in range(1,CH//128): l8+=lsum[:,128*b:128*(b+1)]
        loss_ref[0:8,:]+=l8*(1.0/negcount)
        out=(hf*gh[:,width:width+1]-gh[:,:width])*rho
        gh_ref[rows_of(kt),:width]=out.astype(bf16)
        live=kt+1<tiles
        na,ni=column(jnp.where(live,sp,1.0),jnp.where(live,nk,tiles))
        return na,ni,nidc
    lax.fori_loop(0,tiles,tile,(a0,i0,idc))
    g_ref[0]=tf*acc_ref[width:width+1,:]+tf*acc_ref[width+1:width+2,:]+tf*acc_ref[width+2:width+3,:]-acc_ref[0:width,:]

def run_blocks(h,tables,dst,neg,counts,negcount,CH=256):
    parts,width,ents=tables.shape
    cap=h.shape[0]//parts
    wa=WA
    nn=neg.shape[-1]
    gs=pltpu.PrefetchScalarGridSpec(num_scalar_prefetch=1,grid=(parts,),
      in_specs=[pl.BlockSpec((cap,h.shape[1]),lambda j,c:(j,0)),
                pl.BlockSpec((1,width,ents),lambda j,c:(j,0,0)),
                pl.BlockSpec((1,cap//KT,KT),lambda j,c:(j,0,0)),
                pl.BlockSpec((1,1,nn),lambda j,c:(j,0,0))],
      out_specs=[pl.BlockSpec((cap,width),lambda j,c:(j,0)),
                 pl.BlockSpec((1,width,ents),lambda j,c:(j,0,0)),
                 pl.BlockSpec((16,128),lambda j,c:(0,0))],
      scratch_shapes=[pltpu.VMEM((wa,ents),bf16),pltpu.VMEM((ents,wa),bf16),
                      pltpu.VMEM((wa,ents),f32),pltpu.VMEM((8,ents),f32),pltpu.VMEM((KT,ents),f32)])
    return pl.pallas_call(functools.partial(block_kernel,width,ents,negcount,CH),grid_spec=gs,name="k2_blocks",
      out_shape=[jax.ShapeDtypeStruct((h.shape[0],width),bf16),jax.ShapeDtypeStruct(tables.shape,f32),jax.ShapeDtypeStruct((16,128),f32)],
      compiler_params=pltpu.CompilerParams(vmem_limit_bytes=60<<20,dimension_semantics=("arbitrary",)))(counts,h,tables,dst,neg)


HALF=208

def reduce_kernel(g_ref, gh_ref, src_ref, rid_ref, sc_ref,
                  ge_ref, gr_ref, sco_ref,
                  pr, own, sacc, racc, sa0, sa1, ra0, ra1, sb0, sb1, rb0, rb1, sz, rz, ghb, rp, rsz, rzr, scb,
                  ps, prr, osem, gsem, sas, sar, sbs, sbr, zs, zr, rps, rpr, rzs, rzrr, gxs, gxr, gys, gyr, gds, gdr, css, csr, czs, czr):
    parts,width,ents=g_ref.shape
    nz=4; CK=ents//4; last=nz-1
    cap=src_ref.shape[1]
    nrel=gr_ref.shape[0]
    c,z,k,xn,yn=place()
    e=2*z+k; sib=2*z+1-k
    x=lax.rem(c,2); y=lax.div(c,2); xo=1-x; yo=1-y
    bar=pltpu.get_barrier_semaphore()
    for to in ((c,sib),(xn,e),(yn,e))+tuple((c,lax.rem(e+2*d,parts)) for d in range(1,nz)):
        pl.semaphore_signal(bar,inc=1,device_id=to,device_id_type=MESH)
    order=[lax.rem(z+1+i,nz) for i in range(nz)]
    rows_of=(pl.ds(0,HALF),pl.ds(HALF,width-HALF))
    lo=(0,HALF); num=(HALF,width-HALF)
    def load(i): return pltpu.make_async_copy(g_ref.at[2*order[i]+k],own.at[i%2],osem.at[i%2])
    def gload(b): return pltpu.make_async_copy(gh_ref.at[pl.ds(b*cap,cap),:],ghb.at[b%2],gsem.at[b%2])
    gload(0).start(); load(0).start(); load(1).start()
    pl.semaphore_wait(bar,nz+2)
    def rc(src,dst,s,r,to):
        return pltpu.make_async_remote_copy(src_ref=src,dst_ref=dst,send_sem=s,recv_sem=r,device_id=to,device_id_type=MESH)
    def pair(i,h): return rc(g_ref.at[2*order[i]+1-k,rows_of[h],:],pr.at[i,rows_of[h],:],ps.at[i,h],prr.at[i,h],(c,sib))
    for i in range(2):
        for h in range(2): pair(i,h).start()
    def lane(ck,n=1): return pl.ds(pl.multiple_of(ck*CK,CK),n*CK)
    near=((xn,e),(yn,e)); sa=(sa0,sa1); ra=(ra0,ra1); sb=(sb0,sb1); rb=(rb0,rb1)
    def ac(i,h): return rc(sa[h].at[i],ra[h].at[i],sas.at[i,h],sar.at[i,h],near[h])
    def bc(i,h): return rc(sb[h].at[i],rb[h].at[i],sbs.at[i,h],sbr.at[i,h],near[1-h])
    def zc(i,h): return rc(sz.at[i,rows_of[h],:],rz.at[i,rows_of[h],:],zs.at[i,h],zr.at[i,h],(c,2*order[i]+k))
    gone=((xo,xo+2),(2*yo,2*yo+1))
    kept=((x,x+2),(2*y,2*y+1))
    passed=(x+2*yo,2*y+xo)
    mine=(y,x)
    RB=16
    def strips(h,fn):
        fn(rows_of[h],pl.ds(0,num[h]))
    def st0(i,h):
        if h==0 and i!=last: load(i).wait()
        pair(i,h).wait_recv()
        def one(rows,rel):
            for s in range(2):
                l=lane(gone[h][s])
                sa[h][i,rel,s*CK:(s+1)*CK]=(pr[i,rows,l]+own[i%2,rows,l]).astype(bf16)
                l=lane(kept[h][s])
                pr[i,rows,l]=pr[i,rows,l]+own[i%2,rows,l]
        strips(h,one)
        ac(i,h).start()
        if h==1 and i+2<nz:
            load(i+2).start()
            for g in range(2): pair(i+2,g).start()
    def stB(i,h):
        ac(i,h).wait_recv()
        def one(rows,rel):
            sb[h][i,rel,:]=(pr[i,rows,lane(passed[h])]+ra[h][i,rel,lane(1-mine[h])].astype(f32)).astype(sb0.dtype)
            pr[i,rows,lane(c)]=pr[i,rows,lane(c)]+ra[h][i,rel,lane(mine[h])].astype(f32)
        strips(h,one)
        bc(i,h).start()
    def stZ(i,h):
        bc(i,h).wait_recv()
        def one(rows,rel):
            v=pr[i,rows,lane(c)]+rb[h][i,rel,:].astype(f32)
            if i==last: ge_ref[rows,lane(c)]=v
            else: sz[i,rows,:]=v.astype(sz.dtype)
        strips(h,one)
        if i!=last: zc(i,h).start()
    def both(fn,i):
        fn(i,0); fn(i,1)
    def getblock(b):
        gload(b).wait()
        gload((b+1)%parts).start()
    def slot(ids_ref,acc,b,RC):
        ids=ids_ref[b:b+1,:]
        def chunk(t,_):
            rows=pl.ds(pl.multiple_of(t*RC,8),RC)
            oh=jnp.where(lax.broadcasted_iota(i32,(RC,cap),0)==ids-t*RC,1.0,0.0).astype(bf16)
            d=jnp.dot(oh,ghb[b%2],preferred_element_type=f32)
            if b==0: acc[rows,:]=d
            else: acc[rows,:]=acc[rows,:]+d
            return 0
        lax.fori_loop(0,acc.shape[0]//RC,chunk,0)
    def src(b):
        getblock(b); slot(src_ref,sacc,b,CK)
    def rel(b):
        getblock(b); slot(rid_ref,racc,b,2*nrel)
    def addsrc():
        def it(t,_):
            l=pl.ds(pl.multiple_of(t*128,128),128)
            own[last%2,:,l]=own[last%2,:,l]+sacc[l,:].T
            return 0
        lax.fori_loop(0,ents//128,it,0)
    def grp(g): return pl.ds(pl.multiple_of(g*nrel,8),nrel)
    def relpair(i): return rc(racc.at[grp(2*order[i]+1-k),:],rp.at[i],rps.at[i],rpr.at[i],(c,sib))
    def relz(i): return rc(rsz.at[i],rzr.at[i],rzs.at[i],rzrr.at[i],(c,2*order[i]+k))
    src(0)
    src(1)
    both(st0,0)
    src(2)
    src(3)
    both(st0,1)
    src(4)
    both(stB,0)
    src(5)
    src(6)
    both(st0,2)
    src(7)
    load(last).wait()
    addsrc()
    both(stB,1)
    both(stZ,0)
    rel(0)
    rel(1)
    both(st0,3)
    rel(2)
    both(stB,2)
    both(stZ,1)
    rel(3)
    rel(4)
    rel(5)
    both(stB,3)
    rel(6)
    both(stZ,2)
    rel(7)
    gload(0).wait()
    for i in range(nz): relpair(i).start()
    for i in range(last):
        relpair(i).wait_recv()
        rsz[i]=(racc[grp(2*order[i]+k),:]+rp[i]).astype(rsz.dtype)
        relz(i).start()
    both(stZ,3)
    sq=jnp.zeros((RB,CK),f32)
    def gx(h,l): return rc(ge_ref.at[rows_of[h],l],ge_ref.at[rows_of[h],l],gxs.at[h],gxr.at[h],(xn,e))
    def gy(h,l): return rc(ge_ref.at[rows_of[h],l],ge_ref.at[rows_of[h],l],gys.at[h],gyr.at[h],(yn,e))
    def gd(h,l): return rc(ge_ref.at[rows_of[h],l],ge_ref.at[rows_of[h],l],gds.at[h],gdr.at[h],near[1-h])
    for h in range(2):
        for i in range(last): zc(i,h).wait_recv()
        rows=rows_of[h]
        v=ge_ref[rows,lane(c)]
        for i in range(last): v=v+rz[i,rows,:].astype(f32)
        ge_ref[rows,lane(c)]=v
        v=v*v
        for b in range(0,num[h],RB): sq=sq+v[b:b+RB]
        if h==0: gx(0,lane(c)).start()
        else: gy(1,lane(c)).start()
    gy(0,lane(c)).start(); gx(1,lane(c)).start()
    gx(0,lane(xn)).wait_recv(); gd(0,lane(xn)).start()
    gy(1,lane(yn)).wait_recv(); gd(1,lane(yn)).start()
    relpair(last).wait_recv()
    rv=racc[grp(e),:]+rp[last]
    for i in range(last):
        relz(i).wait_recv()
        rv=rv+rzr[i].astype(f32)
    gr_ref[...]=rv
    one=jnp.sum(sq)+3.0*jnp.sum(rv*rv)
    row=lax.broadcasted_iota(i32,(8,128),0)
    v=jnp.where(row==0,one,jnp.where(row==1,jnp.sum(sc_ref[0:8,:]),jnp.where(row==2,jnp.sum(sc_ref[8:16,:]),0.0)))
    for s,to in enumerate(((c,sib),(xn,e),(yn,e))):
        scb[s]=v
        cp=rc(scb.at[s],scb.at[3+s],css.at[s],csr.at[s],to)
        cp.start(); cp.wait()
        v=v+scb[3+s]
    scb[6+z]=v
    def cz(d): return rc(scb.at[6+z],scb.at[6+z],czs.at[d],czr.at[d],(c,lax.rem(e+2*d,parts)))
    for d in range(1,nz): cz(d).start()
    for d in range(1,nz): cz(d).wait()
    sco_ref[...]=(scb[6]+scb[7])+(scb[8]+scb[9])
    gx(1,lane(xn)).wait_recv(); gy(0,lane(yn)).wait_recv()
    gd(0,lane(3-c)).wait_recv(); gd(1,lane(3-c)).wait_recv()
    for h in range(2):
        gx(h,lane(c)).wait_send(); gy(h,lane(c)).wait_send()
        for i in range(nz):
            pair(i,h).wait_send(); ac(i,h).wait_send(); bc(i,h).wait_send()
            if i<last: zc(i,h).wait_send()
    gd(0,lane(xn)).wait_send(); gd(1,lane(yn)).wait_send()
    for i in range(nz):
        relpair(i).wait_send()
        if i<last: relz(i).wait_send()

def reduce_call(g,gh,src,rid,sc,nrel,BT=bf16,ZT=bf16,RT=bf16):
    parts,width,ents=g.shape
    cap=src.shape[1]; nz=4; CK=ents//4
    D=pltpu.SemaphoreType.DMA
    V=pl.BlockSpec(memory_space=pltpu.VMEM); A=pl.BlockSpec(memory_space=pl.ANY)
    VM=pltpu.VMEM
    rest=width-HALF
    return pl.pallas_call(reduce_kernel,name="k3_reduce",
        in_specs=[A,A,V,V,V],out_specs=[V,V,V],
        out_shape=[jax.ShapeDtypeStruct((width,ents),f32),jax.ShapeDtypeStruct((nrel,width),f32),jax.ShapeDtypeStruct((8,128),f32)],
        scratch_shapes=[VM((nz,width,ents),f32),VM((2,width,ents),f32),VM((ents,width),f32),VM((parts*nrel,width),f32),
            VM((nz,HALF,2*CK),bf16),VM((nz,rest,2*CK),bf16),VM((nz,HALF,2*CK),bf16),VM((nz,rest,2*CK),bf16),
            VM((nz,HALF,CK),BT),VM((nz,rest,CK),BT),VM((nz,HALF,CK),BT),VM((nz,rest,CK),BT),
            VM((nz-1,width,CK),ZT),VM((nz-1,width,CK),ZT),
            VM((2,cap,width),bf16),VM((nz,nrel,width),f32),VM((nz-1,nrel,width),RT),VM((nz-1,nrel,width),RT),VM((10,8,128),f32),
            D((4,2)),D((4,2)),D((2,)),D((2,)),D((4,2)),D((4,2)),D((4,2)),D((4,2)),D((3,2)),D((3,2)),D((4,)),D((4,)),D((3,)),D((3,)),
            D((2,)),D((2,)),D((2,)),D((2,)),D((2,)),D((2,)),D((3,)),D((3,)),D((4,)),D((4,))],
        compiler_params=pltpu.CompilerParams(collective_id=2,has_side_effects=True,vmem_limit_bytes=62<<20))(g,gh,src,rid,sc)


def cube_body(
    ent_table,
    entity_first_moment,
    ent_v,
    rel_table,
    relation_first_moment,
    rel_v,
    src_ids,
    rel_ids,
    dst_ids,
    neg_ids,
    bucket_counts,
):
    parts, slots = src_ids.shape[2:]
    negcount = neg_ids.shape[3]
    nrel = rel_table.shape[1]
    clip_level = 0.01 / math.sqrt(lax.axis_size("rel") * lax.axis_size("ent") * parts * slots)
    padded = -(-negcount // 1024) * 1024
    negs = jnp.pad(neg_ids[0, 0], ((0, 0), (0, padded - negcount)), constant_values=-1)
    tables, hidden, arrived = gather_call(
        ent_table.T, rel_table, src_ids[0, 0], rel_ids[0, 0], negs.reshape(parts, -1, 128)
    )
    back, partial, sums = run_blocks(
        hidden,
        tables,
        dst_ids[0, 0].reshape(parts, -1, KT),
        arrived.reshape(parts, 1, padded),
        bucket_counts[0, 0],
        negcount,
    )
    ent_grad, rel_grad, totals = reduce_call(
        partial, back, src_ids[0, 0], rel_ids[0, 0], sums, nrel
    )
    squares, loss_sum, total = totals[0, 0], totals[1, 0], totals[2, 0]
    grad_norm = jnp.sqrt(squares) / total
    scale = jnp.minimum(1.0, clip_level / grad_norm) / total
    new_ent, new_ent_m, new_ent_v = adamw(ent_table, entity_first_moment, ent_v, scale * ent_grad.T)
    new_rel, new_rel_m, new_rel_v = adamw(
        rel_table, relation_first_moment, rel_v, scale * rel_grad[None]
    )
    return (
        loss_sum,
        total,
        grad_norm,
        new_ent,
        new_ent_m,
        new_ent_v,
        new_ent.astype(jnp.bfloat16),
        new_rel,
        new_rel_m,
        new_rel_v,
        new_rel.astype(jnp.bfloat16),
    )


def solution(mesh):
    body = cube_body if mesh.shape["rel"] == 4 and mesh.shape["ent"] == 8 else general_body
    return jax.shard_map(
        body,
        mesh=mesh,
        in_specs=(
            P("ent", None),
            P("ent", None),
            P("ent", None),
            P(None, ("rel", "ent"), None),
            P(None, ("rel", "ent"), None),
            P(None, ("rel", "ent"), None),
            P("rel", "ent", None, None),
            P("rel", "ent", None, None),
            P("rel", "ent", None, None),
            P("rel", "ent", None, None),
            P("rel", "ent", None),
        ),
        out_specs=(
            P(),
            P(),
            P(),
            P("ent", None),
            P("ent", None),
            P("ent", None),
            P("ent", None),
            P(None, ("rel", "ent"), None),
            P(None, ("rel", "ent"), None),
            P(None, ("rel", "ent"), None),
            P(None, ("rel", "ent"), None),
        ),
        check_vma=False,
    )
```

```python
import functools
import math

import jax
import jax.numpy as jnp
from jax import lax
from jax.experimental import pallas as pl
from jax.experimental.pallas import tpu as pltpu
from jax.sharding import PartitionSpec as P

STEP = 10
f32 = jnp.float32
bf16 = jnp.bfloat16
i32 = jnp.int32
MESH = pl.DeviceIdType.MESH


margin = 2.5
beta_one = 0.9
beta_two = 0.999
learn_rate = 0.05
decay_rate = 0.01
epsilon = 1e-16


def shortened(array):
    return jax.tree.map(lambda a: a.astype(jnp.bfloat16) if a.dtype == jnp.float32 else a, array)


def adamw(weight, moment, second, grad):
    moment = beta_one * moment + (1.0 - beta_one) * grad
    second = beta_two * second + (1.0 - beta_two) * grad * grad
    m_hat = moment / (1.0 - beta_one**STEP)
    v_hat = second / (1.0 - beta_two**STEP)
    weight = weight - learn_rate * (m_hat / (jnp.sqrt(v_hat) + epsilon) + decay_rate * weight)
    return (weight, moment, second)


def general_body(
    ent_table,
    entity_first_moment,
    ent_v,
    rel_table,
    relation_first_moment,
    rel_v,
    src_ids,
    rel_ids,
    dst_ids,
    neg_ids,
    bucket_counts,
):
    parts = src_ids.shape[2]
    slots = src_ids.shape[3]
    width = ent_table.shape[1]
    negcount = neg_ids.shape[3]
    clip_level = 0.01 / math.sqrt(lax.axis_size("rel") * lax.axis_size("ent") * parts * slots)
    ent_low = ent_table.astype(jnp.bfloat16)
    layers = lax.all_gather(rel_table.astype(jnp.bfloat16), "ent", axis=1, tiled=True)
    rel_sum = (
        layers[0].astype(jnp.float32)
        + layers[1].astype(jnp.float32)
        + layers[2].astype(jnp.float32)
    )
    sources = src_ids[0, 0]
    relation = rel_ids[0, 0]
    counts = bucket_counts[0, 0]
    hidden = ent_low[sources].astype(jnp.float32) + rel_sum[relation]
    total = lax.psum(jnp.sum(counts).astype(jnp.float32), ("rel", "ent"))
    arrived, dst_in, count_in = (
        lax.all_to_all(hidden.astype(jnp.bfloat16), "ent", split_axis=0, concat_axis=0, tiled=True),
        lax.all_to_all(dst_ids[0, 0], "ent", split_axis=0, concat_axis=0, tiled=True),
        lax.all_to_all(counts[:, None], "ent", split_axis=0, concat_axis=0, tiled=True),
    )
    live = (jnp.arange(slots, dtype=jnp.int32)[None, :] < count_in).astype(jnp.float32)
    negatives = neg_ids[0, 0]

    def block(args):
        hid, dst, neg, alive = args
        weight = alive / total
        hid_f = hid.astype(jnp.float32)
        diff = hid_f - ent_low[dst].astype(jnp.float32)
        pos_dist = jnp.sqrt(jnp.sum(diff * diff, -1) + 1.0)
        rows = ent_low[neg]
        rows_f = rows.astype(jnp.float32)
        prod = lax.dot_general(
            hid, rows, (((1,), (1,)), ((), ())), preferred_element_type=jnp.float32
        )
        sq = (
            jnp.sum(hid_f * hid_f, -1)[:, None] + jnp.sum(rows_f * rows_f, -1)[None, :] - 2.0 * prod
        )
        neg_dist = jnp.sqrt(sq + 1.0)
        per_edge = jax.nn.softplus(pos_dist - margin) + jnp.mean(
            jax.nn.softplus(margin - neg_dist), -1
        )
        loss = jnp.sum(alive * per_edge)
        g_pos = weight * jax.nn.sigmoid(pos_dist - margin)
        g_diff = (g_pos / pos_dist)[:, None] * diff
        g_sq = -(weight[:, None] / negcount) * jax.nn.sigmoid(margin - neg_dist) / (2.0 * neg_dist)
        g_prod = (-2.0 * g_sq).astype(jnp.bfloat16)
        g_hid = (
            g_diff
            + 2.0 * hid_f * jnp.sum(g_sq, 1)[:, None]
            + jnp.dot(g_prod, rows, preferred_element_type=jnp.float32)
        )
        g_rows = 2.0 * rows_f * jnp.sum(g_sq, 0)[:, None] + lax.dot_general(
            g_prod, hid, (((0,), (0,)), ((), ())), preferred_element_type=jnp.float32
        )
        return (loss, g_hid.astype(jnp.bfloat16), -g_diff, g_rows)

    losses, back, g_target, g_negative = lax.map(
        block, (arrived, dst_in, negatives, live), batch_size=min(4, parts)
    )
    returned = (
        jax.tree.map(
            lambda part, own: part.astype(own.dtype),
            lax.all_to_all(shortened(back), "ent", split_axis=0, concat_axis=0, tiled=True),
            back,
        )
        .reshape(-1, width)
        .astype(jnp.float32)
    )
    ent_grad = jnp.zeros(ent_table.shape, jnp.float32)
    ent_grad = ent_grad.at[dst_in.reshape(-1)].add(g_target.reshape(-1, width))
    ent_grad = ent_grad.at[negatives.reshape(-1)].add(g_negative.reshape(-1, width))
    ent_grad = ent_grad.at[sources.reshape(-1)].add(returned)
    ent_grad = lax.psum(ent_grad, "rel")
    rel_local = jnp.zeros(rel_sum.shape, jnp.float32).at[relation.reshape(-1)].add(returned)
    rel_grad = lax.psum_scatter(rel_local, "ent", scatter_dimension=0, tiled=True)
    own_squares = jnp.where(
        lax.axis_index("rel") == 0, jnp.sum(ent_grad * ent_grad), 0.0
    ) + 3.0 * jnp.sum(rel_grad * rel_grad)
    squares, loss_sum = lax.psum((own_squares, jnp.sum(losses)), ("rel", "ent"))
    grad_norm = jnp.sqrt(squares)
    scale = jnp.minimum(1.0, clip_level / grad_norm)
    new_ent, new_ent_m, new_ent_v = adamw(ent_table, entity_first_moment, ent_v, scale * ent_grad)
    new_rel, new_rel_m, new_rel_v = adamw(
        rel_table, relation_first_moment, rel_v, scale * rel_grad[None]
    )
    return (
        loss_sum,
        total,
        grad_norm,
        new_ent,
        new_ent_m,
        new_ent_v,
        new_ent.astype(jnp.bfloat16),
        new_rel,
        new_rel_m,
        new_rel_v,
        new_rel.astype(jnp.bfloat16),
    )


KT1=256
RP=256

def split3(x):
    hi=x.astype(bf16).astype(f32); r=x-hi
    mid=r.astype(bf16).astype(f32); lo=r-mid
    return hi,mid,lo

def place():
    r=lax.axis_index("rel"); e=lax.axis_index("ent")
    z=lax.div(e,2); k=lax.rem(e,2)
    xn=r+1-2*lax.rem(r,2)
    yn=lax.rem(r+2,4)
    return r,z,k,xn,yn

def gather_kernel(et_ref, rt_ref, src_ref, rid_ref, neg_ref,
                  tab_ref, h_ref, negout_ref,
                  tb, rall, eh, hb, lsem, hsem, us, ds, zr, xs, xr, ys, yr, fs, fr, cs, cr, rcs, rcr, ns, nr):
    width,ents=et_ref.shape
    nz=4; parts=8
    CK=ents//4
    cap=src_ref.shape[1]
    c,z,k,xn,yn=place()
    e=2*z+k
    half=208
    sib=2*z+1-k
    bar=pltpu.get_barrier_semaphore()
    for d in range(1,parts):
        pl.semaphore_signal(bar,inc=1,device_id=(c,lax.rem(e+d,parts)),device_id_type=MESH)
    pl.semaphore_signal(bar,inc=1,device_id=(xn,e),device_id_type=MESH)
    pl.semaphore_signal(bar,inc=1,device_id=(yn,e),device_id_type=MESH)
    tb[...]=et_ref[...].astype(bf16)
    low=[rt_ref[l].astype(bf16).astype(f32) for l in range(3)]
    rsum=jnp.concatenate([low[0]+low[1]+low[2],jnp.zeros((RP-rt_ref.shape[1],width),f32)],0)
    rall[e]=rsum.T.astype(bf16)
    pl.semaphore_wait(bar,parts+1)
    def rc(src,dst,s,r,to):
        return pltpu.make_async_remote_copy(src_ref=src,dst_ref=dst,send_sem=s,recv_sem=r,device_id=to,device_id_type=MESH)
    rows_of=(pl.ds(0,half),pl.ds(half,width-half))
    def lane(ck): return pl.ds(pl.multiple_of(ck*CK,CK),CK)
    SEQ=((2,1),(0,1),(2,2),(1,1),(2,3),(0,2),(1,2),(0,3),(1,3))
    def part(o,u,own=False):
        if u==2: return rall.at[2*o+k]
        return tb.at[rows_of[u],lane(c)] if own else tab_ref.at[2*o+k,rows_of[u],lane(c)]
    def up(o,u,own): return rc(part(o,u,own),part(o,u),us.at[u,o],zr.at[u,o],(c,2*(z+1)+k))
    def down(o,u,own): return rc(part(o,u,own),part(o,u),ds.at[u,o],zr.at[u,o],(c,2*(z-1)+k))
    def sides(dist,fn):
        @pl.when(z>=dist)
        def _(): fn(z-dist)
        @pl.when(z+dist<nz)
        def _(): fn(z+dist)
    def along(n,act):
        u,dist=SEQ[n]
        f=dist-1
        @pl.when(jnp.logical_and(z<nz-1,z>=f))
        def _(): act(up(z-f,u,f==0))
        @pl.when(jnp.logical_and(z>0,z+f<nz))
        def _(): act(down(z+f,u,f==0))
    def xc(o,h,l): return rc(tab_ref.at[2*o+k,rows_of[h],l],tab_ref.at[2*o+k,rows_of[h],l],xs.at[o,h],xr.at[o,h],(xn,e))
    def yc(o,h,l): return rc(tab_ref.at[2*o+k,rows_of[h],l],tab_ref.at[2*o+k,rows_of[h],l],ys.at[o,h],yr.at[o,h],(yn,e))
    def fc(o,h,l):
        v=tab_ref.at[2*o+k,rows_of[h],l]
        return rc(v,v,fs.at[o,h],fr.at[o,h],((yn,e),(xn,e))[h])
    def cc(o,h,kk,own=False):
        v=tab_ref.at[2*o+kk,rows_of[h],:]
        return rc(tb.at[rows_of[h],:] if own else v,v,cs.at[o,h],cr.at[o,h],(c,sib))
    def rel_sib(o,kk):
        return rc(rall.at[2*o+kk],rall.at[2*o+kk],rcs.at[o],rcr.at[o],(c,sib))
    along(0,lambda cp: cp.start())
    along(1,lambda cp: cp.start())
    rel_sib(z,k).start()
    def neg_copy(to,own):
        return rc(neg_ref.at[to],negout_ref.at[own],ns.at[to],nr.at[own],(c,to))
    for d in range(1,parts):
        neg_copy(lax.rem(e+d,parts),e).start()
    own_neg=pltpu.make_async_copy(neg_ref.at[e],negout_ref.at[e],lsem.at[1])
    own_neg.start()
    own_tab=pltpu.make_async_copy(tb,tab_ref.at[e],lsem.at[0])
    own_tab.start()
    for h in range(2): cc(z,h,k,True).start()
    def Z(n):
        u,dist=SEQ[n]
        def fn(o):
            up(o,u,False).wait_recv()
            if u==2: rel_sib(o,k).start()
            else:
                xc(o,u,lane(c)).start(); yc(o,u,lane(c)).start()
        sides(dist,fn)
        if n+2<len(SEQ): along(n+2,lambda cp: cp.start())
    def C(dist,h):
        def fn(o):
            if h==0: xc(o,0,lane(xn)).wait_recv(); fc(o,0,lane(xn)).start()
            else: yc(o,1,lane(yn)).wait_recv(); fc(o,1,lane(yn)).start()
        sides(dist,fn)
    def W(dist,h):
        def fn(o):
            if h==0: yc(o,0,lane(yn)).wait_recv()
            else: xc(o,1,lane(xn)).wait_recv()
            fc(o,h,lane(3-c)).wait_recv()
            cc(o,h,k).start()
        sides(dist,fn)
    def onehot(ids):
        return jnp.where(lax.broadcasted_iota(i32,(ents,KT1),0)==ids,1.0,0.0).astype(bf16)
    nt=cap//KT1
    def src_slot(b):
        def tile(t,_):
            l=pl.ds(pl.multiple_of(t*KT1,KT1),KT1)
            eh[b,:,l]=jnp.dot(tb[...],onehot(src_ref[b:b+1,l]),preferred_element_type=f32).astype(bf16)
            return 0
        lax.fori_loop(0,nt,tile,0)
    def out_copy(b):
        return pltpu.make_async_copy(hb.at[b%2],h_ref.at[pl.ds(b*cap,cap),:],hsem.at[b%2])
    nrel=rt_ref.shape[1]
    def rel_slot(b):
        if b>=2: out_copy(b-2).wait()
        def tile(t,_):
            l=pl.ds(pl.multiple_of(t*KT1,KT1),KT1)
            q=rid_ref[b:b+1,l]
            g=jnp.floor((q.astype(f32)+0.5)*(1.0/nrel)).astype(i32)
            q=q+(RP-nrel)*g
            acc=eh[b,:,l].astype(f32)
            for g0 in range(0,parts):
                oh=jnp.where(lax.broadcasted_iota(i32,(RP,KT1),0)+RP*g0==q,1.0,0.0).astype(bf16)
                acc=acc+jnp.dot(rall[g0],oh,preferred_element_type=f32)
            hid=acc.astype(bf16)
            hf=hid.astype(f32)
            hi,mid,lo=split3(jnp.sum(hf*hf,0,keepdims=True))
            row=lax.broadcasted_iota(i32,(hb.shape[2]-width,KT1),0)
            ex=jnp.where(row==0,hi,jnp.where(row==1,mid,jnp.where(row==2,lo,jnp.where(row<6,1.0,0.0))))
            hb[b%2,pl.ds(pl.multiple_of(t*KT1,KT1),KT1),:]=jnp.concatenate([hf,ex],0).T.astype(bf16)
            return 0
        lax.fori_loop(0,nt,tile,0)
        out_copy(b).start()
    def allrel():
        for o in range(nz): rel_sib(o,1-k).wait_recv()
    src_slot(0)
    src_slot(1)
    Z(0)
    src_slot(2)
    Z(1)
    src_slot(3)
    Z(2)
    src_slot(4)
    C(1,0)
    src_slot(5)
    Z(3)
    src_slot(6)
    Z(4)
    W(1,0)
    src_slot(7)
    C(1,1)
    Z(5)
    allrel()
    rel_slot(0)
    W(1,1)
    Z(6)
    rel_slot(1)
    C(2,0)
    Z(7)
    rel_slot(2)
    W(2,0)
    C(2,1)
    Z(8)
    rel_slot(3)
    W(2,1)
    C(3,0)
    rel_slot(4)
    C(3,1)
    W(3,0)
    rel_slot(5)
    W(3,1)
    rel_slot(6)
    rel_slot(7)
    for n in range(len(SEQ)): along(n,lambda cp: cp.wait_send())
    for h in range(2):
        for o in range(nz): cc(o,h,1-k).wait_recv()
        cc(z,h,k,True).wait_send()
        for dist in range(1,nz):
            def fn(o):
                cc(o,h,k).wait_send()
                xc(o,h,lane(c)).wait_send(); yc(o,h,lane(c)).wait_send()
                fc(o,h,(lane(xn),lane(yn))[h]).wait_send()
            sides(dist,fn)
    for o in range(nz): rel_sib(o,k).wait_send()
    for d in range(1,parts):
        o=lax.rem(e+d,parts)
        neg_copy(o,e).wait_send()
        neg_copy(e,o).wait_recv()
    own_tab.wait(); own_neg.wait()
    out_copy(6).wait(); out_copy(7).wait()

def gather_call(et,rt,src,rid,negs):
    width,ents=et.shape
    parts,cap=src.shape
    D=pltpu.SemaphoreType.DMA
    V=pl.BlockSpec(memory_space=pltpu.VMEM); A=pl.BlockSpec(memory_space=pl.ANY)
    return pl.pallas_call(gather_kernel,name="k1_gather",
        in_specs=[V]*5,out_specs=[A,A,V],
        out_shape=[jax.ShapeDtypeStruct((parts,width,ents),bf16),jax.ShapeDtypeStruct((parts*cap,512),bf16),jax.ShapeDtypeStruct(negs.shape,i32)],
        scratch_shapes=[pltpu.VMEM((width,ents),bf16),pltpu.VMEM((parts,width,RP),bf16),pltpu.VMEM((parts,width,cap),bf16),pltpu.VMEM((2,cap,512),bf16),
            D((2,)),D((2,)),D((3,4)),D((3,4)),D((3,4)),D((4,2)),D((4,2)),D((4,2)),D((4,2)),D((4,2)),D((4,2)),D((4,2)),D((4,2)),D((4,)),D((4,)),D((8,)),D((8,))],
        compiler_params=pltpu.CompilerParams(collective_id=1,has_side_effects=True,vmem_limit_bytes=60<<20))(et,rt,src,rid,negs)


KT = 256
WA=416
def block_kernel(width, ents, negcount, CH,
                 counts_ref, h_ref, t_ref, dst_ref, neg_ref, gh_ref, g_ref, loss_ref,
                 ta_ref, tr_ref, acc_ref, crow_ref, s_ref, lane_ref):
    j=pl.program_id(0)
    wa=ta_ref.shape[0]
    count=counts_ref[j]
    tiles=lax.div(count+(KT-1),KT)
    t=t_ref[0]
    tf=t.astype(f32)
    norm=(jnp.sum(tf*tf,0,keepdims=True)+1.0)*0.25
    hi,mid,lo=split3(norm)
    ta_ref[0:width,:]=t*bf16(-0.5)
    sub=lax.broadcasted_iota(jnp.int32,(wa-width,ents),0)
    pad=jnp.where(sub<3,0.25,0.0)
    pad=jnp.where(sub==3,hi,pad)
    pad=jnp.where(sub==4,mid,pad)
    pad=jnp.where(sub==5,lo,pad)
    ta_ref[width:,:]=pad.astype(bf16)
    tcat=jnp.concatenate([t, jnp.where(sub==0,1.0,0.0).astype(bf16)],0)
    tr_ref[...]=tcat.T
    ids=neg_ref[0]
    nn=ids.shape[1]
    ohi=jnp.where(lax.broadcasted_iota(jnp.int32,(ents//128,nn),0)==lax.shift_right_arithmetic(ids,7),1.0,0.0).astype(bf16)
    olo=jnp.where(lax.broadcasted_iota(jnp.int32,(128,nn),0)==(ids&127),1.0,0.0).astype(bf16)
    c=lax.dot_general(ohi,olo,(((1,),(1,)),((),())),preferred_element_type=f32)
    for i in range(ents//128):
        crow_ref[0:1,128*i:128*(i+1)]=c[i:i+1,:]
    acc_ref[...]=jnp.zeros_like(acc_ref)
    def dead(kt,_):
        gh_ref[pl.ds(pl.multiple_of(kt*KT,KT),KT),:]=jnp.zeros((KT,gh_ref.shape[1]),bf16)
        return 0
    lax.fori_loop(tiles,gh_ref.shape[0]//KT,dead,0)
    @pl.when(j==0)
    def _(): loss_ref[...]=jnp.zeros_like(loss_ref)
    first=jnp.logical_and(lax.broadcasted_iota(jnp.int32,(8,128),0)==0,lax.broadcasted_iota(jnp.int32,(8,128),1)==0)
    loss_ref[8:16,:]+=jnp.where(first,count.astype(f32),0.0)
    eye=lax.broadcasted_iota(jnp.int32,(KT,KT),0)==lax.broadcasted_iota(jnp.int32,(KT,KT),1)
    lane_ref[...]=lax.broadcasted_iota(jnp.int32,lane_ref.shape,1)
    nch=ents//CH
    def rows_of(kt): return pl.ds(pl.multiple_of(kt*KT,KT),KT)
    def live_of(kt): return (lax.broadcasted_iota(jnp.int32,(KT,1),0)+kt*KT)<count
    def idcol(kt):
        idr=dst_ref[0,pl.ds(kt,1),:].astype(f32)
        return jnp.sum(jnp.where(eye,idr,0.0),1,keepdims=True).astype(jnp.int32)
    def aug(kt):
        hb=h_ref[rows_of(kt),:]
        last=hb[:,width//128*128:wa].astype(f32)
        lane=lax.broadcasted_iota(jnp.int32,last.shape,1)+width//128*128
        last=jnp.where(jnp.logical_and(lane==width,jnp.logical_not(live_of(kt))),4e6,last)
        return jnp.concatenate([hb[:,:width//128*128],last.astype(bf16)],1)
    def sdot(ha,ci): return jnp.dot(ha,ta_ref[:,ci*CH:(ci+1)*CH],preferred_element_type=f32)
    def post(s,idc,ci,sp):
        es=jnp.where(idc==lane_ref[0:1,ci*CH:(ci+1)*CH],s,0.0)
        for a in range(CH//128): sp=sp+es[:,128*a:128*(a+1)]
        s_ref[:,ci*CH:(ci+1)*CH]=s
        return sp
    def column(sp,kt):
        live=live_of(kt)
        sq=jnp.sum(sp,1,keepdims=True)*4.0
        rr=lax.rsqrt(sq)
        x=sq*rr-margin
        a=jnp.where(live,jax.nn.sigmoid(x)*rr,0.0)
        inva=jnp.where(live,1.0/a,0.0)
        pos=jnp.where(live,jnp.maximum(x,0.0)+jnp.log(1.0+jnp.exp(-jnp.abs(x))),0.0)
        p8=pos[0:8]
        for b in range(1,KT//8): p8+=pos[8*b:8*b+8]
        loss_ref[0:8,:]+=jnp.where(lax.broadcasted_iota(jnp.int32,(8,128),1)==0,p8,0.0)
        return a,inva
    ha=aug(0); idc=idcol(0); sp=jnp.zeros((KT,128),f32)
    for ci in range(nch): sp=post(sdot(ha,ci),idc,ci,sp)
    a0,i0=column(sp,0)
    def tile(kt,carry):
        rho,inva,idc=carry
        nk=jnp.minimum(kt+1,tiles-1)
        hb=h_ref[rows_of(kt),:]
        hf=hb[:,:width].astype(f32)
        hi,mid,lo=split3(rho)
        ex=lax.broadcasted_iota(jnp.int32,(KT,wa-width),1)
        pad=jnp.where(ex==0,hi,jnp.where(ex==1,mid,jnp.where(ex==2,lo,0.0)))
        hat=jnp.concatenate([(hf*rho),pad],1).astype(bf16).T
        ha=aug(nk); nidc=idcol(nk)
        gh=jnp.zeros((KT,wa),f32)
        sp=jnp.zeros((KT,128),f32)
        lsum=jnp.zeros((8,CH),f32)
        rs=jnp.zeros((KT,128),f32)
        ms=[None]*nch
        invn=inva*(0.25/negcount)
        pend=None
        for ci in range(nch+1):
            if ci<nch:
                cols=slice(ci*CH,(ci+1)*CH)
                s=s_ref[:,cols]
                r=lax.rsqrt(s)
                th=jnp.tanh(margin*0.5-s*r)
                sp=post(sdot(ha,ci),nidc,ci,sp)
                cr=crow_ref[0:1,cols]
                mask=idc==lane_ref[0:1,cols]
                xf=((1.0+th)*cr)*(r*invn)
                for b in range(CH//128): rs=rs+xf[:,128*b:128*(b+1)]
                ms[ci]=(jnp.where(mask,1.0,0.0)-xf).astype(bf16)
                o=1.0-th
                p=o[0:8]
                for b in range(1,KT//8): p=p*o[8*b:8*b+8]
                lsum+=(math.log(2.0)*(KT//8)-jnp.log(p))*cr
            if ci>=1:
                pc=slice((ci-1)*CH,ci*CH)
                gh+=jnp.dot(ms[ci-1],tr_ref[pc,:],preferred_element_type=f32)
                acc_ref[:,pc]+=jnp.dot(hat,ms[ci-1],preferred_element_type=f32)
        l8=lsum[:,0:128]
        for b in range(1,CH//128): l8+=lsum[:,128*b:128*(b+1)]
        loss_ref[0:8,:]+=l8*(1.0/negcount)
        out=(hf*(1.0-jnp.sum(rs,1,keepdims=True))-gh[:,:width])*rho
        gh_ref[rows_of(kt),:width]=out.astype(bf16)
        live=kt+1<tiles
        na,ni=column(jnp.where(live,sp,1.0),jnp.where(live,nk,tiles))
        return na,ni,nidc
    lax.fori_loop(0,tiles,tile,(a0,i0,idc))
    g_ref[0]=tf*acc_ref[width:width+1,:]+tf*acc_ref[width+1:width+2,:]+tf*acc_ref[width+2:width+3,:]-acc_ref[0:width,:]

def run_blocks(h,tables,dst,neg,counts,negcount,CH=256):
    parts,width,ents=tables.shape
    cap=h.shape[0]//parts
    wa=WA
    nn=neg.shape[-1]
    gs=pltpu.PrefetchScalarGridSpec(num_scalar_prefetch=1,grid=(parts,),
      in_specs=[pl.BlockSpec((cap,h.shape[1]),lambda j,c:(j,0)),
                pl.BlockSpec((1,width,ents),lambda j,c:(j,0,0)),
                pl.BlockSpec((1,cap//KT,KT),lambda j,c:(j,0,0)),
                pl.BlockSpec((1,1,nn),lambda j,c:(j,0,0))],
      out_specs=[pl.BlockSpec((cap,width),lambda j,c:(j,0)),
                 pl.BlockSpec((1,width,ents),lambda j,c:(j,0,0)),
                 pl.BlockSpec((16,128),lambda j,c:(0,0))],
      scratch_shapes=[pltpu.VMEM((wa,ents),bf16),pltpu.VMEM((ents,wa),bf16),
                      pltpu.VMEM((wa,ents),f32),pltpu.VMEM((8,ents),f32),pltpu.VMEM((KT,ents),f32),pltpu.VMEM((8,ents),jnp.int32)])
    return pl.pallas_call(functools.partial(block_kernel,width,ents,negcount,CH),grid_spec=gs,name="k2_blocks",
      out_shape=[jax.ShapeDtypeStruct((h.shape[0],width),bf16),jax.ShapeDtypeStruct(tables.shape,f32),jax.ShapeDtypeStruct((16,128),f32)],
      compiler_params=pltpu.CompilerParams(vmem_limit_bytes=60<<20,dimension_semantics=("arbitrary",)))(counts,h,tables,dst,neg)


HALF=208

def reduce_kernel(g_ref, gh_ref, src_ref, rid_ref, sc_ref,
                  ge_ref, gr_ref, sco_ref,
                  pr, own, sacc, racc, sa0, sa1, ra0, ra1, sb0, sb1, rb0, rb1, sz, rz, ghb, rp, rsz, rzr, scb,
                  ps, prr, osem, gsem, sas, sar, sbs, sbr, zs, zr, rps, rpr, rzs, rzrr, gxs, gxr, gys, gyr, gds, gdr, css, csr, czs, czr):
    parts,width,ents=g_ref.shape
    nz=4; CK=ents//4; last=nz-1
    cap=src_ref.shape[1]
    nrel=gr_ref.shape[0]
    c,z,k,xn,yn=place()
    e=2*z+k; sib=2*z+1-k
    x=lax.rem(c,2); y=lax.div(c,2); xo=1-x; yo=1-y
    bar=pltpu.get_barrier_semaphore()
    for to in ((c,sib),(xn,e),(yn,e))+tuple((c,lax.rem(e+2*d,parts)) for d in range(1,nz)):
        pl.semaphore_signal(bar,inc=1,device_id=to,device_id_type=MESH)
    order=[lax.rem(z+1+i,nz) for i in range(nz)]
    rows_of=(pl.ds(0,HALF),pl.ds(HALF,width-HALF))
    lo=(0,HALF); num=(HALF,width-HALF)
    def load(i): return pltpu.make_async_copy(g_ref.at[2*order[i]+k],own.at[i%2],osem.at[i%2])
    def gload(b): return pltpu.make_async_copy(gh_ref.at[pl.ds(b*cap,cap),:],ghb.at[b%2],gsem.at[b%2])
    gload(0).start(); load(0).start(); load(1).start()
    pl.semaphore_wait(bar,nz+2)
    def rc(src,dst,s,r,to):
        return pltpu.make_async_remote_copy(src_ref=src,dst_ref=dst,send_sem=s,recv_sem=r,device_id=to,device_id_type=MESH)
    def pair(i,h): return rc(g_ref.at[2*order[i]+1-k,rows_of[h],:],pr.at[i,rows_of[h],:],ps.at[i,h],prr.at[i,h],(c,sib))
    for i in range(2):
        for h in range(2): pair(i,h).start()
    def lane(ck,n=1): return pl.ds(pl.multiple_of(ck*CK,CK),n*CK)
    near=((xn,e),(yn,e)); sa=(sa0,sa1); ra=(ra0,ra1); sb=(sb0,sb1); rb=(rb0,rb1)
    def ac(i,h): return rc(sa[h].at[i],ra[h].at[i],sas.at[i,h],sar.at[i,h],near[h])
    def bc(i,h): return rc(sb[h].at[i],rb[h].at[i],sbs.at[i,h],sbr.at[i,h],near[1-h])
    def zc(i,h): return rc(sz.at[i,rows_of[h],:],rz.at[i,rows_of[h],:],zs.at[i,h],zr.at[i,h],(c,2*order[i]+k))
    gone=((xo,xo+2),(2*yo,2*yo+1))
    kept=((x,x+2),(2*y,2*y+1))
    passed=(x+2*yo,2*y+xo)
    mine=(y,x)
    RB=16
    def strips(h,fn):
        fn(rows_of[h],pl.ds(0,num[h]))
    def st0(i,h):
        if h==0 and i!=last: load(i).wait()
        pair(i,h).wait_recv()
        def one(rows,rel):
            for s in range(2):
                l=lane(gone[h][s])
                sa[h][i,rel,s*CK:(s+1)*CK]=(pr[i,rows,l]+own[i%2,rows,l]).astype(bf16)
                l=lane(kept[h][s])
                pr[i,rows,l]=pr[i,rows,l]+own[i%2,rows,l]
        strips(h,one)
        ac(i,h).start()
        if h==1 and i+2<nz:
            load(i+2).start()
            for g in range(2): pair(i+2,g).start()
    def stB(i,h):
        ac(i,h).wait_recv()
        def one(rows,rel):
            sb[h][i,rel,:]=(pr[i,rows,lane(passed[h])]+ra[h][i,rel,lane(1-mine[h])].astype(f32)).astype(sb0.dtype)
            pr[i,rows,lane(c)]=pr[i,rows,lane(c)]+ra[h][i,rel,lane(mine[h])].astype(f32)
        strips(h,one)
        bc(i,h).start()
    def stZ(i,h):
        bc(i,h).wait_recv()
        def one(rows,rel):
            v=pr[i,rows,lane(c)]+rb[h][i,rel,:].astype(f32)
            if i==last: ge_ref[rows,lane(c)]=v
            else: sz[i,rows,:]=v.astype(sz.dtype)
        strips(h,one)
        if i!=last: zc(i,h).start()
    def both(fn,i):
        fn(i,0); fn(i,1)
    def getblock(b):
        gload(b).wait()
        gload((b+1)%parts).start()
    def slot(ids_ref,acc,b,RC):
        ids=ids_ref[b:b+1,:]
        def chunk(t,_):
            rows=pl.ds(pl.multiple_of(t*RC,8),RC)
            oh=jnp.where(lax.broadcasted_iota(i32,(RC,cap),0)==ids-t*RC,1.0,0.0).astype(bf16)
            d=jnp.dot(oh,ghb[b%2],preferred_element_type=f32)
            if b==0: acc[rows,:]=d
            else: acc[rows,:]=acc[rows,:]+d
            return 0
        lax.fori_loop(0,acc.shape[0]//RC,chunk,0)
    def src(b):
        getblock(b); slot(src_ref,sacc,b,CK)
    def rel(b):
        getblock(b); slot(rid_ref,racc,b,2*nrel)
    def addsrc():
        def it(t,_):
            l=pl.ds(pl.multiple_of(t*128,128),128)
            own[last%2,:,l]=own[last%2,:,l]+sacc[l,:].T
            return 0
        lax.fori_loop(0,ents//128,it,0)
    def grp(g): return pl.ds(pl.multiple_of(g*nrel,8),nrel)
    def relpair(i): return rc(racc.at[grp(2*order[i]+1-k),:],rp.at[i],rps.at[i],rpr.at[i],(c,sib))
    def relz(i): return rc(rsz.at[i],rzr.at[i],rzs.at[i],rzrr.at[i],(c,2*order[i]+k))
    src(0)
    src(1)
    both(st0,0)
    src(2)
    src(3)
    both(st0,1)
    src(4)
    both(stB,0)
    src(5)
    src(6)
    both(st0,2)
    src(7)
    load(last).wait()
    addsrc()
    both(stB,1)
    both(stZ,0)
    rel(0)
    rel(1)
    both(st0,3)
    rel(2)
    both(stB,2)
    both(stZ,1)
    rel(3)
    rel(4)
    rel(5)
    both(stB,3)
    rel(6)
    both(stZ,2)
    rel(7)
    for i in range(nz): relpair(i).start()
    for i in range(last):
        relpair(i).wait_recv()
        rsz[i]=(racc[grp(2*order[i]+k),:]+rp[i]).astype(rsz.dtype)
        relz(i).start()
    both(stZ,3)
    gload(0).wait()
    sq=jnp.zeros((RB,CK),f32)
    def gx(h,l): return rc(ge_ref.at[rows_of[h],l],ge_ref.at[rows_of[h],l],gxs.at[h],gxr.at[h],(xn,e))
    def gy(h,l): return rc(ge_ref.at[rows_of[h],l],ge_ref.at[rows_of[h],l],gys.at[h],gyr.at[h],(yn,e))
    def gd(h,l): return rc(ge_ref.at[rows_of[h],l],ge_ref.at[rows_of[h],l],gds.at[h],gdr.at[h],near[1-h])
    for h in range(2):
        for i in range(last): zc(i,h).wait_recv()
        rows=rows_of[h]
        v=ge_ref[rows,lane(c)]
        for i in range(last): v=v+rz[i,rows,:].astype(f32)
        ge_ref[rows,lane(c)]=v
        v=v*v
        for b in range(0,num[h],RB): sq=sq+v[b:b+RB]
        if h==0: gx(0,lane(c)).start()
        else: gy(1,lane(c)).start()
    gy(0,lane(c)).start(); gx(1,lane(c)).start()
    relpair(last).wait_recv()
    rv=racc[grp(e),:]+rp[last]
    for i in range(last):
        relz(i).wait_recv()
        rv=rv+rzr[i].astype(f32)
    gr_ref[...]=rv
    one=jnp.sum(sq)+3.0*jnp.sum(rv*rv)
    row=lax.broadcasted_iota(i32,(8,128),0)
    v=jnp.where(row==0,one,jnp.where(row==1,jnp.sum(sc_ref[0:8,:]),jnp.where(row==2,jnp.sum(sc_ref[8:16,:]),0.0)))
    def swap(s,v,to):
        scb[s]=v
        cp=rc(scb.at[s],scb.at[3+s],css.at[s],csr.at[s],to)
        cp.start(); cp.wait()
        return v+scb[3+s]
    v=swap(0,v,(c,sib))
    scb[6+z]=v
    def cz(d): return rc(scb.at[6+z],scb.at[6+z],czs.at[d],czr.at[d],(c,lax.rem(e+2*d,parts)))
    for d in range(1,nz): cz(d).start()
    gx(0,lane(xn)).wait_recv(); gd(0,lane(xn)).start()
    gy(1,lane(yn)).wait_recv(); gd(1,lane(yn)).start()
    for d in range(1,nz): cz(d).wait()
    v=(scb[6]+scb[7])+(scb[8]+scb[9])
    v=swap(1,v,(xn,e))
    v=swap(2,v,(yn,e))
    live=v[2:3,:]
    norm=jnp.sqrt(v[0:1,:])/live
    clip=0.01/math.sqrt(4*parts*parts*cap)
    scale=jnp.minimum(1.0,clip/norm)/live
    sco_ref[...]=jnp.where(row==0,norm,jnp.where(row==3,scale,v))
    gx(1,lane(xn)).wait_recv(); gy(0,lane(yn)).wait_recv()
    gd(0,lane(3-c)).wait_recv(); gd(1,lane(3-c)).wait_recv()
    for h in range(2):
        gx(h,lane(c)).wait_send(); gy(h,lane(c)).wait_send()
        for i in range(nz):
            pair(i,h).wait_send(); ac(i,h).wait_send(); bc(i,h).wait_send()
            if i<last: zc(i,h).wait_send()
    gd(0,lane(xn)).wait_send(); gd(1,lane(yn)).wait_send()
    for i in range(nz):
        relpair(i).wait_send()
        if i<last: relz(i).wait_send()

def reduce_call(g,gh,src,rid,sc,nrel,BT=bf16,ZT=bf16,RT=bf16):
    parts,width,ents=g.shape
    cap=src.shape[1]; nz=4; CK=ents//4
    D=pltpu.SemaphoreType.DMA
    V=pl.BlockSpec(memory_space=pltpu.VMEM); A=pl.BlockSpec(memory_space=pl.ANY)
    VM=pltpu.VMEM
    rest=width-HALF
    return pl.pallas_call(reduce_kernel,name="k3_reduce",
        in_specs=[A,A,V,V,V],out_specs=[V,V,V],
        out_shape=[jax.ShapeDtypeStruct((width,ents),f32),jax.ShapeDtypeStruct((nrel,width),f32),jax.ShapeDtypeStruct((8,128),f32)],
        scratch_shapes=[VM((nz,width,ents),f32),VM((2,width,ents),f32),VM((ents,width),f32),VM((parts*nrel,width),f32),
            VM((nz,HALF,2*CK),bf16),VM((nz,rest,2*CK),bf16),VM((nz,HALF,2*CK),bf16),VM((nz,rest,2*CK),bf16),
            VM((nz,HALF,CK),BT),VM((nz,rest,CK),BT),VM((nz,HALF,CK),BT),VM((nz,rest,CK),BT),
            VM((nz-1,width,CK),ZT),VM((nz-1,width,CK),ZT),
            VM((2,cap,width),bf16),VM((nz,nrel,width),f32),VM((nz-1,nrel,width),RT),VM((nz-1,nrel,width),RT),VM((10,8,128),f32),
            D((4,2)),D((4,2)),D((2,)),D((2,)),D((4,2)),D((4,2)),D((4,2)),D((4,2)),D((3,2)),D((3,2)),D((4,)),D((4,)),D((3,)),D((3,)),
            D((2,)),D((2,)),D((2,)),D((2,)),D((2,)),D((2,)),D((3,)),D((3,)),D((4,)),D((4,))],
        compiler_params=pltpu.CompilerParams(collective_id=2,has_side_effects=True,vmem_limit_bytes=62<<20))(g,gh,src,rid,sc)


def cube_body(
    ent_table,
    entity_first_moment,
    ent_v,
    rel_table,
    relation_first_moment,
    rel_v,
    src_ids,
    rel_ids,
    dst_ids,
    neg_ids,
    bucket_counts,
):
    parts = src_ids.shape[2]
    negcount = neg_ids.shape[3]
    nrel = rel_table.shape[1]
    padded = -(-negcount // 1024) * 1024
    negs = jnp.pad(neg_ids[0, 0], ((0, 0), (0, padded - negcount)), constant_values=-1)
    tables, hidden, arrived = gather_call(
        ent_table.T, rel_table, src_ids[0, 0], rel_ids[0, 0], negs.reshape(parts, -1, 128)
    )
    back, partial, sums = run_blocks(
        hidden,
        tables,
        dst_ids[0, 0].reshape(parts, -1, KT),
        arrived.reshape(parts, 1, padded),
        bucket_counts[0, 0],
        negcount,
    )
    ent_grad, rel_grad, totals = reduce_call(
        partial, back, src_ids[0, 0], rel_ids[0, 0], sums, nrel
    )
    grad_norm, loss_sum, total, scale = totals[0, 0], totals[1, 0], totals[2, 0], totals[3, 0]
    new_ent, new_ent_m, new_ent_v = adamw(ent_table, entity_first_moment, ent_v, scale * ent_grad.T)
    new_rel, new_rel_m, new_rel_v = adamw(
        rel_table, relation_first_moment, rel_v, scale * rel_grad[None]
    )
    return (
        loss_sum,
        total,
        grad_norm,
        new_ent,
        new_ent_m,
        new_ent_v,
        new_ent.astype(jnp.bfloat16),
        new_rel,
        new_rel_m,
        new_rel_v,
        new_rel.astype(jnp.bfloat16),
    )


def solution(mesh):
    body = cube_body if mesh.shape["rel"] == 4 and mesh.shape["ent"] == 8 else general_body
    return jax.shard_map(
        body,
        mesh=mesh,
        in_specs=(
            P("ent", None),
            P("ent", None),
            P("ent", None),
            P(None, ("rel", "ent"), None),
            P(None, ("rel", "ent"), None),
            P(None, ("rel", "ent"), None),
            P("rel", "ent", None, None),
            P("rel", "ent", None, None),
            P("rel", "ent", None, None),
            P("rel", "ent", None, None),
            P("rel", "ent", None),
        ),
        out_specs=(
            P(),
            P(),
            P(),
            P("ent", None),
            P("ent", None),
            P("ent", None),
            P("ent", None),
            P(None, ("rel", "ent"), None),
            P(None, ("rel", "ent"), None),
            P(None, ("rel", "ent"), None),
            P(None, ("rel", "ent"), None),
        ),
        check_vma=False,
    )
```

```python
import functools
import math

import jax
import jax.numpy as jnp
from jax import lax
from jax.experimental import pallas as pl
from jax.experimental.pallas import tpu as pltpu
from jax.sharding import PartitionSpec as P

STEP = 10
f32 = jnp.float32
bf16 = jnp.bfloat16
i32 = jnp.int32
MESH = pl.DeviceIdType.MESH


margin = 2.5
beta_one = 0.9
beta_two = 0.999
learn_rate = 0.05
decay_rate = 0.01
epsilon = 1e-16


def shortened(array):
    return jax.tree.map(lambda a: a.astype(jnp.bfloat16) if a.dtype == jnp.float32 else a, array)


def adamw(weight, moment, second, grad):
    moment = beta_one * moment + (1.0 - beta_one) * grad
    second = beta_two * second + (1.0 - beta_two) * grad * grad
    m_hat = moment / (1.0 - beta_one**STEP)
    v_hat = second / (1.0 - beta_two**STEP)
    weight = weight - learn_rate * (m_hat / (jnp.sqrt(v_hat) + epsilon) + decay_rate * weight)
    return (weight, moment, second)


def general_body(
    ent_table,
    entity_first_moment,
    ent_v,
    rel_table,
    relation_first_moment,
    rel_v,
    src_ids,
    rel_ids,
    dst_ids,
    neg_ids,
    bucket_counts,
):
    parts = src_ids.shape[2]
    slots = src_ids.shape[3]
    width = ent_table.shape[1]
    negcount = neg_ids.shape[3]
    clip_level = 0.01 / math.sqrt(lax.axis_size("rel") * lax.axis_size("ent") * parts * slots)
    ent_low = ent_table.astype(jnp.bfloat16)
    layers = lax.all_gather(rel_table.astype(jnp.bfloat16), "ent", axis=1, tiled=True)
    rel_sum = (
        layers[0].astype(jnp.float32)
        + layers[1].astype(jnp.float32)
        + layers[2].astype(jnp.float32)
    )
    sources = src_ids[0, 0]
    relation = rel_ids[0, 0]
    counts = bucket_counts[0, 0]
    hidden = ent_low[sources].astype(jnp.float32) + rel_sum[relation]
    total = lax.psum(jnp.sum(counts).astype(jnp.float32), ("rel", "ent"))
    arrived, dst_in, count_in = (
        lax.all_to_all(hidden.astype(jnp.bfloat16), "ent", split_axis=0, concat_axis=0, tiled=True),
        lax.all_to_all(dst_ids[0, 0], "ent", split_axis=0, concat_axis=0, tiled=True),
        lax.all_to_all(counts[:, None], "ent", split_axis=0, concat_axis=0, tiled=True),
    )
    live = (jnp.arange(slots, dtype=jnp.int32)[None, :] < count_in).astype(jnp.float32)
    negatives = neg_ids[0, 0]

    def block(args):
        hid, dst, neg, alive = args
        weight = alive / total
        hid_f = hid.astype(jnp.float32)
        diff = hid_f - ent_low[dst].astype(jnp.float32)
        pos_dist = jnp.sqrt(jnp.sum(diff * diff, -1) + 1.0)
        rows = ent_low[neg]
        rows_f = rows.astype(jnp.float32)
        prod = lax.dot_general(
            hid, rows, (((1,), (1,)), ((), ())), preferred_element_type=jnp.float32
        )
        sq = (
            jnp.sum(hid_f * hid_f, -1)[:, None] + jnp.sum(rows_f * rows_f, -1)[None, :] - 2.0 * prod
        )
        neg_dist = jnp.sqrt(sq + 1.0)
        per_edge = jax.nn.softplus(pos_dist - margin) + jnp.mean(
            jax.nn.softplus(margin - neg_dist), -1
        )
        loss = jnp.sum(alive * per_edge)
        g_pos = weight * jax.nn.sigmoid(pos_dist - margin)
        g_diff = (g_pos / pos_dist)[:, None] * diff
        g_sq = -(weight[:, None] / negcount) * jax.nn.sigmoid(margin - neg_dist) / (2.0 * neg_dist)
        g_prod = (-2.0 * g_sq).astype(jnp.bfloat16)
        g_hid = (
            g_diff
            + 2.0 * hid_f * jnp.sum(g_sq, 1)[:, None]
            + jnp.dot(g_prod, rows, preferred_element_type=jnp.float32)
        )
        g_rows = 2.0 * rows_f * jnp.sum(g_sq, 0)[:, None] + lax.dot_general(
            g_prod, hid, (((0,), (0,)), ((), ())), preferred_element_type=jnp.float32
        )
        return (loss, g_hid.astype(jnp.bfloat16), -g_diff, g_rows)

    losses, back, g_target, g_negative = lax.map(
        block, (arrived, dst_in, negatives, live), batch_size=min(4, parts)
    )
    returned = (
        jax.tree.map(
            lambda part, own: part.astype(own.dtype),
            lax.all_to_all(shortened(back), "ent", split_axis=0, concat_axis=0, tiled=True),
            back,
        )
        .reshape(-1, width)
        .astype(jnp.float32)
    )
    ent_grad = jnp.zeros(ent_table.shape, jnp.float32)
    ent_grad = ent_grad.at[dst_in.reshape(-1)].add(g_target.reshape(-1, width))
    ent_grad = ent_grad.at[negatives.reshape(-1)].add(g_negative.reshape(-1, width))
    ent_grad = ent_grad.at[sources.reshape(-1)].add(returned)
    ent_grad = lax.psum(ent_grad, "rel")
    rel_local = jnp.zeros(rel_sum.shape, jnp.float32).at[relation.reshape(-1)].add(returned)
    rel_grad = lax.psum_scatter(rel_local, "ent", scatter_dimension=0, tiled=True)
    own_squares = jnp.where(
        lax.axis_index("rel") == 0, jnp.sum(ent_grad * ent_grad), 0.0
    ) + 3.0 * jnp.sum(rel_grad * rel_grad)
    squares, loss_sum = lax.psum((own_squares, jnp.sum(losses)), ("rel", "ent"))
    grad_norm = jnp.sqrt(squares)
    scale = jnp.minimum(1.0, clip_level / grad_norm)
    new_ent, new_ent_m, new_ent_v = adamw(ent_table, entity_first_moment, ent_v, scale * ent_grad)
    new_rel, new_rel_m, new_rel_v = adamw(
        rel_table, relation_first_moment, rel_v, scale * rel_grad[None]
    )
    return (
        loss_sum,
        total,
        grad_norm,
        new_ent,
        new_ent_m,
        new_ent_v,
        new_ent.astype(jnp.bfloat16),
        new_rel,
        new_rel_m,
        new_rel_v,
        new_rel.astype(jnp.bfloat16),
    )


KT1=256
RP=256

def split3(x):
    hi=x.astype(bf16).astype(f32); r=x-hi
    mid=r.astype(bf16).astype(f32); lo=r-mid
    return hi,mid,lo

def place():
    r=lax.axis_index("rel"); e=lax.axis_index("ent")
    z=lax.div(e,2); k=lax.rem(e,2)
    xn=r+1-2*lax.rem(r,2)
    yn=lax.rem(r+2,4)
    return r,z,k,xn,yn

def gather_kernel(et_ref, rt_ref, src_ref, rid_ref, neg_ref,
                  tab_ref, h_ref, negout_ref,
                  tb, rall, eh, hb, lsem, hsem, us, ds, zr, xs, xr, ys, yr, fs, fr, cs, cr, rcs, rcr, ns, nr):
    width,ents=et_ref.shape
    nz=4; parts=8
    CK=ents//4
    cap=src_ref.shape[1]
    c,z,k,xn,yn=place()
    e=2*z+k
    half=208
    sib=2*z+1-k
    bar=pltpu.get_barrier_semaphore()
    for d in range(1,parts):
        pl.semaphore_signal(bar,inc=1,device_id=(c,lax.rem(e+d,parts)),device_id_type=MESH)
    pl.semaphore_signal(bar,inc=1,device_id=(xn,e),device_id_type=MESH)
    pl.semaphore_signal(bar,inc=1,device_id=(yn,e),device_id_type=MESH)
    tb[...]=et_ref[...].astype(bf16)
    low=[rt_ref[l].astype(bf16).astype(f32) for l in range(3)]
    rsum=jnp.concatenate([low[0]+low[1]+low[2],jnp.zeros((RP-rt_ref.shape[1],width),f32)],0)
    rall[e]=rsum.T.astype(bf16)
    pl.semaphore_wait(bar,parts+1)
    def rc(src,dst,s,r,to):
        return pltpu.make_async_remote_copy(src_ref=src,dst_ref=dst,send_sem=s,recv_sem=r,device_id=to,device_id_type=MESH)
    rows_of=(pl.ds(0,half),pl.ds(half,width-half))
    def lane(ck): return pl.ds(pl.multiple_of(ck*CK,CK),CK)
    SEQ=((2,1),(0,1),(2,2),(1,1),(2,3),(0,2),(1,2),(0,3),(1,3))
    def part(o,u,own=False):
        if u==2: return rall.at[2*o+k]
        return tb.at[rows_of[u],lane(c)] if own else tab_ref.at[2*o+k,rows_of[u],lane(c)]
    def up(o,u,own): return rc(part(o,u,own),part(o,u),us.at[u,o],zr.at[u,o],(c,2*(z+1)+k))
    def down(o,u,own): return rc(part(o,u,own),part(o,u),ds.at[u,o],zr.at[u,o],(c,2*(z-1)+k))
    def sides(dist,fn):
        @pl.when(z>=dist)
        def _(): fn(z-dist)
        @pl.when(z+dist<nz)
        def _(): fn(z+dist)
    def along(n,act):
        u,dist=SEQ[n]
        f=dist-1
        @pl.when(jnp.logical_and(z<nz-1,z>=f))
        def _(): act(up(z-f,u,f==0))
        @pl.when(jnp.logical_and(z>0,z+f<nz))
        def _(): act(down(z+f,u,f==0))
    def xc(o,h,l): return rc(tab_ref.at[2*o+k,rows_of[h],l],tab_ref.at[2*o+k,rows_of[h],l],xs.at[o,h],xr.at[o,h],(xn,e))
    def yc(o,h,l): return rc(tab_ref.at[2*o+k,rows_of[h],l],tab_ref.at[2*o+k,rows_of[h],l],ys.at[o,h],yr.at[o,h],(yn,e))
    def fc(o,h,l):
        v=tab_ref.at[2*o+k,rows_of[h],l]
        return rc(v,v,fs.at[o,h],fr.at[o,h],((yn,e),(xn,e))[h])
    def cc(o,h,kk,own=False):
        v=tab_ref.at[2*o+kk,rows_of[h],:]
        return rc(tb.at[rows_of[h],:] if own else v,v,cs.at[o,h],cr.at[o,h],(c,sib))
    def rel_sib(o,kk):
        return rc(rall.at[2*o+kk],rall.at[2*o+kk],rcs.at[o],rcr.at[o],(c,sib))
    along(0,lambda cp: cp.start())
    along(1,lambda cp: cp.start())
    rel_sib(z,k).start()
    def neg_copy(to,own):
        return rc(neg_ref.at[to],negout_ref.at[own],ns.at[to],nr.at[own],(c,to))
    for d in range(1,parts):
        neg_copy(lax.rem(e+d,parts),e).start()
    own_neg=pltpu.make_async_copy(neg_ref.at[e],negout_ref.at[e],lsem.at[1])
    own_neg.start()
    own_tab=pltpu.make_async_copy(tb,tab_ref.at[e],lsem.at[0])
    own_tab.start()
    for h in range(2): cc(z,h,k,True).start()
    def Z(n):
        u,dist=SEQ[n]
        def fn(o):
            up(o,u,False).wait_recv()
            if u==2: rel_sib(o,k).start()
            else:
                xc(o,u,lane(c)).start(); yc(o,u,lane(c)).start()
        sides(dist,fn)
        if n+2<len(SEQ): along(n+2,lambda cp: cp.start())
    def C(dist,h):
        def fn(o):
            if h==0: xc(o,0,lane(xn)).wait_recv(); fc(o,0,lane(xn)).start()
            else: yc(o,1,lane(yn)).wait_recv(); fc(o,1,lane(yn)).start()
        sides(dist,fn)
    def W(dist,h):
        def fn(o):
            if h==0: yc(o,0,lane(yn)).wait_recv()
            else: xc(o,1,lane(xn)).wait_recv()
            fc(o,h,lane(3-c)).wait_recv()
            cc(o,h,k).start()
        sides(dist,fn)
    def onehot(ids):
        return jnp.where(lax.broadcasted_iota(i32,(ents,KT1),0)==ids,1.0,0.0).astype(bf16)
    nt=cap//KT1
    def src_slot(b):
        def tile(t,_):
            l=pl.ds(pl.multiple_of(t*KT1,KT1),KT1)
            eh[b,:,l]=jnp.dot(tb[...],onehot(src_ref[b:b+1,l]),preferred_element_type=f32).astype(bf16)
            return 0
        lax.fori_loop(0,nt,tile,0)
    def out_copy(b):
        return pltpu.make_async_copy(hb.at[b%2],h_ref.at[pl.ds(b*cap,cap),:],hsem.at[b%2])
    nrel=rt_ref.shape[1]
    def rel_slot(b):
        if b>=2: out_copy(b-2).wait()
        def tile(t,_):
            l=pl.ds(pl.multiple_of(t*KT1,KT1),KT1)
            q=rid_ref[b:b+1,l]
            g=jnp.floor((q.astype(f32)+0.5)*(1.0/nrel)).astype(i32)
            q=q+(RP-nrel)*g
            acc=eh[b,:,l].astype(f32)
            for g0 in range(0,parts):
                oh=jnp.where(lax.broadcasted_iota(i32,(RP,KT1),0)+RP*g0==q,1.0,0.0).astype(bf16)
                acc=acc+jnp.dot(rall[g0],oh,preferred_element_type=f32)
            hid=acc.astype(bf16)
            hf=hid.astype(f32)
            hi,mid,lo=split3(jnp.sum(hf*hf,0,keepdims=True))
            row=lax.broadcasted_iota(i32,(hb.shape[2]-width,KT1),0)
            ex=jnp.where(row==0,hi,jnp.where(row==1,mid,jnp.where(row==2,lo,jnp.where(row<6,1.0,0.0))))
            hb[b%2,pl.ds(pl.multiple_of(t*KT1,KT1),KT1),:]=jnp.concatenate([hf,ex],0).T.astype(bf16)
            return 0
        lax.fori_loop(0,nt,tile,0)
        out_copy(b).start()
    def allrel():
        for o in range(nz): rel_sib(o,1-k).wait_recv()
    src_slot(0)
    src_slot(1)
    Z(0)
    src_slot(2)
    Z(1)
    src_slot(3)
    Z(2)
    src_slot(4)
    C(1,0)
    src_slot(5)
    Z(3)
    src_slot(6)
    Z(4)
    W(1,0)
    src_slot(7)
    C(1,1)
    Z(5)
    allrel()
    rel_slot(0)
    W(1,1)
    Z(6)
    rel_slot(1)
    C(2,0)
    Z(7)
    rel_slot(2)
    W(2,0)
    C(2,1)
    Z(8)
    rel_slot(3)
    W(2,1)
    C(3,0)
    rel_slot(4)
    C(3,1)
    W(3,0)
    rel_slot(5)
    W(3,1)
    rel_slot(6)
    rel_slot(7)
    for n in range(len(SEQ)): along(n,lambda cp: cp.wait_send())
    for h in range(2):
        for o in range(nz): cc(o,h,1-k).wait_recv()
        cc(z,h,k,True).wait_send()
        for dist in range(1,nz):
            def fn(o):
                cc(o,h,k).wait_send()
                xc(o,h,lane(c)).wait_send(); yc(o,h,lane(c)).wait_send()
                fc(o,h,(lane(xn),lane(yn))[h]).wait_send()
            sides(dist,fn)
    for o in range(nz): rel_sib(o,k).wait_send()
    for d in range(1,parts):
        o=lax.rem(e+d,parts)
        neg_copy(o,e).wait_send()
        neg_copy(e,o).wait_recv()
    own_tab.wait(); own_neg.wait()
    out_copy(6).wait(); out_copy(7).wait()

def gather_call(et,rt,src,rid,negs):
    width,ents=et.shape
    parts,cap=src.shape
    D=pltpu.SemaphoreType.DMA
    V=pl.BlockSpec(memory_space=pltpu.VMEM); A=pl.BlockSpec(memory_space=pl.ANY)
    return pl.pallas_call(gather_kernel,name="k1_gather",
        in_specs=[V]*5,out_specs=[A,A,V],
        out_shape=[jax.ShapeDtypeStruct((parts,width,ents),bf16),jax.ShapeDtypeStruct((parts*cap,512),bf16),jax.ShapeDtypeStruct(negs.shape,i32)],
        scratch_shapes=[pltpu.VMEM((width,ents),bf16),pltpu.VMEM((parts,width,RP),bf16),pltpu.VMEM((parts,width,cap),bf16),pltpu.VMEM((2,cap,512),bf16),
            D((2,)),D((2,)),D((3,4)),D((3,4)),D((3,4)),D((4,2)),D((4,2)),D((4,2)),D((4,2)),D((4,2)),D((4,2)),D((4,2)),D((4,2)),D((4,)),D((4,)),D((8,)),D((8,))],
        compiler_params=pltpu.CompilerParams(collective_id=1,has_side_effects=True,vmem_limit_bytes=60<<20))(et,rt,src,rid,negs)


KT = 256
WA=416
SB=32
def block_kernel(width, ents, negcount, CH,
                 counts_ref, h_ref, t_ref, dst_ref, neg_ref, gh_ref, g_ref, loss_ref,
                 ta_ref, tr_ref, acc_ref, crow_ref, s_ref, lane_ref, m_ref):
    j=pl.program_id(0)
    wa=ta_ref.shape[0]
    count=counts_ref[j]
    tiles=lax.div(count+(KT-1),KT)
    t=t_ref[0]
    tf=t.astype(f32)
    norm=(jnp.sum(tf*tf,0,keepdims=True)+1.0)*0.25
    hi,mid,lo=split3(norm)
    ta_ref[0:width,:]=t*bf16(-0.5)
    sub=lax.broadcasted_iota(jnp.int32,(wa-width,ents),0)
    pad=jnp.where(sub<3,0.25,0.0)
    pad=jnp.where(sub==3,hi,pad)
    pad=jnp.where(sub==4,mid,pad)
    pad=jnp.where(sub==5,lo,pad)
    ta_ref[width:,:]=pad.astype(bf16)
    tcat=jnp.concatenate([t, jnp.where(sub==0,1.0,0.0).astype(bf16)],0)
    tr_ref[...]=tcat.T
    ids=neg_ref[0]
    nn=ids.shape[1]
    ohi=jnp.where(lax.broadcasted_iota(jnp.int32,(ents//128,nn),0)==lax.shift_right_arithmetic(ids,7),1.0,0.0).astype(bf16)
    olo=jnp.where(lax.broadcasted_iota(jnp.int32,(128,nn),0)==(ids&127),1.0,0.0).astype(bf16)
    c=lax.dot_general(ohi,olo,(((1,),(1,)),((),())),preferred_element_type=f32)
    for i in range(ents//128):
        crow_ref[0:1,128*i:128*(i+1)]=c[i:i+1,:]
    acc_ref[...]=jnp.zeros_like(acc_ref)
    def dead(kt,_):
        gh_ref[pl.ds(pl.multiple_of(kt*KT,KT),KT),:]=jnp.zeros((KT,gh_ref.shape[1]),bf16)
        return 0
    lax.fori_loop(tiles,gh_ref.shape[0]//KT,dead,0)
    @pl.when(j==0)
    def _(): loss_ref[...]=jnp.zeros_like(loss_ref)
    first=jnp.logical_and(lax.broadcasted_iota(jnp.int32,(8,128),0)==0,lax.broadcasted_iota(jnp.int32,(8,128),1)==0)
    loss_ref[8:16,:]+=jnp.where(first,count.astype(f32),0.0)
    eye=lax.broadcasted_iota(jnp.int32,(KT,KT),0)==lax.broadcasted_iota(jnp.int32,(KT,KT),1)
    lanes=lax.broadcasted_iota(jnp.int32,(SB,CH),1).astype(f32).astype(bf16)
    lane_ref[...]=lax.broadcasted_iota(jnp.int32,lane_ref.shape,1)
    nch=ents//CH
    def rows_of(kt): return pl.ds(pl.multiple_of(kt*KT,KT),KT)
    def live_of(kt): return (lax.broadcasted_iota(jnp.int32,(KT,1),0)+kt*KT)<count
    def idcol(kt):
        idr=dst_ref[pl.ds(j,1),pl.ds(pl.multiple_of(kt*KT,KT),KT)].astype(f32)
        return jnp.sum(jnp.where(eye,idr,0.0),1,keepdims=True).astype(jnp.int32)
    def aug(kt):
        hb=h_ref[rows_of(kt),:]
        last=hb[:,width//128*128:wa].astype(f32)
        lane=lax.broadcasted_iota(jnp.int32,last.shape,1)+width//128*128
        last=jnp.where(jnp.logical_and(lane==width,jnp.logical_not(live_of(kt))),4e6,last)
        return jnp.concatenate([hb[:,:width//128*128],last.astype(bf16)],1)
    def sdot(ha,ci): return jnp.dot(ha,ta_ref[:,ci*CH:(ci+1)*CH],preferred_element_type=f32)
    def post(s,idc,ci,sp):
        es=jnp.where(idc==lane_ref[0:1,ci*CH:(ci+1)*CH],s,0.0)
        for a in range(CH//128): sp=sp+es[:,128*a:128*(a+1)]
        s_ref[:,ci*CH:(ci+1)*CH]=s
        return sp
    def column(sp,kt):
        live=live_of(kt)
        sq=jnp.sum(sp,1,keepdims=True)*4.0
        rr=lax.rsqrt(sq)
        x=sq*rr-margin
        a=jnp.where(live,jax.nn.sigmoid(x)*rr,0.0)
        inva=jnp.where(live,1.0/a,0.0)
        pos=jnp.where(live,jnp.maximum(x,0.0)+jnp.log(1.0+jnp.exp(-jnp.abs(x))),0.0)
        p8=pos[0:8]
        for b in range(1,KT//8): p8+=pos[8*b:8*b+8]
        loss_ref[0:8,:]+=jnp.where(lax.broadcasted_iota(jnp.int32,(8,128),1)==0,p8,0.0)
        return a,inva
    ha=aug(0); idc=idcol(0); sp=jnp.zeros((KT,128),f32)
    for ci in range(nch): sp=post(sdot(ha,ci),idc,ci,sp)
    a0,i0=column(sp,0)
    def tile(kt,carry):
        rho,inva,idc=carry
        nk=jnp.minimum(kt+1,tiles-1)
        hb=h_ref[rows_of(kt),:]
        hf=hb[:,:width].astype(f32)
        hi,mid,lo=split3(rho)
        ex=lax.broadcasted_iota(jnp.int32,(KT,wa-width),1)
        pad=jnp.where(ex==0,hi,jnp.where(ex==1,mid,jnp.where(ex==2,lo,0.0)))
        hat=jnp.concatenate([(hf*rho),pad],1).astype(bf16).T
        ha=aug(nk); nidc=idcol(nk)
        gh=jnp.zeros((KT,wa),f32)
        sp=jnp.zeros((KT,128),f32)
        lsum=jnp.zeros((8,CH),f32)
        rs=[jnp.zeros((SB,128),f32)]*(KT//SB)
        invn=inva*(0.25/negcount)
        pend=None
        for ci in range(nch+1):
            if ci<nch:
                cols=slice(ci*CH,(ci+1)*CH)
                cr=crow_ref[0:1,cols]
                p=None
                for sub in range(KT//SB):
                    at=slice(sub*SB,(sub+1)*SB)
                    s=s_ref[at,cols]
                    r=lax.rsqrt(s)
                    th=jnp.tanh(margin*0.5-s*r)
                    mask=(idc[at]-ci*CH).astype(f32).astype(bf16)==lanes
                    xf=((1.0+th)*cr)*(r*invn[at])
                    for b in range(CH//128): rs[sub]=rs[sub]+xf[:,128*b:128*(b+1)]
                    m_ref[at,cols]=jnp.where(mask,bf16(1.0),bf16(0.0))-xf.astype(bf16)
                    o=1.0-th
                    for b in range(SB//8): p=o[8*b:8*b+8] if p is None else p*o[8*b:8*b+8]
                lsum+=(math.log(2.0)*(KT//8)-jnp.log(p))*cr
                sp=post(sdot(ha,ci),nidc,ci,sp)
            if ci>=1:
                pc=slice((ci-1)*CH,ci*CH)
                gh+=jnp.dot(m_ref[:,pc],tr_ref[pc,:],preferred_element_type=f32)
                acc_ref[:,pc]+=jnp.dot(hat,m_ref[:,pc],preferred_element_type=f32)
        l8=lsum[:,0:128]
        for b in range(1,CH//128): l8+=lsum[:,128*b:128*(b+1)]
        loss_ref[0:8,:]+=l8*(1.0/negcount)
        out=(hf*(1.0-jnp.sum(jnp.concatenate(rs,0),1,keepdims=True))-gh[:,:width])*rho
        gh_ref[rows_of(kt),:width]=out.astype(bf16)
        live=kt+1<tiles
        na,ni=column(jnp.where(live,sp,1.0),jnp.where(live,nk,tiles))
        return na,ni,nidc
    lax.fori_loop(0,tiles,tile,(a0,i0,idc))
    g_ref[0]=tf*acc_ref[width:width+1,:]+tf*acc_ref[width+1:width+2,:]+tf*acc_ref[width+2:width+3,:]-acc_ref[0:width,:]

def run_blocks(h,tables,dst,neg,counts,negcount,CH=256):
    parts,width,ents=tables.shape
    cap=h.shape[0]//parts
    wa=WA
    nn=neg.shape[-1]
    gs=pltpu.PrefetchScalarGridSpec(num_scalar_prefetch=1,grid=(parts,),
      in_specs=[pl.BlockSpec((cap,h.shape[1]),lambda j,c:(j,0)),
                pl.BlockSpec((1,width,ents),lambda j,c:(j,0,0)),
                pl.BlockSpec((parts,cap),lambda j,c:(0,0)),
                pl.BlockSpec((1,1,nn),lambda j,c:(j,0,0))],
      out_specs=[pl.BlockSpec((cap,width),lambda j,c:(j,0)),
                 pl.BlockSpec((1,width,ents),lambda j,c:(j,0,0)),
                 pl.BlockSpec((16,128),lambda j,c:(0,0))],
      scratch_shapes=[pltpu.VMEM((wa,ents),bf16),pltpu.VMEM((ents,wa),bf16),
                      pltpu.VMEM((wa,ents),f32),pltpu.VMEM((8,ents),f32),pltpu.VMEM((KT,ents),f32),pltpu.VMEM((8,ents),jnp.int32),pltpu.VMEM((KT,ents),bf16)])
    return pl.pallas_call(functools.partial(block_kernel,width,ents,negcount,CH),grid_spec=gs,name="k2_blocks",
      out_shape=[jax.ShapeDtypeStruct((h.shape[0],width),bf16),jax.ShapeDtypeStruct(tables.shape,f32),jax.ShapeDtypeStruct((16,128),f32)],
      compiler_params=pltpu.CompilerParams(vmem_limit_bytes=60<<20,dimension_semantics=("arbitrary",)))(counts,h,tables,dst,neg)


HALF=208

def reduce_kernel(g_ref, gh_ref, src_ref, rid_ref, sc_ref,
                  ge_ref, gr_ref, sco_ref,
                  pr, own, sacc, racc, sa0, sa1, ra0, ra1, sb0, sb1, rb0, rb1, sz, rz, ghb, rp, rsz, rzr, scb,
                  ps, prr, osem, gsem, sas, sar, sbs, sbr, zs, zr, rps, rpr, rzs, rzrr, gxs, gxr, gys, gyr, gds, gdr, css, csr, czs, czr):
    parts,width,ents=g_ref.shape
    nz=4; CK=ents//4; last=nz-1
    cap=src_ref.shape[1]
    nrel=gr_ref.shape[0]
    c,z,k,xn,yn=place()
    e=2*z+k; sib=2*z+1-k
    x=lax.rem(c,2); y=lax.div(c,2); xo=1-x; yo=1-y
    bar=pltpu.get_barrier_semaphore()
    for to in ((c,sib),(xn,e),(yn,e))+tuple((c,lax.rem(e+2*d,parts)) for d in range(1,nz)):
        pl.semaphore_signal(bar,inc=1,device_id=to,device_id_type=MESH)
    order=[lax.rem(z+1+i,nz) for i in range(nz)]
    rows_of=(pl.ds(0,HALF),pl.ds(HALF,width-HALF))
    lo=(0,HALF); num=(HALF,width-HALF)
    def load(i): return pltpu.make_async_copy(g_ref.at[2*order[i]+k],own.at[i%2],osem.at[i%2])
    def gload(b): return pltpu.make_async_copy(gh_ref.at[pl.ds(b*cap,cap),:],ghb.at[b%2],gsem.at[b%2])
    gload(0).start(); load(0).start(); load(1).start()
    pl.semaphore_wait(bar,nz+2)
    def rc(src,dst,s,r,to):
        return pltpu.make_async_remote_copy(src_ref=src,dst_ref=dst,send_sem=s,recv_sem=r,device_id=to,device_id_type=MESH)
    def pair(i,h): return rc(g_ref.at[2*order[i]+1-k,rows_of[h],:],pr.at[i,rows_of[h],:],ps.at[i,h],prr.at[i,h],(c,sib))
    for i in range(2):
        for h in range(2): pair(i,h).start()
    def lane(ck,n=1): return pl.ds(pl.multiple_of(ck*CK,CK),n*CK)
    near=((xn,e),(yn,e)); sa=(sa0,sa1); ra=(ra0,ra1); sb=(sb0,sb1); rb=(rb0,rb1)
    def ac(i,h): return rc(sa[h].at[i],ra[h].at[i],sas.at[i,h],sar.at[i,h],near[h])
    def bc(i,h): return rc(sb[h].at[i],rb[h].at[i],sbs.at[i,h],sbr.at[i,h],near[1-h])
    def zc(i,h): return rc(sz.at[i,rows_of[h],:],rz.at[i,rows_of[h],:],zs.at[i,h],zr.at[i,h],(c,2*order[i]+k))
    gone=((xo,xo+2),(2*yo,2*yo+1))
    kept=((x,x+2),(2*y,2*y+1))
    passed=(x+2*yo,2*y+xo)
    mine=(y,x)
    RB=16
    def strips(h,fn):
        fn(rows_of[h],pl.ds(0,num[h]))
    def st0(i,h):
        if h==0 and i!=last: load(i).wait()
        pair(i,h).wait_recv()
        def one(rows,rel):
            for s in range(2):
                l=lane(gone[h][s])
                sa[h][i,rel,s*CK:(s+1)*CK]=(pr[i,rows,l]+own[i%2,rows,l]).astype(bf16)
                l=lane(kept[h][s])
                pr[i,rows,l]=pr[i,rows,l]+own[i%2,rows,l]
        strips(h,one)
        ac(i,h).start()
        if h==1 and i+2<nz:
            load(i+2).start()
            for g in range(2): pair(i+2,g).start()
    def stB(i,h):
        ac(i,h).wait_recv()
        def one(rows,rel):
            sb[h][i,rel,:]=(pr[i,rows,lane(passed[h])]+ra[h][i,rel,lane(1-mine[h])].astype(f32)).astype(sb0.dtype)
            pr[i,rows,lane(c)]=pr[i,rows,lane(c)]+ra[h][i,rel,lane(mine[h])].astype(f32)
        strips(h,one)
        bc(i,h).start()
    def stZ(i,h):
        bc(i,h).wait_recv()
        def one(rows,rel):
            v=pr[i,rows,lane(c)]+rb[h][i,rel,:].astype(f32)
            if i==last: ge_ref[rows,lane(c)]=v
            else: sz[i,rows,:]=v.astype(sz.dtype)
        strips(h,one)
        if i!=last: zc(i,h).start()
    def both(fn,i):
        fn(i,0); fn(i,1)
    def getblock(b):
        gload(b).wait()
        gload((b+1)%parts).start()
    def slot(ids_ref,acc,b,RC):
        ids=ids_ref[b:b+1,:]
        def chunk(t,_):
            rows=pl.ds(pl.multiple_of(t*RC,8),RC)
            oh=jnp.where(lax.broadcasted_iota(i32,(RC,cap),0)==ids-t*RC,1.0,0.0).astype(bf16)
            d=jnp.dot(oh,ghb[b%2],preferred_element_type=f32)
            if b==0: acc[rows,:]=d
            else: acc[rows,:]=acc[rows,:]+d
            return 0
        lax.fori_loop(0,acc.shape[0]//RC,chunk,0)
    def src(b):
        getblock(b); slot(src_ref,sacc,b,CK)
    def rel(b):
        getblock(b); slot(rid_ref,racc,b,2*nrel)
    def addsrc():
        def it(t,_):
            l=pl.ds(pl.multiple_of(t*128,128),128)
            own[last%2,:,l]=own[last%2,:,l]+sacc[l,:].T
            return 0
        lax.fori_loop(0,ents//128,it,0)
    def grp(g): return pl.ds(pl.multiple_of(g*nrel,8),nrel)
    def relpair(i): return rc(racc.at[grp(2*order[i]+1-k),:],rp.at[i],rps.at[i],rpr.at[i],(c,sib))
    def relz(i): return rc(rsz.at[i],rzr.at[i],rzs.at[i],rzrr.at[i],(c,2*order[i]+k))
    src(0)
    src(1)
    both(st0,0)
    src(2)
    src(3)
    both(st0,1)
    src(4)
    both(stB,0)
    src(5)
    src(6)
    both(st0,2)
    src(7)
    load(last).wait()
    addsrc()
    both(stB,1)
    both(stZ,0)
    rel(0)
    rel(1)
    both(st0,3)
    rel(2)
    both(stB,2)
    both(stZ,1)
    rel(3)
    rel(4)
    rel(5)
    both(stB,3)
    rel(6)
    both(stZ,2)
    rel(7)
    for i in range(nz): relpair(i).start()
    for i in range(last):
        relpair(i).wait_recv()
        rsz[i]=(racc[grp(2*order[i]+k),:]+rp[i]).astype(rsz.dtype)
        relz(i).start()
    both(stZ,3)
    gload(0).wait()
    sq=jnp.zeros((RB,CK),f32)
    def gx(h,l): return rc(ge_ref.at[rows_of[h],l],ge_ref.at[rows_of[h],l],gxs.at[h],gxr.at[h],(xn,e))
    def gy(h,l): return rc(ge_ref.at[rows_of[h],l],ge_ref.at[rows_of[h],l],gys.at[h],gyr.at[h],(yn,e))
    def gd(h,l): return rc(ge_ref.at[rows_of[h],l],ge_ref.at[rows_of[h],l],gds.at[h],gdr.at[h],near[1-h])
    for h in range(2):
        for i in range(last): zc(i,h).wait_recv()
        rows=rows_of[h]
        v=ge_ref[rows,lane(c)]
        for i in range(last): v=v+rz[i,rows,:].astype(f32)
        ge_ref[rows,lane(c)]=v
        v=v*v
        for b in range(0,num[h],RB): sq=sq+v[b:b+RB]
        if h==0: gx(0,lane(c)).start()
        else: gy(1,lane(c)).start()
    gy(0,lane(c)).start(); gx(1,lane(c)).start()
    relpair(last).wait_recv()
    rv=racc[grp(e),:]+rp[last]
    for i in range(last):
        relz(i).wait_recv()
        rv=rv+rzr[i].astype(f32)
    gr_ref[...]=rv
    one=jnp.sum(sq)+3.0*jnp.sum(rv*rv)
    row=lax.broadcasted_iota(i32,(8,128),0)
    v=jnp.where(row==0,one,jnp.where(row==1,jnp.sum(sc_ref[0:8,:]),jnp.where(row==2,jnp.sum(sc_ref[8:16,:]),0.0)))
    def swap(s,v,to):
        scb[s]=v
        cp=rc(scb.at[s],scb.at[3+s],css.at[s],csr.at[s],to)
        cp.start(); cp.wait()
        return v+scb[3+s]
    v=swap(0,v,(c,sib))
    scb[6+z]=v
    def cz(d): return rc(scb.at[6+z],scb.at[6+z],czs.at[d],czr.at[d],(c,lax.rem(e+2*d,parts)))
    for d in range(1,nz): cz(d).start()
    gx(0,lane(xn)).wait_recv(); gd(0,lane(xn)).start()
    gy(1,lane(yn)).wait_recv(); gd(1,lane(yn)).start()
    for d in range(1,nz): cz(d).wait()
    v=(scb[6]+scb[7])+(scb[8]+scb[9])
    v=swap(1,v,(xn,e))
    v=swap(2,v,(yn,e))
    live=v[2:3,:]
    norm=jnp.sqrt(v[0:1,:])/live
    clip=0.01/math.sqrt(4*parts*parts*cap)
    scale=jnp.minimum(1.0,clip/norm)/live
    sco_ref[...]=jnp.where(row==0,norm,jnp.where(row==3,scale,v))
    gx(1,lane(xn)).wait_recv(); gy(0,lane(yn)).wait_recv()
    gd(0,lane(3-c)).wait_recv(); gd(1,lane(3-c)).wait_recv()
    for h in range(2):
        gx(h,lane(c)).wait_send(); gy(h,lane(c)).wait_send()
        for i in range(nz):
            pair(i,h).wait_send(); ac(i,h).wait_send(); bc(i,h).wait_send()
            if i<last: zc(i,h).wait_send()
    gd(0,lane(xn)).wait_send(); gd(1,lane(yn)).wait_send()
    for i in range(nz):
        relpair(i).wait_send()
        if i<last: relz(i).wait_send()

def reduce_call(g,gh,src,rid,sc,nrel,BT=bf16,ZT=bf16,RT=bf16):
    parts,width,ents=g.shape
    cap=src.shape[1]; nz=4; CK=ents//4
    D=pltpu.SemaphoreType.DMA
    V=pl.BlockSpec(memory_space=pltpu.VMEM); A=pl.BlockSpec(memory_space=pl.ANY)
    VM=pltpu.VMEM
    rest=width-HALF
    return pl.pallas_call(reduce_kernel,name="k3_reduce",
        in_specs=[A,A,V,V,V],out_specs=[V,V,V],
        out_shape=[jax.ShapeDtypeStruct((width,ents),f32),jax.ShapeDtypeStruct((nrel,width),f32),jax.ShapeDtypeStruct((8,128),f32)],
        scratch_shapes=[VM((nz,width,ents),f32),VM((2,width,ents),f32),VM((ents,width),f32),VM((parts*nrel,width),f32),
            VM((nz,HALF,2*CK),bf16),VM((nz,rest,2*CK),bf16),VM((nz,HALF,2*CK),bf16),VM((nz,rest,2*CK),bf16),
            VM((nz,HALF,CK),BT),VM((nz,rest,CK),BT),VM((nz,HALF,CK),BT),VM((nz,rest,CK),BT),
            VM((nz-1,width,CK),ZT),VM((nz-1,width,CK),ZT),
            VM((2,cap,width),bf16),VM((nz,nrel,width),f32),VM((nz-1,nrel,width),RT),VM((nz-1,nrel,width),RT),VM((10,8,128),f32),
            D((4,2)),D((4,2)),D((2,)),D((2,)),D((4,2)),D((4,2)),D((4,2)),D((4,2)),D((3,2)),D((3,2)),D((4,)),D((4,)),D((3,)),D((3,)),
            D((2,)),D((2,)),D((2,)),D((2,)),D((2,)),D((2,)),D((3,)),D((3,)),D((4,)),D((4,))],
        compiler_params=pltpu.CompilerParams(collective_id=2,has_side_effects=True,vmem_limit_bytes=62<<20))(g,gh,src,rid,sc)


def cube_body(
    ent_table,
    entity_first_moment,
    ent_v,
    rel_table,
    relation_first_moment,
    rel_v,
    src_ids,
    rel_ids,
    dst_ids,
    neg_ids,
    bucket_counts,
):
    parts = src_ids.shape[2]
    negcount = neg_ids.shape[3]
    nrel = rel_table.shape[1]
    padded = -(-negcount // 1024) * 1024
    negs = jnp.pad(neg_ids[0, 0], ((0, 0), (0, padded - negcount)), constant_values=-1)
    tables, hidden, arrived = gather_call(
        ent_table.T, rel_table, src_ids[0, 0], rel_ids[0, 0], negs.reshape(parts, -1, 128)
    )
    back, partial, sums = run_blocks(
        hidden,
        tables,
        dst_ids[0, 0],
        arrived.reshape(parts, 1, padded),
        bucket_counts[0, 0],
        negcount,
    )
    ent_grad, rel_grad, totals = reduce_call(
        partial, back, src_ids[0, 0], rel_ids[0, 0], sums, nrel
    )
    grad_norm, loss_sum, total, scale = totals[0, 0], totals[1, 0], totals[2, 0], totals[3, 0]
    new_ent, new_ent_m, new_ent_v = adamw(ent_table, entity_first_moment, ent_v, scale * ent_grad.T)
    new_rel, new_rel_m, new_rel_v = adamw(
        rel_table, relation_first_moment, rel_v, scale * rel_grad[None]
    )
    return (
        loss_sum,
        total,
        grad_norm,
        new_ent,
        new_ent_m,
        new_ent_v,
        new_ent.astype(jnp.bfloat16),
        new_rel,
        new_rel_m,
        new_rel_v,
        new_rel.astype(jnp.bfloat16),
    )


def solution(mesh):
    body = cube_body if mesh.shape["rel"] == 4 and mesh.shape["ent"] == 8 else general_body
    return jax.shard_map(
        body,
        mesh=mesh,
        in_specs=(
            P("ent", None),
            P("ent", None),
            P("ent", None),
            P(None, ("rel", "ent"), None),
            P(None, ("rel", "ent"), None),
            P(None, ("rel", "ent"), None),
            P("rel", "ent", None, None),
            P("rel", "ent", None, None),
            P("rel", "ent", None, None),
            P("rel", "ent", None, None),
            P("rel", "ent", None),
        ),
        out_specs=(
            P(),
            P(),
            P(),
            P("ent", None),
            P("ent", None),
            P("ent", None),
            P("ent", None),
            P(None, ("rel", "ent"), None),
            P(None, ("rel", "ent"), None),
            P(None, ("rel", "ent"), None),
            P(None, ("rel", "ent"), None),
        ),
        check_vma=False,
    )
```

```python
import functools
import math

import jax
import jax.numpy as jnp
from jax import lax
from jax.experimental import pallas as pl
from jax.experimental.pallas import tpu as pltpu
from jax.sharding import PartitionSpec as P

STEP = 10
f32 = jnp.float32
bf16 = jnp.bfloat16
i32 = jnp.int32
MESH = pl.DeviceIdType.MESH


margin = 2.5
beta_one = 0.9
beta_two = 0.999
learn_rate = 0.05
decay_rate = 0.01
epsilon = 1e-16


def shortened(array):
    return jax.tree.map(lambda a: a.astype(jnp.bfloat16) if a.dtype == jnp.float32 else a, array)


def adamw(weight, moment, second, grad):
    moment = beta_one * moment + (1.0 - beta_one) * grad
    second = beta_two * second + (1.0 - beta_two) * grad * grad
    m_hat = moment / (1.0 - beta_one**STEP)
    v_hat = second / (1.0 - beta_two**STEP)
    weight = weight - learn_rate * (m_hat / (jnp.sqrt(v_hat) + epsilon) + decay_rate * weight)
    return (weight, moment, second)


def general_body(
    ent_table,
    entity_first_moment,
    ent_v,
    rel_table,
    relation_first_moment,
    rel_v,
    src_ids,
    rel_ids,
    dst_ids,
    neg_ids,
    bucket_counts,
):
    parts = src_ids.shape[2]
    slots = src_ids.shape[3]
    width = ent_table.shape[1]
    negcount = neg_ids.shape[3]
    clip_level = 0.01 / math.sqrt(lax.axis_size("rel") * lax.axis_size("ent") * parts * slots)
    ent_low = ent_table.astype(jnp.bfloat16)
    layers = lax.all_gather(rel_table.astype(jnp.bfloat16), "ent", axis=1, tiled=True)
    rel_sum = (
        layers[0].astype(jnp.float32)
        + layers[1].astype(jnp.float32)
        + layers[2].astype(jnp.float32)
    )
    sources = src_ids[0, 0]
    relation = rel_ids[0, 0]
    counts = bucket_counts[0, 0]
    hidden = ent_low[sources].astype(jnp.float32) + rel_sum[relation]
    total = lax.psum(jnp.sum(counts).astype(jnp.float32), ("rel", "ent"))
    arrived, dst_in, count_in = (
        lax.all_to_all(hidden.astype(jnp.bfloat16), "ent", split_axis=0, concat_axis=0, tiled=True),
        lax.all_to_all(dst_ids[0, 0], "ent", split_axis=0, concat_axis=0, tiled=True),
        lax.all_to_all(counts[:, None], "ent", split_axis=0, concat_axis=0, tiled=True),
    )
    live = (jnp.arange(slots, dtype=jnp.int32)[None, :] < count_in).astype(jnp.float32)
    negatives = neg_ids[0, 0]

    def block(args):
        hid, dst, neg, alive = args
        weight = alive / total
        hid_f = hid.astype(jnp.float32)
        diff = hid_f - ent_low[dst].astype(jnp.float32)
        pos_dist = jnp.sqrt(jnp.sum(diff * diff, -1) + 1.0)
        rows = ent_low[neg]
        rows_f = rows.astype(jnp.float32)
        prod = lax.dot_general(
            hid, rows, (((1,), (1,)), ((), ())), preferred_element_type=jnp.float32
        )
        sq = (
            jnp.sum(hid_f * hid_f, -1)[:, None] + jnp.sum(rows_f * rows_f, -1)[None, :] - 2.0 * prod
        )
        neg_dist = jnp.sqrt(sq + 1.0)
        per_edge = jax.nn.softplus(pos_dist - margin) + jnp.mean(
            jax.nn.softplus(margin - neg_dist), -1
        )
        loss = jnp.sum(alive * per_edge)
        g_pos = weight * jax.nn.sigmoid(pos_dist - margin)
        g_diff = (g_pos / pos_dist)[:, None] * diff
        g_sq = -(weight[:, None] / negcount) * jax.nn.sigmoid(margin - neg_dist) / (2.0 * neg_dist)
        g_prod = (-2.0 * g_sq).astype(jnp.bfloat16)
        g_hid = (
            g_diff
            + 2.0 * hid_f * jnp.sum(g_sq, 1)[:, None]
            + jnp.dot(g_prod, rows, preferred_element_type=jnp.float32)
        )
        g_rows = 2.0 * rows_f * jnp.sum(g_sq, 0)[:, None] + lax.dot_general(
            g_prod, hid, (((0,), (0,)), ((), ())), preferred_element_type=jnp.float32
        )
        return (loss, g_hid.astype(jnp.bfloat16), -g_diff, g_rows)

    losses, back, g_target, g_negative = lax.map(
        block, (arrived, dst_in, negatives, live), batch_size=min(4, parts)
    )
    returned = (
        jax.tree.map(
            lambda part, own: part.astype(own.dtype),
            lax.all_to_all(shortened(back), "ent", split_axis=0, concat_axis=0, tiled=True),
            back,
        )
        .reshape(-1, width)
        .astype(jnp.float32)
    )
    ent_grad = jnp.zeros(ent_table.shape, jnp.float32)
    ent_grad = ent_grad.at[dst_in.reshape(-1)].add(g_target.reshape(-1, width))
    ent_grad = ent_grad.at[negatives.reshape(-1)].add(g_negative.reshape(-1, width))
    ent_grad = ent_grad.at[sources.reshape(-1)].add(returned)
    ent_grad = lax.psum(ent_grad, "rel")
    rel_local = jnp.zeros(rel_sum.shape, jnp.float32).at[relation.reshape(-1)].add(returned)
    rel_grad = lax.psum_scatter(rel_local, "ent", scatter_dimension=0, tiled=True)
    own_squares = jnp.where(
        lax.axis_index("rel") == 0, jnp.sum(ent_grad * ent_grad), 0.0
    ) + 3.0 * jnp.sum(rel_grad * rel_grad)
    squares, loss_sum = lax.psum((own_squares, jnp.sum(losses)), ("rel", "ent"))
    grad_norm = jnp.sqrt(squares)
    scale = jnp.minimum(1.0, clip_level / grad_norm)
    new_ent, new_ent_m, new_ent_v = adamw(ent_table, entity_first_moment, ent_v, scale * ent_grad)
    new_rel, new_rel_m, new_rel_v = adamw(
        rel_table, relation_first_moment, rel_v, scale * rel_grad[None]
    )
    return (
        loss_sum,
        total,
        grad_norm,
        new_ent,
        new_ent_m,
        new_ent_v,
        new_ent.astype(jnp.bfloat16),
        new_rel,
        new_rel_m,
        new_rel_v,
        new_rel.astype(jnp.bfloat16),
    )


KT1=256
RP=256

def split3(x):
    hi=x.astype(bf16).astype(f32); r=x-hi
    mid=r.astype(bf16).astype(f32); lo=r-mid
    return hi,mid,lo

def place():
    r=lax.axis_index("rel"); e=lax.axis_index("ent")
    z=lax.div(e,2); k=lax.rem(e,2)
    xn=r+1-2*lax.rem(r,2)
    yn=lax.rem(r+2,4)
    return r,z,k,xn,yn

def gather_kernel(et_ref, rt_ref, src_ref, rid_ref, neg_ref,
                  tab_ref, h_ref, negout_ref,
                  tb, rall, eh, hb, lsem, hsem, us, ds, zr, xs, xr, ys, yr, fs, fr, cs, cr, rcs, rcr, ns, nr):
    width,ents=et_ref.shape
    nz=4; parts=8
    CK=ents//4
    cap=src_ref.shape[1]
    c,z,k,xn,yn=place()
    e=2*z+k
    half=208
    sib=2*z+1-k
    bar=pltpu.get_barrier_semaphore()
    for d in range(1,parts):
        pl.semaphore_signal(bar,inc=1,device_id=(c,lax.rem(e+d,parts)),device_id_type=MESH)
    pl.semaphore_signal(bar,inc=1,device_id=(xn,e),device_id_type=MESH)
    pl.semaphore_signal(bar,inc=1,device_id=(yn,e),device_id_type=MESH)
    tb[...]=et_ref[...].astype(bf16)
    low=[rt_ref[l].astype(bf16).astype(f32) for l in range(3)]
    rsum=jnp.concatenate([low[0]+low[1]+low[2],jnp.zeros((RP-rt_ref.shape[1],width),f32)],0)
    rall[e]=rsum.T.astype(bf16)
    pl.semaphore_wait(bar,parts+1)
    def rc(src,dst,s,r,to):
        return pltpu.make_async_remote_copy(src_ref=src,dst_ref=dst,send_sem=s,recv_sem=r,device_id=to,device_id_type=MESH)
    rows_of=(pl.ds(0,half),pl.ds(half,width-half))
    def lane(ck): return pl.ds(pl.multiple_of(ck*CK,CK),CK)
    SEQ=((2,1),(0,1),(2,2),(1,1),(2,3),(0,2),(1,2),(0,3),(1,3))
    def part(o,u,own=False):
        if u==2: return rall.at[2*o+k]
        return tb.at[rows_of[u],lane(c)] if own else tab_ref.at[2*o+k,rows_of[u],lane(c)]
    def up(o,u,own): return rc(part(o,u,own),part(o,u),us.at[u,o],zr.at[u,o],(c,2*(z+1)+k))
    def down(o,u,own): return rc(part(o,u,own),part(o,u),ds.at[u,o],zr.at[u,o],(c,2*(z-1)+k))
    def sides(dist,fn):
        @pl.when(z>=dist)
        def _(): fn(z-dist)
        @pl.when(z+dist<nz)
        def _(): fn(z+dist)
    def along(n,act):
        u,dist=SEQ[n]
        f=dist-1
        @pl.when(jnp.logical_and(z<nz-1,z>=f))
        def _(): act(up(z-f,u,f==0))
        @pl.when(jnp.logical_and(z>0,z+f<nz))
        def _(): act(down(z+f,u,f==0))
    def xc(o,h,l): return rc(tab_ref.at[2*o+k,rows_of[h],l],tab_ref.at[2*o+k,rows_of[h],l],xs.at[o,h],xr.at[o,h],(xn,e))
    def yc(o,h,l): return rc(tab_ref.at[2*o+k,rows_of[h],l],tab_ref.at[2*o+k,rows_of[h],l],ys.at[o,h],yr.at[o,h],(yn,e))
    def fc(o,h,l):
        v=tab_ref.at[2*o+k,rows_of[h],l]
        return rc(v,v,fs.at[o,h],fr.at[o,h],((yn,e),(xn,e))[h])
    def cc(o,h,kk,own=False):
        v=tab_ref.at[2*o+kk,rows_of[h],:]
        return rc(tb.at[rows_of[h],:] if own else v,v,cs.at[o,h],cr.at[o,h],(c,sib))
    def rel_sib(o,kk):
        return rc(rall.at[2*o+kk],rall.at[2*o+kk],rcs.at[o],rcr.at[o],(c,sib))
    along(0,lambda cp: cp.start())
    along(1,lambda cp: cp.start())
    rel_sib(z,k).start()
    def neg_copy(to,own):
        return rc(neg_ref.at[to],negout_ref.at[own],ns.at[to],nr.at[own],(c,to))
    for d in range(1,parts):
        neg_copy(lax.rem(e+d,parts),e).start()
    own_neg=pltpu.make_async_copy(neg_ref.at[e],negout_ref.at[e],lsem.at[1])
    own_neg.start()
    own_tab=pltpu.make_async_copy(tb,tab_ref.at[e],lsem.at[0])
    own_tab.start()
    for h in range(2): cc(z,h,k,True).start()
    def Z(n):
        u,dist=SEQ[n]
        def fn(o):
            up(o,u,False).wait_recv()
            if u==2: rel_sib(o,k).start()
            else:
                xc(o,u,lane(c)).start(); yc(o,u,lane(c)).start()
        sides(dist,fn)
        if n+2<len(SEQ): along(n+2,lambda cp: cp.start())
    def C(dist,h):
        def fn(o):
            if h==0: xc(o,0,lane(xn)).wait_recv(); fc(o,0,lane(xn)).start()
            else: yc(o,1,lane(yn)).wait_recv(); fc(o,1,lane(yn)).start()
        sides(dist,fn)
    def W(dist,h):
        def fn(o):
            if h==0: yc(o,0,lane(yn)).wait_recv()
            else: xc(o,1,lane(xn)).wait_recv()
            fc(o,h,lane(3-c)).wait_recv()
            cc(o,h,k).start()
        sides(dist,fn)
    def onehot(ids):
        return jnp.where(lax.broadcasted_iota(i32,(ents,KT1),0)==ids,1.0,0.0).astype(bf16)
    nt=cap//KT1
    def src_slot(b):
        def tile(t,_):
            l=pl.ds(pl.multiple_of(t*KT1,KT1),KT1)
            eh[b,:,l]=jnp.dot(tb[...],onehot(src_ref[b:b+1,l]),preferred_element_type=f32).astype(bf16)
            return 0
        lax.fori_loop(0,nt,tile,0)
    def out_copy(b):
        return pltpu.make_async_copy(hb.at[b%2],h_ref.at[pl.ds(b*cap,cap),:],hsem.at[b%2])
    nrel=rt_ref.shape[1]
    def rel_slot(b):
        if b>=2: out_copy(b-2).wait()
        def tile(t,_):
            l=pl.ds(pl.multiple_of(t*KT1,KT1),KT1)
            q=rid_ref[b:b+1,l]
            g=jnp.floor((q.astype(f32)+0.5)*(1.0/nrel)).astype(i32)
            q=q+(RP-nrel)*g
            acc=eh[b,:,l].astype(f32)
            for g0 in range(0,parts):
                oh=jnp.where(lax.broadcasted_iota(i32,(RP,KT1),0)+RP*g0==q,1.0,0.0).astype(bf16)
                acc=acc+jnp.dot(rall[g0],oh,preferred_element_type=f32)
            hid=acc.astype(bf16)
            hf=hid.astype(f32)
            hi,mid,lo=split3(jnp.sum(hf*hf,0,keepdims=True))
            row=lax.broadcasted_iota(i32,(hb.shape[2]-width,KT1),0)
            ex=jnp.where(row==0,hi,jnp.where(row==1,mid,jnp.where(row==2,lo,jnp.where(row<6,1.0,0.0))))
            hb[b%2,pl.ds(pl.multiple_of(t*KT1,KT1),KT1),:]=jnp.concatenate([hf,ex],0).T.astype(bf16)
            return 0
        lax.fori_loop(0,nt,tile,0)
        out_copy(b).start()
    def allrel():
        for o in range(nz): rel_sib(o,1-k).wait_recv()
    src_slot(0)
    src_slot(1)
    Z(0)
    src_slot(2)
    Z(1)
    src_slot(3)
    Z(2)
    src_slot(4)
    C(1,0)
    src_slot(5)
    Z(3)
    src_slot(6)
    Z(4)
    W(1,0)
    src_slot(7)
    C(1,1)
    Z(5)
    allrel()
    rel_slot(0)
    W(1,1)
    Z(6)
    rel_slot(1)
    C(2,0)
    Z(7)
    rel_slot(2)
    W(2,0)
    C(2,1)
    Z(8)
    rel_slot(3)
    W(2,1)
    C(3,0)
    rel_slot(4)
    C(3,1)
    W(3,0)
    rel_slot(5)
    W(3,1)
    rel_slot(6)
    rel_slot(7)
    for n in range(len(SEQ)): along(n,lambda cp: cp.wait_send())
    for h in range(2):
        for o in range(nz): cc(o,h,1-k).wait_recv()
        cc(z,h,k,True).wait_send()
        for dist in range(1,nz):
            def fn(o):
                cc(o,h,k).wait_send()
                xc(o,h,lane(c)).wait_send(); yc(o,h,lane(c)).wait_send()
                fc(o,h,(lane(xn),lane(yn))[h]).wait_send()
            sides(dist,fn)
    for o in range(nz): rel_sib(o,k).wait_send()
    for d in range(1,parts):
        o=lax.rem(e+d,parts)
        neg_copy(o,e).wait_send()
        neg_copy(e,o).wait_recv()
    own_tab.wait(); own_neg.wait()
    out_copy(6).wait(); out_copy(7).wait()

def gather_call(et,rt,src,rid,negs):
    width,ents=et.shape
    parts,cap=src.shape
    D=pltpu.SemaphoreType.DMA
    V=pl.BlockSpec(memory_space=pltpu.VMEM); A=pl.BlockSpec(memory_space=pl.ANY)
    return pl.pallas_call(gather_kernel,name="k1_gather",
        in_specs=[V]*5,out_specs=[A,A,V],
        out_shape=[jax.ShapeDtypeStruct((parts,width,ents),bf16),jax.ShapeDtypeStruct((parts*cap,512),bf16),jax.ShapeDtypeStruct(negs.shape,i32)],
        scratch_shapes=[pltpu.VMEM((width,ents),bf16),pltpu.VMEM((parts,width,RP),bf16),pltpu.VMEM((parts,width,cap),bf16),pltpu.VMEM((2,cap,512),bf16),
            D((2,)),D((2,)),D((3,4)),D((3,4)),D((3,4)),D((4,2)),D((4,2)),D((4,2)),D((4,2)),D((4,2)),D((4,2)),D((4,2)),D((4,2)),D((4,)),D((4,)),D((8,)),D((8,))],
        compiler_params=pltpu.CompilerParams(collective_id=1,has_side_effects=True,vmem_limit_bytes=60<<20))(et,rt,src,rid,negs)


KT = 256
WA=416
SB=32
def block_kernel(width, ents, negcount, CH,
                 counts_ref, h_ref, t_ref, dst_ref, neg_ref, gh_ref, g_ref, loss_ref,
                 ta_ref, tr_ref, acc_ref, crow_ref, s_ref, lane_ref, m_ref):
    j=pl.program_id(0)
    wa=ta_ref.shape[0]
    count=counts_ref[j]
    tiles=lax.div(count+(KT-1),KT)
    t=t_ref[0]
    tf=t.astype(f32)
    norm=(jnp.sum(tf*tf,0,keepdims=True)+1.0)*0.25
    hi,mid,lo=split3(norm)
    ta_ref[0:width,:]=t*bf16(-0.5)
    sub=lax.broadcasted_iota(jnp.int32,(wa-width,ents),0)
    pad=jnp.where(sub<3,0.25,0.0)
    pad=jnp.where(sub==3,hi,pad)
    pad=jnp.where(sub==4,mid,pad)
    pad=jnp.where(sub==5,lo,pad)
    ta_ref[width:,:]=pad.astype(bf16)
    tcat=jnp.concatenate([t, jnp.where(sub==0,1.0,0.0).astype(bf16)],0)
    tr_ref[...]=tcat.T
    ids=neg_ref[0]
    nn=ids.shape[1]
    ohi=jnp.where(lax.broadcasted_iota(jnp.int32,(ents//128,nn),0)==lax.shift_right_arithmetic(ids,7),1.0,0.0).astype(bf16)
    olo=jnp.where(lax.broadcasted_iota(jnp.int32,(128,nn),0)==(ids&127),1.0,0.0).astype(bf16)
    c=lax.dot_general(ohi,olo,(((1,),(1,)),((),())),preferred_element_type=f32)
    for i in range(ents//128):
        crow_ref[0:1,128*i:128*(i+1)]=c[i:i+1,:]
    acc_ref[...]=jnp.zeros_like(acc_ref)
    def dead(kt,_):
        gh_ref[pl.ds(pl.multiple_of(kt*KT,KT),KT),:]=jnp.zeros((KT,gh_ref.shape[1]),bf16)
        return 0
    lax.fori_loop(tiles,gh_ref.shape[0]//KT,dead,0)
    @pl.when(j==0)
    def _(): loss_ref[...]=jnp.zeros_like(loss_ref)
    first=jnp.logical_and(lax.broadcasted_iota(jnp.int32,(8,128),0)==0,lax.broadcasted_iota(jnp.int32,(8,128),1)==0)
    loss_ref[8:16,:]+=jnp.where(first,count.astype(f32),0.0)
    eye=lax.broadcasted_iota(jnp.int32,(KT,KT),0)==lax.broadcasted_iota(jnp.int32,(KT,KT),1)
    lanes=lax.broadcasted_iota(jnp.int32,(SB,CH),1).astype(f32).astype(bf16)
    lane_ref[...]=lax.broadcasted_iota(jnp.int32,lane_ref.shape,1)
    nch=ents//CH
    def rows_of(kt): return pl.ds(pl.multiple_of(kt*KT,KT),KT)
    def live_of(kt): return (lax.broadcasted_iota(jnp.int32,(KT,1),0)+kt*KT)<count
    def idcol(kt):
        idr=dst_ref[pl.ds(j,1),pl.ds(pl.multiple_of(kt*KT,KT),KT)].astype(f32)
        return jnp.sum(jnp.where(eye,idr,0.0),1,keepdims=True).astype(jnp.int32)
    def aug(kt):
        hb=h_ref[rows_of(kt),:]
        last=hb[:,width//128*128:wa].astype(f32)
        lane=lax.broadcasted_iota(jnp.int32,last.shape,1)+width//128*128
        last=jnp.where(jnp.logical_and(lane==width,jnp.logical_not(live_of(kt))),4e6,last)
        return jnp.concatenate([hb[:,:width//128*128],last.astype(bf16)],1)
    def sdot(ha,ci): return jnp.dot(ha,ta_ref[:,ci*CH:(ci+1)*CH],preferred_element_type=f32)
    def post(s,idc,ci,sp):
        es=jnp.where(idc==lane_ref[0:1,ci*CH:(ci+1)*CH],s,0.0)
        for a in range(CH//128): sp=sp+es[:,128*a:128*(a+1)]
        s_ref[:,ci*CH:(ci+1)*CH]=s
        return sp
    def column(sp,kt):
        live=live_of(kt)
        sq=jnp.sum(sp,1,keepdims=True)*4.0
        rr=lax.rsqrt(sq)
        x=sq*rr-margin
        a=jnp.where(live,jax.nn.sigmoid(x)*rr,0.0)
        inva=jnp.where(live,1.0/a,0.0)
        pos=jnp.where(live,jnp.maximum(x,0.0)+jnp.log(1.0+jnp.exp(-jnp.abs(x))),0.0)
        p8=pos[0:8]
        for b in range(1,KT//8): p8+=pos[8*b:8*b+8]
        loss_ref[0:8,:]+=jnp.where(lax.broadcasted_iota(jnp.int32,(8,128),1)==0,p8,0.0)
        return a,inva
    ha=aug(0); idc=idcol(0); sp=jnp.zeros((KT,128),f32)
    for ci in range(nch): sp=post(sdot(ha,ci),idc,ci,sp)
    a0,i0=column(sp,0)
    def tile(kt,carry):
        rho,inva,idc=carry
        nk=jnp.minimum(kt+1,tiles-1)
        hb=h_ref[rows_of(kt),:]
        hf=hb[:,:width].astype(f32)
        hi,mid,lo=split3(rho)
        ex=lax.broadcasted_iota(jnp.int32,(KT,wa-width),1)
        pad=jnp.where(ex==0,hi,jnp.where(ex==1,mid,jnp.where(ex==2,lo,0.0)))
        hat=jnp.concatenate([(hf*rho),pad],1).astype(bf16).T
        ha=aug(nk); nidc=idcol(nk)
        gh=jnp.zeros((KT,wa),f32)
        sp=jnp.zeros((KT,128),f32)
        lsum=jnp.zeros((8,CH),f32)
        rs=[jnp.zeros((SB,128),f32)]*(KT//SB)
        invn=inva*(0.25/negcount)
        pend=None
        for ci in range(nch+1):
            if ci<nch:
                cols=slice(ci*CH,(ci+1)*CH)
                cr=crow_ref[0:1,cols]
                p=None
                for sub in range(KT//SB):
                    at=slice(sub*SB,(sub+1)*SB)
                    s=s_ref[at,cols]
                    r=lax.rsqrt(s)
                    th=jnp.tanh(margin*0.5-s*r)
                    mask=(idc[at]-ci*CH).astype(f32).astype(bf16)==lanes
                    xf=((1.0+th)*cr)*(r*invn[at])
                    for b in range(CH//128): rs[sub]=rs[sub]+xf[:,128*b:128*(b+1)]
                    m_ref[at,cols]=jnp.where(mask,bf16(1.0),bf16(0.0))-xf.astype(bf16)
                    o=1.0-th
                    for b in range(SB//8): p=o[8*b:8*b+8] if p is None else p*o[8*b:8*b+8]
                lsum+=(math.log(2.0)*(KT//8)-jnp.log(p))*cr
                sp=post(sdot(ha,ci),nidc,ci,sp)
            if ci>=1:
                pc=slice((ci-1)*CH,ci*CH)
                gh+=jnp.dot(m_ref[:,pc],tr_ref[pc,:],preferred_element_type=f32)
                acc_ref[:,pc]+=jnp.dot(hat,m_ref[:,pc],preferred_element_type=f32)
        l8=lsum[:,0:128]
        for b in range(1,CH//128): l8+=lsum[:,128*b:128*(b+1)]
        loss_ref[0:8,:]+=l8*(1.0/negcount)
        out=(hf*(1.0-jnp.sum(jnp.concatenate(rs,0),1,keepdims=True))-gh[:,:width])*rho
        gh_ref[rows_of(kt),:width]=out.astype(bf16)
        live=kt+1<tiles
        na,ni=column(jnp.where(live,sp,1.0),jnp.where(live,nk,tiles))
        return na,ni,nidc
    lax.fori_loop(0,tiles,tile,(a0,i0,idc))
    g_ref[0]=tf*acc_ref[width:width+1,:]+tf*acc_ref[width+1:width+2,:]+tf*acc_ref[width+2:width+3,:]-acc_ref[0:width,:]

def run_blocks(h,tables,dst,neg,counts,negcount,CH=256):
    parts,width,ents=tables.shape
    cap=h.shape[0]//parts
    wa=WA
    nn=neg.shape[-1]
    gs=pltpu.PrefetchScalarGridSpec(num_scalar_prefetch=1,grid=(parts,),
      in_specs=[pl.BlockSpec((cap,h.shape[1]),lambda j,c:(j,0)),
                pl.BlockSpec((1,width,ents),lambda j,c:(j,0,0)),
                pl.BlockSpec((parts,cap),lambda j,c:(0,0)),
                pl.BlockSpec((1,1,nn),lambda j,c:(j,0,0))],
      out_specs=[pl.BlockSpec((cap,width),lambda j,c:(j,0)),
                 pl.BlockSpec((1,width,ents),lambda j,c:(j,0,0)),
                 pl.BlockSpec((16,128),lambda j,c:(0,0))],
      scratch_shapes=[pltpu.VMEM((wa,ents),bf16),pltpu.VMEM((ents,wa),bf16),
                      pltpu.VMEM((wa,ents),f32),pltpu.VMEM((8,ents),f32),pltpu.VMEM((KT,ents),f32),pltpu.VMEM((8,ents),jnp.int32),pltpu.VMEM((KT,ents),bf16)])
    return pl.pallas_call(functools.partial(block_kernel,width,ents,negcount,CH),grid_spec=gs,name="k2_blocks",
      out_shape=[jax.ShapeDtypeStruct((h.shape[0],width),bf16),jax.ShapeDtypeStruct(tables.shape,f32),jax.ShapeDtypeStruct((16,128),f32)],
      compiler_params=pltpu.CompilerParams(vmem_limit_bytes=60<<20,dimension_semantics=("arbitrary",)))(counts,h,tables,dst,neg)


HALF=208

def reduce_kernel(g_ref, gh_ref, src_ref, rid_ref, sc_ref,
                  ge_ref, gr_ref, sco_ref,
                  pr, own, sacc, racc, sa0, sa1, ra0, ra1, sb0, sb1, rb0, rb1, sz, rz, ghb, rp, rsz, rzr, scb,
                  ps, prr, osem, gsem, sas, sar, sbs, sbr, zs, zr, rps, rpr, rzs, rzrr, gxs, gxr, gys, gyr, gds, gdr, css, csr, czs, czr):
    parts,width,ents=g_ref.shape
    nz=4; CK=ents//4; last=nz-1
    cap=src_ref.shape[1]
    nrel=gr_ref.shape[0]
    c,z,k,xn,yn=place()
    e=2*z+k; sib=2*z+1-k
    x=lax.rem(c,2); y=lax.div(c,2); xo=1-x; yo=1-y
    bar=pltpu.get_barrier_semaphore()
    for to in ((c,sib),(xn,e),(yn,e))+tuple((c,lax.rem(e+2*d,parts)) for d in range(1,nz)):
        pl.semaphore_signal(bar,inc=1,device_id=to,device_id_type=MESH)
    order=[lax.rem(z+1+i,nz) for i in range(nz)]
    rows_of=(pl.ds(0,HALF),pl.ds(HALF,width-HALF))
    lo=(0,HALF); num=(HALF,width-HALF)
    def load(i): return pltpu.make_async_copy(g_ref.at[2*order[i]+k],own.at[i%2],osem.at[i%2])
    def gload(b): return pltpu.make_async_copy(gh_ref.at[pl.ds(b*cap,cap),:],ghb.at[b%2],gsem.at[b%2])
    gload(0).start(); load(0).start(); load(1).start()
    pl.semaphore_wait(bar,nz+2)
    def rc(src,dst,s,r,to):
        return pltpu.make_async_remote_copy(src_ref=src,dst_ref=dst,send_sem=s,recv_sem=r,device_id=to,device_id_type=MESH)
    def pair(i,h): return rc(g_ref.at[2*order[i]+1-k,rows_of[h],:],pr.at[i,rows_of[h],:],ps.at[i,h],prr.at[i,h],(c,sib))
    for i in range(2):
        for h in range(2): pair(i,h).start()
    def lane(ck,n=1): return pl.ds(pl.multiple_of(ck*CK,CK),n*CK)
    near=((xn,e),(yn,e)); sa=(sa0,sa1); ra=(ra0,ra1); sb=(sb0,sb1); rb=(rb0,rb1)
    def ac(i,h): return rc(sa[h].at[i],ra[h].at[i],sas.at[i,h],sar.at[i,h],near[h])
    def bc(i,h): return rc(sb[h].at[i],rb[h].at[i],sbs.at[i,h],sbr.at[i,h],near[1-h])
    def zc(i,h): return rc(sz.at[i,rows_of[h],:],rz.at[i,rows_of[h],:],zs.at[i,h],zr.at[i,h],(c,2*order[i]+k))
    gone=((xo,xo+2),(2*yo,2*yo+1))
    kept=((x,x+2),(2*y,2*y+1))
    passed=(x+2*yo,2*y+xo)
    mine=(y,x)
    RB=16
    def strips(h,fn):
        fn(rows_of[h],pl.ds(0,num[h]))
    def st0(i,h):
        if h==0 and i!=last: load(i).wait()
        pair(i,h).wait_recv()
        def one(rows,rel):
            for s in range(2):
                l=lane(gone[h][s])
                sa[h][i,rel,s*CK:(s+1)*CK]=(pr[i,rows,l]+own[i%2,rows,l]).astype(bf16)
                l=lane(kept[h][s])
                pr[i,rows,l]=pr[i,rows,l]+own[i%2,rows,l]
        strips(h,one)
        ac(i,h).start()
        if h==1 and i+2<nz:
            load(i+2).start()
            for g in range(2): pair(i+2,g).start()
    def stB(i,h):
        ac(i,h).wait_recv()
        def one(rows,rel):
            sb[h][i,rel,:]=(pr[i,rows,lane(passed[h])]+ra[h][i,rel,lane(1-mine[h])].astype(f32)).astype(sb0.dtype)
            pr[i,rows,lane(c)]=pr[i,rows,lane(c)]+ra[h][i,rel,lane(mine[h])].astype(f32)
        strips(h,one)
        bc(i,h).start()
    def stZ(i,h):
        bc(i,h).wait_recv()
        def one(rows,rel):
            v=pr[i,rows,lane(c)]+rb[h][i,rel,:].astype(f32)
            if i==last: ge_ref[rows,lane(c)]=v
            else: sz[i,rows,:]=v.astype(sz.dtype)
        strips(h,one)
        if i!=last: zc(i,h).start()
    def both(fn,i):
        fn(i,0); fn(i,1)
    def getblock(b):
        gload(b).wait()
        gload((b+1)%parts).start()
    def slot(ids_ref,acc,b,RC):
        ids=ids_ref[b:b+1,:]
        def chunk(t,_):
            rows=pl.ds(pl.multiple_of(t*RC,8),RC)
            oh=jnp.where(lax.broadcasted_iota(i32,(RC,cap),0)==ids-t*RC,1.0,0.0).astype(bf16)
            d=jnp.dot(oh,ghb[b%2],preferred_element_type=f32)
            if b==0: acc[rows,:]=d
            else: acc[rows,:]=acc[rows,:]+d
            return 0
        lax.fori_loop(0,acc.shape[0]//RC,chunk,0)
    def src(b):
        getblock(b); slot(src_ref,sacc,b,CK)
    def rel(b):
        getblock(b); slot(rid_ref,racc,b,2*nrel)
    def addsrc():
        def it(t,_):
            l=pl.ds(pl.multiple_of(t*128,128),128)
            own[last%2,:,l]=own[last%2,:,l]+sacc[l,:].T
            return 0
        lax.fori_loop(0,ents//128,it,0)
    def grp(g): return pl.ds(pl.multiple_of(g*nrel,8),nrel)
    def relpair(i): return rc(racc.at[grp(2*order[i]+1-k),:],rp.at[i],rps.at[i],rpr.at[i],(c,sib))
    def relz(i): return rc(rsz.at[i],rzr.at[i],rzs.at[i],rzrr.at[i],(c,2*order[i]+k))
    src(0)
    both(st0,0)
    src(1)
    src(2)
    src(3)
    both(st0,1)
    src(4)
    both(stB,0)
    src(5)
    src(6)
    both(st0,2)
    src(7)
    load(last).wait()
    addsrc()
    both(stB,1)
    both(stZ,0)
    rel(0)
    both(st0,3)
    rel(1)
    both(stB,2)
    both(stZ,1)
    rel(2)
    rel(3)
    rel(4)
    rel(5)
    both(stB,3)
    rel(6)
    both(stZ,2)
    rel(7)
    for i in range(nz): relpair(i).start()
    for i in range(last):
        relpair(i).wait_recv()
        rsz[i]=(racc[grp(2*order[i]+k),:]+rp[i]).astype(rsz.dtype)
        relz(i).start()
    both(stZ,3)
    gload(0).wait()
    sq=jnp.zeros((RB,CK),f32)
    def gx(h,l): return rc(ge_ref.at[rows_of[h],l],ge_ref.at[rows_of[h],l],gxs.at[h],gxr.at[h],(xn,e))
    def gy(h,l): return rc(ge_ref.at[rows_of[h],l],ge_ref.at[rows_of[h],l],gys.at[h],gyr.at[h],(yn,e))
    def gd(h,l): return rc(ge_ref.at[rows_of[h],l],ge_ref.at[rows_of[h],l],gds.at[h],gdr.at[h],near[1-h])
    for h in range(2):
        for i in range(last): zc(i,h).wait_recv()
        rows=rows_of[h]
        v=ge_ref[rows,lane(c)]
        for i in range(last): v=v+rz[i,rows,:].astype(f32)
        ge_ref[rows,lane(c)]=v
        v=v*v
        for b in range(0,num[h],RB): sq=sq+v[b:b+RB]
        if h==0: gx(0,lane(c)).start()
        else: gy(1,lane(c)).start()
    gy(0,lane(c)).start(); gx(1,lane(c)).start()
    relpair(last).wait_recv()
    rv=racc[grp(e),:]+rp[last]
    for i in range(last):
        relz(i).wait_recv()
        rv=rv+rzr[i].astype(f32)
    gr_ref[...]=rv
    one=jnp.sum(sq)+3.0*jnp.sum(rv*rv)
    row=lax.broadcasted_iota(i32,(8,128),0)
    v=jnp.where(row==0,one,jnp.where(row==1,jnp.sum(sc_ref[0:8,:]),jnp.where(row==2,jnp.sum(sc_ref[8:16,:]),0.0)))
    def swap(s,v,to):
        scb[s]=v
        cp=rc(scb.at[s],scb.at[3+s],css.at[s],csr.at[s],to)
        cp.start(); cp.wait()
        return v+scb[3+s]
    v=swap(0,v,(c,sib))
    scb[6+z]=v
    def cz(d): return rc(scb.at[6+z],scb.at[6+z],czs.at[d],czr.at[d],(c,lax.rem(e+2*d,parts)))
    for d in range(1,nz): cz(d).start()
    gx(0,lane(xn)).wait_recv(); gd(0,lane(xn)).start()
    gy(1,lane(yn)).wait_recv(); gd(1,lane(yn)).start()
    for d in range(1,nz): cz(d).wait()
    v=(scb[6]+scb[7])+(scb[8]+scb[9])
    v=swap(1,v,(xn,e))
    v=swap(2,v,(yn,e))
    live=v[2:3,:]
    norm=jnp.sqrt(v[0:1,:])/live
    clip=0.01/math.sqrt(4*parts*parts*cap)
    scale=jnp.minimum(1.0,clip/norm)/live
    sco_ref[...]=jnp.where(row==0,norm,jnp.where(row==3,scale,v))
    gx(1,lane(xn)).wait_recv(); gy(0,lane(yn)).wait_recv()
    gd(0,lane(3-c)).wait_recv(); gd(1,lane(3-c)).wait_recv()
    for h in range(2):
        gx(h,lane(c)).wait_send(); gy(h,lane(c)).wait_send()
        for i in range(nz):
            pair(i,h).wait_send(); ac(i,h).wait_send(); bc(i,h).wait_send()
            if i<last: zc(i,h).wait_send()
    gd(0,lane(xn)).wait_send(); gd(1,lane(yn)).wait_send()
    for i in range(nz):
        relpair(i).wait_send()
        if i<last: relz(i).wait_send()

def reduce_call(g,gh,src,rid,sc,nrel,BT=bf16,ZT=bf16,RT=bf16):
    parts,width,ents=g.shape
    cap=src.shape[1]; nz=4; CK=ents//4
    D=pltpu.SemaphoreType.DMA
    V=pl.BlockSpec(memory_space=pltpu.VMEM); A=pl.BlockSpec(memory_space=pl.ANY)
    VM=pltpu.VMEM
    rest=width-HALF
    return pl.pallas_call(reduce_kernel,name="k3_reduce",
        in_specs=[A,A,V,V,V],out_specs=[V,V,V],
        out_shape=[jax.ShapeDtypeStruct((width,ents),f32),jax.ShapeDtypeStruct((nrel,width),f32),jax.ShapeDtypeStruct((8,128),f32)],
        scratch_shapes=[VM((nz,width,ents),f32),VM((2,width,ents),f32),VM((ents,width),f32),VM((parts*nrel,width),f32),
            VM((nz,HALF,2*CK),bf16),VM((nz,rest,2*CK),bf16),VM((nz,HALF,2*CK),bf16),VM((nz,rest,2*CK),bf16),
            VM((nz,HALF,CK),BT),VM((nz,rest,CK),BT),VM((nz,HALF,CK),BT),VM((nz,rest,CK),BT),
            VM((nz-1,width,CK),ZT),VM((nz-1,width,CK),ZT),
            VM((2,cap,width),bf16),VM((nz,nrel,width),f32),VM((nz-1,nrel,width),RT),VM((nz-1,nrel,width),RT),VM((10,8,128),f32),
            D((4,2)),D((4,2)),D((2,)),D((2,)),D((4,2)),D((4,2)),D((4,2)),D((4,2)),D((3,2)),D((3,2)),D((4,)),D((4,)),D((3,)),D((3,)),
            D((2,)),D((2,)),D((2,)),D((2,)),D((2,)),D((2,)),D((3,)),D((3,)),D((4,)),D((4,))],
        compiler_params=pltpu.CompilerParams(collective_id=2,has_side_effects=True,vmem_limit_bytes=62<<20))(g,gh,src,rid,sc)


def cube_body(
    ent_table,
    entity_first_moment,
    ent_v,
    rel_table,
    relation_first_moment,
    rel_v,
    src_ids,
    rel_ids,
    dst_ids,
    neg_ids,
    bucket_counts,
):
    parts = src_ids.shape[2]
    negcount = neg_ids.shape[3]
    nrel = rel_table.shape[1]
    padded = -(-negcount // 1024) * 1024
    negs = jnp.pad(neg_ids[0, 0], ((0, 0), (0, padded - negcount)), constant_values=-1)
    tables, hidden, arrived = gather_call(
        ent_table.T, rel_table, src_ids[0, 0], rel_ids[0, 0], negs.reshape(parts, -1, 128)
    )
    back, partial, sums = run_blocks(
        hidden,
        tables,
        dst_ids[0, 0],
        arrived.reshape(parts, 1, padded),
        bucket_counts[0, 0],
        negcount,
    )
    ent_grad, rel_grad, totals = reduce_call(
        partial, back, src_ids[0, 0], rel_ids[0, 0], sums, nrel
    )
    grad_norm, loss_sum, total, scale = totals[0, 0], totals[1, 0], totals[2, 0], totals[3, 0]
    new_ent, new_ent_m, new_ent_v = adamw(ent_table, entity_first_moment, ent_v, scale * ent_grad.T)
    new_rel, new_rel_m, new_rel_v = adamw(
        rel_table, relation_first_moment, rel_v, scale * rel_grad[None]
    )
    return (
        loss_sum,
        total,
        grad_norm,
        new_ent,
        new_ent_m,
        new_ent_v,
        new_ent.astype(jnp.bfloat16),
        new_rel,
        new_rel_m,
        new_rel_v,
        new_rel.astype(jnp.bfloat16),
    )


def solution(mesh):
    body = cube_body if mesh.shape["rel"] == 4 and mesh.shape["ent"] == 8 else general_body
    return jax.shard_map(
        body,
        mesh=mesh,
        in_specs=(
            P("ent", None),
            P("ent", None),
            P("ent", None),
            P(None, ("rel", "ent"), None),
            P(None, ("rel", "ent"), None),
            P(None, ("rel", "ent"), None),
            P("rel", "ent", None, None),
            P("rel", "ent", None, None),
            P("rel", "ent", None, None),
            P("rel", "ent", None, None),
            P("rel", "ent", None),
        ),
        out_specs=(
            P(),
            P(),
            P(),
            P("ent", None),
            P("ent", None),
            P("ent", None),
            P("ent", None),
            P(None, ("rel", "ent"), None),
            P(None, ("rel", "ent"), None),
            P(None, ("rel", "ent"), None),
            P(None, ("rel", "ent"), None),
        ),
        check_vma=False,
    )
```

```python
import functools
import math

import jax
import jax.numpy as jnp
from jax import lax
from jax.experimental import pallas as pl
from jax.experimental.pallas import tpu as pltpu
from jax.sharding import PartitionSpec as P

STEP = 10
f32 = jnp.float32
bf16 = jnp.bfloat16
i32 = jnp.int32
MESH = pl.DeviceIdType.MESH


margin = 2.5
beta_one = 0.9
beta_two = 0.999
learn_rate = 0.05
decay_rate = 0.01
epsilon = 1e-16


def shortened(array):
    return jax.tree.map(lambda a: a.astype(jnp.bfloat16) if a.dtype == jnp.float32 else a, array)


def adamw(weight, moment, second, grad):
    moment = beta_one * moment + (1.0 - beta_one) * grad
    second = beta_two * second + (1.0 - beta_two) * grad * grad
    m_hat = moment / (1.0 - beta_one**STEP)
    v_hat = second / (1.0 - beta_two**STEP)
    weight = weight - learn_rate * (m_hat / (jnp.sqrt(v_hat) + epsilon) + decay_rate * weight)
    return (weight, moment, second)


def general_body(
    ent_table,
    entity_first_moment,
    ent_v,
    rel_table,
    relation_first_moment,
    rel_v,
    src_ids,
    rel_ids,
    dst_ids,
    neg_ids,
    bucket_counts,
):
    parts = src_ids.shape[2]
    slots = src_ids.shape[3]
    width = ent_table.shape[1]
    negcount = neg_ids.shape[3]
    clip_level = 0.01 / math.sqrt(lax.axis_size("rel") * lax.axis_size("ent") * parts * slots)
    ent_low = ent_table.astype(jnp.bfloat16)
    layers = lax.all_gather(rel_table.astype(jnp.bfloat16), "ent", axis=1, tiled=True)
    rel_sum = (
        layers[0].astype(jnp.float32)
        + layers[1].astype(jnp.float32)
        + layers[2].astype(jnp.float32)
    )
    sources = src_ids[0, 0]
    relation = rel_ids[0, 0]
    counts = bucket_counts[0, 0]
    hidden = ent_low[sources].astype(jnp.float32) + rel_sum[relation]
    total = lax.psum(jnp.sum(counts).astype(jnp.float32), ("rel", "ent"))
    arrived, dst_in, count_in = (
        lax.all_to_all(hidden.astype(jnp.bfloat16), "ent", split_axis=0, concat_axis=0, tiled=True),
        lax.all_to_all(dst_ids[0, 0], "ent", split_axis=0, concat_axis=0, tiled=True),
        lax.all_to_all(counts[:, None], "ent", split_axis=0, concat_axis=0, tiled=True),
    )
    live = (jnp.arange(slots, dtype=jnp.int32)[None, :] < count_in).astype(jnp.float32)
    negatives = neg_ids[0, 0]

    def block(args):
        hid, dst, neg, alive = args
        weight = alive / total
        hid_f = hid.astype(jnp.float32)
        diff = hid_f - ent_low[dst].astype(jnp.float32)
        pos_dist = jnp.sqrt(jnp.sum(diff * diff, -1) + 1.0)
        rows = ent_low[neg]
        rows_f = rows.astype(jnp.float32)
        prod = lax.dot_general(
            hid, rows, (((1,), (1,)), ((), ())), preferred_element_type=jnp.float32
        )
        sq = (
            jnp.sum(hid_f * hid_f, -1)[:, None] + jnp.sum(rows_f * rows_f, -1)[None, :] - 2.0 * prod
        )
        neg_dist = jnp.sqrt(sq + 1.0)
        per_edge = jax.nn.softplus(pos_dist - margin) + jnp.mean(
            jax.nn.softplus(margin - neg_dist), -1
        )
        loss = jnp.sum(alive * per_edge)
        g_pos = weight * jax.nn.sigmoid(pos_dist - margin)
        g_diff = (g_pos / pos_dist)[:, None] * diff
        g_sq = -(weight[:, None] / negcount) * jax.nn.sigmoid(margin - neg_dist) / (2.0 * neg_dist)
        g_prod = (-2.0 * g_sq).astype(jnp.bfloat16)
        g_hid = (
            g_diff
            + 2.0 * hid_f * jnp.sum(g_sq, 1)[:, None]
            + jnp.dot(g_prod, rows, preferred_element_type=jnp.float32)
        )
        g_rows = 2.0 * rows_f * jnp.sum(g_sq, 0)[:, None] + lax.dot_general(
            g_prod, hid, (((0,), (0,)), ((), ())), preferred_element_type=jnp.float32
        )
        return (loss, g_hid.astype(jnp.bfloat16), -g_diff, g_rows)

    losses, back, g_target, g_negative = lax.map(
        block, (arrived, dst_in, negatives, live), batch_size=min(4, parts)
    )
    returned = (
        jax.tree.map(
            lambda part, own: part.astype(own.dtype),
            lax.all_to_all(shortened(back), "ent", split_axis=0, concat_axis=0, tiled=True),
            back,
        )
        .reshape(-1, width)
        .astype(jnp.float32)
    )
    ent_grad = jnp.zeros(ent_table.shape, jnp.float32)
    ent_grad = ent_grad.at[dst_in.reshape(-1)].add(g_target.reshape(-1, width))
    ent_grad = ent_grad.at[negatives.reshape(-1)].add(g_negative.reshape(-1, width))
    ent_grad = ent_grad.at[sources.reshape(-1)].add(returned)
    ent_grad = lax.psum(ent_grad, "rel")
    rel_local = jnp.zeros(rel_sum.shape, jnp.float32).at[relation.reshape(-1)].add(returned)
    rel_grad = lax.psum_scatter(rel_local, "ent", scatter_dimension=0, tiled=True)
    own_squares = jnp.where(
        lax.axis_index("rel") == 0, jnp.sum(ent_grad * ent_grad), 0.0
    ) + 3.0 * jnp.sum(rel_grad * rel_grad)
    squares, loss_sum = lax.psum((own_squares, jnp.sum(losses)), ("rel", "ent"))
    grad_norm = jnp.sqrt(squares)
    scale = jnp.minimum(1.0, clip_level / grad_norm)
    new_ent, new_ent_m, new_ent_v = adamw(ent_table, entity_first_moment, ent_v, scale * ent_grad)
    new_rel, new_rel_m, new_rel_v = adamw(
        rel_table, relation_first_moment, rel_v, scale * rel_grad[None]
    )
    return (
        loss_sum,
        total,
        grad_norm,
        new_ent,
        new_ent_m,
        new_ent_v,
        new_ent.astype(jnp.bfloat16),
        new_rel,
        new_rel_m,
        new_rel_v,
        new_rel.astype(jnp.bfloat16),
    )


KT1=256
RP=256

def split3(x):
    hi=x.astype(bf16).astype(f32); r=x-hi
    mid=r.astype(bf16).astype(f32); lo=r-mid
    return hi,mid,lo

def place():
    r=lax.axis_index("rel"); e=lax.axis_index("ent")
    z=lax.div(e,2); k=lax.rem(e,2)
    xn=r+1-2*lax.rem(r,2)
    yn=lax.rem(r+2,4)
    return r,z,k,xn,yn

def gather_kernel(et_ref, rt_ref, src_ref, rid_ref, neg_ref,
                  tab_ref, h_ref, negout_ref,
                  tb, rall, eh, hb, lsem, hsem, us, ds, zr, xs, xr, ys, yr, fs, fr, cs, cr, rcs, rcr, ns, nr):
    width,ents=et_ref.shape
    nz=4; parts=8
    CK=ents//4
    cap=src_ref.shape[1]
    c,z,k,xn,yn=place()
    e=2*z+k
    half=208
    sib=2*z+1-k
    bar=pltpu.get_barrier_semaphore()
    for d in range(1,parts):
        pl.semaphore_signal(bar,inc=1,device_id=(c,lax.rem(e+d,parts)),device_id_type=MESH)
    pl.semaphore_signal(bar,inc=1,device_id=(xn,e),device_id_type=MESH)
    pl.semaphore_signal(bar,inc=1,device_id=(yn,e),device_id_type=MESH)
    tb[...]=et_ref[...].astype(bf16)
    low=[rt_ref[l].astype(bf16).astype(f32) for l in range(3)]
    rsum=jnp.concatenate([low[0]+low[1]+low[2],jnp.zeros((RP-rt_ref.shape[1],width),f32)],0)
    rall[e]=rsum.T.astype(bf16)
    pl.semaphore_wait(bar,parts+1)
    def rc(src,dst,s,r,to):
        return pltpu.make_async_remote_copy(src_ref=src,dst_ref=dst,send_sem=s,recv_sem=r,device_id=to,device_id_type=MESH)
    rows_of=(pl.ds(0,half),pl.ds(half,width-half))
    def lane(ck): return pl.ds(pl.multiple_of(ck*CK,CK),CK)
    SEQ=((2,1),(0,1),(2,2),(1,1),(2,3),(0,2),(1,2),(0,3),(1,3))
    def part(o,u,own=False):
        if u==2: return rall.at[2*o+k]
        return tb.at[rows_of[u],lane(c)] if own else tab_ref.at[2*o+k,rows_of[u],lane(c)]
    def up(o,u,own): return rc(part(o,u,own),part(o,u),us.at[u,o],zr.at[u,o],(c,2*(z+1)+k))
    def down(o,u,own): return rc(part(o,u,own),part(o,u),ds.at[u,o],zr.at[u,o],(c,2*(z-1)+k))
    def sides(dist,fn):
        @pl.when(z>=dist)
        def _(): fn(z-dist)
        @pl.when(z+dist<nz)
        def _(): fn(z+dist)
    def along(n,act):
        u,dist=SEQ[n]
        f=dist-1
        @pl.when(jnp.logical_and(z<nz-1,z>=f))
        def _(): act(up(z-f,u,f==0))
        @pl.when(jnp.logical_and(z>0,z+f<nz))
        def _(): act(down(z+f,u,f==0))
    def xc(o,h,l): return rc(tab_ref.at[2*o+k,rows_of[h],l],tab_ref.at[2*o+k,rows_of[h],l],xs.at[o,h],xr.at[o,h],(xn,e))
    def yc(o,h,l): return rc(tab_ref.at[2*o+k,rows_of[h],l],tab_ref.at[2*o+k,rows_of[h],l],ys.at[o,h],yr.at[o,h],(yn,e))
    def fc(o,h,l):
        v=tab_ref.at[2*o+k,rows_of[h],l]
        return rc(v,v,fs.at[o,h],fr.at[o,h],((yn,e),(xn,e))[h])
    def cc(o,h,kk,own=False):
        v=tab_ref.at[2*o+kk,rows_of[h],:]
        return rc(tb.at[rows_of[h],:] if own else v,v,cs.at[o,h],cr.at[o,h],(c,sib))
    def rel_sib(o,kk):
        return rc(rall.at[2*o+kk],rall.at[2*o+kk],rcs.at[o],rcr.at[o],(c,sib))
    along(0,lambda cp: cp.start())
    along(1,lambda cp: cp.start())
    rel_sib(z,k).start()
    def neg_copy(to,own):
        return rc(neg_ref.at[to],negout_ref.at[own],ns.at[to],nr.at[own],(c,to))
    for d in range(1,parts):
        neg_copy(lax.rem(e+d,parts),e).start()
    own_neg=pltpu.make_async_copy(neg_ref.at[e],negout_ref.at[e],lsem.at[1])
    own_neg.start()
    own_tab=pltpu.make_async_copy(tb,tab_ref.at[e],lsem.at[0])
    own_tab.start()
    for h in range(2): cc(z,h,k,True).start()
    def Z(n):
        u,dist=SEQ[n]
        def fn(o):
            up(o,u,False).wait_recv()
            if u==2: rel_sib(o,k).start()
            else:
                xc(o,u,lane(c)).start(); yc(o,u,lane(c)).start()
        sides(dist,fn)
        if n+2<len(SEQ): along(n+2,lambda cp: cp.start())
    def C(dist,h):
        def fn(o):
            if h==0: xc(o,0,lane(xn)).wait_recv(); fc(o,0,lane(xn)).start()
            else: yc(o,1,lane(yn)).wait_recv(); fc(o,1,lane(yn)).start()
        sides(dist,fn)
    def W(dist,h):
        def fn(o):
            if h==0: yc(o,0,lane(yn)).wait_recv()
            else: xc(o,1,lane(xn)).wait_recv()
            fc(o,h,lane(3-c)).wait_recv()
            cc(o,h,k).start()
        sides(dist,fn)
    def onehot(ids):
        return jnp.where(lax.broadcasted_iota(i32,(ents,KT1),0)==ids,1.0,0.0).astype(bf16)
    nt=cap//KT1
    def src_slot(b):
        def tile(t,_):
            l=pl.ds(pl.multiple_of(t*KT1,KT1),KT1)
            eh[b,:,l]=jnp.dot(tb[...],onehot(src_ref[b:b+1,l]),preferred_element_type=f32).astype(bf16)
            return 0
        lax.fori_loop(0,nt,tile,0)
    def out_copy(b):
        return pltpu.make_async_copy(hb.at[b%2],h_ref.at[pl.ds(b*cap,cap),:],hsem.at[b%2])
    nrel=rt_ref.shape[1]
    def rel_slot(b):
        if b>=2: out_copy(b-2).wait()
        def tile(t,_):
            l=pl.ds(pl.multiple_of(t*KT1,KT1),KT1)
            q=rid_ref[b:b+1,l]
            g=jnp.floor((q.astype(f32)+0.5)*(1.0/nrel)).astype(i32)
            q=q+(RP-nrel)*g
            acc=eh[b,:,l].astype(f32)
            for g0 in range(0,parts):
                oh=jnp.where(lax.broadcasted_iota(i32,(RP,KT1),0)+RP*g0==q,1.0,0.0).astype(bf16)
                acc=acc+jnp.dot(rall[g0],oh,preferred_element_type=f32)
            hid=acc.astype(bf16)
            hf=hid.astype(f32)
            hi,mid,lo=split3(jnp.sum(hf*hf,0,keepdims=True))
            row=lax.broadcasted_iota(i32,(hb.shape[2]-width,KT1),0)
            ex=jnp.where(row==0,hi,jnp.where(row==1,mid,jnp.where(row==2,lo,jnp.where(row<6,1.0,0.0))))
            hb[b%2,pl.ds(pl.multiple_of(t*KT1,KT1),KT1),:]=jnp.concatenate([hf,ex],0).T.astype(bf16)
            return 0
        lax.fori_loop(0,nt,tile,0)
        out_copy(b).start()
    def allrel():
        for o in range(nz): rel_sib(o,1-k).wait_recv()
    src_slot(0)
    src_slot(1)
    Z(0)
    src_slot(2)
    Z(1)
    src_slot(3)
    Z(2)
    src_slot(4)
    C(1,0)
    src_slot(5)
    Z(3)
    src_slot(6)
    Z(4)
    W(1,0)
    src_slot(7)
    C(1,1)
    Z(5)
    allrel()
    rel_slot(0)
    W(1,1)
    Z(6)
    rel_slot(1)
    C(2,0)
    Z(7)
    rel_slot(2)
    W(2,0)
    C(2,1)
    Z(8)
    rel_slot(3)
    W(2,1)
    C(3,0)
    rel_slot(4)
    C(3,1)
    W(3,0)
    rel_slot(5)
    W(3,1)
    rel_slot(6)
    rel_slot(7)
    for n in range(len(SEQ)): along(n,lambda cp: cp.wait_send())
    for h in range(2):
        for o in range(nz): cc(o,h,1-k).wait_recv()
        cc(z,h,k,True).wait_send()
        for dist in range(1,nz):
            def fn(o):
                cc(o,h,k).wait_send()
                xc(o,h,lane(c)).wait_send(); yc(o,h,lane(c)).wait_send()
                fc(o,h,(lane(xn),lane(yn))[h]).wait_send()
            sides(dist,fn)
    for o in range(nz): rel_sib(o,k).wait_send()
    for d in range(1,parts):
        o=lax.rem(e+d,parts)
        neg_copy(o,e).wait_send()
        neg_copy(e,o).wait_recv()
    own_tab.wait(); own_neg.wait()
    out_copy(6).wait(); out_copy(7).wait()

def gather_call(et,rt,src,rid,negs):
    width,ents=et.shape
    parts,cap=src.shape
    D=pltpu.SemaphoreType.DMA
    V=pl.BlockSpec(memory_space=pltpu.VMEM); A=pl.BlockSpec(memory_space=pl.ANY)
    return pl.pallas_call(gather_kernel,name="k1_gather",
        in_specs=[V]*5,out_specs=[A,A,V],
        out_shape=[jax.ShapeDtypeStruct((parts,width,ents),bf16),jax.ShapeDtypeStruct((parts*cap,512),bf16),jax.ShapeDtypeStruct(negs.shape,i32)],
        scratch_shapes=[pltpu.VMEM((width,ents),bf16),pltpu.VMEM((parts,width,RP),bf16),pltpu.VMEM((parts,width,cap),bf16),pltpu.VMEM((2,cap,512),bf16),
            D((2,)),D((2,)),D((3,4)),D((3,4)),D((3,4)),D((4,2)),D((4,2)),D((4,2)),D((4,2)),D((4,2)),D((4,2)),D((4,2)),D((4,2)),D((4,)),D((4,)),D((8,)),D((8,))],
        compiler_params=pltpu.CompilerParams(collective_id=1,has_side_effects=True,vmem_limit_bytes=60<<20))(et,rt,src,rid,negs)


KT = 256
WA=416
SB=32
def block_kernel(width, ents, negcount, CH,
                 counts_ref, h_ref, t_ref, dst_ref, neg_ref, gh_ref, g_ref, loss_ref,
                 ta_ref, tr_ref, acc_ref, crow_ref, s_ref, lane_ref, m_ref):
    j=pl.program_id(0)
    wa=ta_ref.shape[0]
    count=counts_ref[j]
    tiles=lax.div(count+(KT-1),KT)
    t=t_ref[0]
    tf=t.astype(f32)
    norm=(jnp.sum(tf*tf,0,keepdims=True)+1.0)*0.25
    hi,mid,lo=split3(norm)
    ta_ref[0:width,:]=t*bf16(-0.5)
    sub=lax.broadcasted_iota(jnp.int32,(wa-width,ents),0)
    pad=jnp.where(sub<3,0.25,0.0)
    pad=jnp.where(sub==3,hi,pad)
    pad=jnp.where(sub==4,mid,pad)
    pad=jnp.where(sub==5,lo,pad)
    ta_ref[width:,:]=pad.astype(bf16)
    tcat=jnp.concatenate([t, jnp.where(sub==0,1.0,0.0).astype(bf16)],0)
    tr_ref[...]=tcat.T
    ids=neg_ref[0]
    nn=ids.shape[1]
    ohi=jnp.where(lax.broadcasted_iota(jnp.int32,(ents//128,nn),0)==lax.shift_right_arithmetic(ids,7),1.0,0.0).astype(bf16)
    olo=jnp.where(lax.broadcasted_iota(jnp.int32,(128,nn),0)==(ids&127),1.0,0.0).astype(bf16)
    c=lax.dot_general(ohi,olo,(((1,),(1,)),((),())),preferred_element_type=f32)
    for i in range(ents//128):
        crow_ref[0:1,128*i:128*(i+1)]=c[i:i+1,:]
    acc_ref[...]=jnp.zeros_like(acc_ref)
    def dead(kt,_):
        gh_ref[pl.ds(pl.multiple_of(kt*KT,KT),KT),:]=jnp.zeros((KT,gh_ref.shape[1]),bf16)
        return 0
    lax.fori_loop(tiles,gh_ref.shape[0]//KT,dead,0)
    @pl.when(j==0)
    def _(): loss_ref[...]=jnp.zeros_like(loss_ref)
    first=jnp.logical_and(lax.broadcasted_iota(jnp.int32,(8,128),0)==0,lax.broadcasted_iota(jnp.int32,(8,128),1)==0)
    loss_ref[8:16,:]+=jnp.where(first,count.astype(f32),0.0)
    eye=lax.broadcasted_iota(jnp.int32,(KT,KT),0)==lax.broadcasted_iota(jnp.int32,(KT,KT),1)
    lanes=lax.broadcasted_iota(jnp.int32,(SB,CH),1).astype(f32).astype(bf16)
    lane_ref[...]=lax.broadcasted_iota(jnp.int32,lane_ref.shape,1)
    nch=ents//CH
    def rows_of(kt): return pl.ds(pl.multiple_of(kt*KT,KT),KT)
    def live_of(kt): return (lax.broadcasted_iota(jnp.int32,(KT,1),0)+kt*KT)<count
    def idcol(kt):
        idr=dst_ref[pl.ds(j,1),pl.ds(pl.multiple_of(kt*KT,KT),KT)].astype(f32)
        return jnp.sum(jnp.where(eye,idr,0.0),1,keepdims=True).astype(jnp.int32)
    def aug(kt):
        hb=h_ref[rows_of(kt),:]
        last=hb[:,width//128*128:wa].astype(f32)
        lane=lax.broadcasted_iota(jnp.int32,last.shape,1)+width//128*128
        last=jnp.where(jnp.logical_and(lane==width,jnp.logical_not(live_of(kt))),4e6,last)
        return jnp.concatenate([hb[:,:width//128*128],last.astype(bf16)],1)
    def sdot(ha,ci): return jnp.dot(ha,ta_ref[:,ci*CH:(ci+1)*CH],preferred_element_type=f32)
    def post(s,idc,ci,sp):
        es=jnp.where(idc==lane_ref[0:1,ci*CH:(ci+1)*CH],s,0.0)
        for a in range(CH//128): sp=sp+es[:,128*a:128*(a+1)]
        s_ref[:,ci*CH:(ci+1)*CH]=s
        return sp
    def column(sp,kt):
        live=live_of(kt)
        sq=jnp.sum(sp,1,keepdims=True)*4.0
        rr=lax.rsqrt(sq)
        x=sq*rr-margin
        a=jnp.where(live,jax.nn.sigmoid(x)*rr,0.0)
        inva=jnp.where(live,1.0/a,0.0)
        pos=jnp.where(live,jnp.maximum(x,0.0)+jnp.log(1.0+jnp.exp(-jnp.abs(x))),0.0)
        p8=pos[0:8]
        for b in range(1,KT//8): p8+=pos[8*b:8*b+8]
        loss_ref[0:8,:]+=jnp.where(lax.broadcasted_iota(jnp.int32,(8,128),1)==0,p8,0.0)
        return a,inva
    ha=aug(0); idc=idcol(0); sp=jnp.zeros((KT,128),f32)
    for ci in range(nch): sp=post(sdot(ha,ci),idc,ci,sp)
    a0,i0=column(sp,0)
    def tile(kt,carry):
        rho,inva,idc=carry
        nk=jnp.minimum(kt+1,tiles-1)
        hb=h_ref[rows_of(kt),:]
        hf=hb[:,:width].astype(f32)
        hi,mid,lo=split3(rho)
        ex=lax.broadcasted_iota(jnp.int32,(KT,wa-width),1)
        pad=jnp.where(ex==0,hi,jnp.where(ex==1,mid,jnp.where(ex==2,lo,0.0)))
        hat=jnp.concatenate([(hf*rho),pad],1).astype(bf16).T
        ha=aug(nk); nidc=idcol(nk)
        gh=jnp.zeros((KT,wa),f32)
        sp=jnp.zeros((KT,128),f32)
        lsum=jnp.zeros((8,CH),f32)
        rs=[jnp.zeros((SB,128),f32)]*(KT//SB)
        invn=inva*(0.25/negcount)
        pend=None
        for ci in range(nch+1):
            if ci<nch:
                cols=slice(ci*CH,(ci+1)*CH)
                cr=crow_ref[0:1,cols]
                p=None
                for sub in range(KT//SB):
                    at=slice(sub*SB,(sub+1)*SB)
                    s=s_ref[at,cols]
                    r=lax.rsqrt(s)
                    th=jnp.tanh(margin*0.5-s*r)
                    mask=(idc[at]-ci*CH).astype(f32).astype(bf16)==lanes
                    xf=((1.0+th)*cr)*(r*invn[at])
                    for b in range(CH//128): rs[sub]=rs[sub]+xf[:,128*b:128*(b+1)]
                    m_ref[at,cols]=jnp.where(mask,bf16(1.0),bf16(0.0))-xf.astype(bf16)
                    o=1.0-th
                    for b in range(SB//8): p=o[8*b:8*b+8] if p is None else p*o[8*b:8*b+8]
                lsum+=(math.log(2.0)*(KT//8)-jnp.log(p))*cr
                sp=post(sdot(ha,ci),nidc,ci,sp)
            if ci>=1:
                pc=slice((ci-1)*CH,ci*CH)
                gh+=jnp.dot(m_ref[:,pc],tr_ref[pc,:],preferred_element_type=f32)
                acc_ref[:,pc]+=jnp.dot(hat,m_ref[:,pc],preferred_element_type=f32)
        l8=lsum[:,0:128]
        for b in range(1,CH//128): l8+=lsum[:,128*b:128*(b+1)]
        loss_ref[0:8,:]+=l8*(1.0/negcount)
        out=(hf*(1.0-jnp.sum(jnp.concatenate(rs,0),1,keepdims=True))-gh[:,:width])*rho
        gh_ref[rows_of(kt),:width]=out.astype(bf16)
        live=kt+1<tiles
        na,ni=column(jnp.where(live,sp,1.0),jnp.where(live,nk,tiles))
        return na,ni,nidc
    lax.fori_loop(0,tiles,tile,(a0,i0,idc))
    g_ref[0]=tf*(acc_ref[width:width+1,:]+acc_ref[width+1:width+2,:]+acc_ref[width+2:width+3,:])-acc_ref[0:width,:]

def run_blocks(h,tables,dst,neg,counts,negcount,CH=256):
    parts,width,ents=tables.shape
    cap=h.shape[0]//parts
    wa=WA
    nn=neg.shape[-1]
    gs=pltpu.PrefetchScalarGridSpec(num_scalar_prefetch=1,grid=(parts,),
      in_specs=[pl.BlockSpec((cap,h.shape[1]),lambda j,c:(j,0)),
                pl.BlockSpec((1,width,ents),lambda j,c:(j,0,0)),
                pl.BlockSpec((parts,cap),lambda j,c:(0,0)),
                pl.BlockSpec((1,1,nn),lambda j,c:(j,0,0))],
      out_specs=[pl.BlockSpec((cap,width),lambda j,c:(j,0)),
                 pl.BlockSpec((1,width,ents),lambda j,c:(j,0,0)),
                 pl.BlockSpec((16,128),lambda j,c:(0,0))],
      scratch_shapes=[pltpu.VMEM((wa,ents),bf16),pltpu.VMEM((ents,wa),bf16),
                      pltpu.VMEM((wa,ents),f32),pltpu.VMEM((8,ents),f32),pltpu.VMEM((KT,ents),f32),pltpu.VMEM((8,ents),jnp.int32),pltpu.VMEM((KT,ents),bf16)])
    return pl.pallas_call(functools.partial(block_kernel,width,ents,negcount,CH),grid_spec=gs,name="k2_blocks",
      out_shape=[jax.ShapeDtypeStruct((h.shape[0],width),bf16),jax.ShapeDtypeStruct(tables.shape,f32),jax.ShapeDtypeStruct((16,128),f32)],
      compiler_params=pltpu.CompilerParams(vmem_limit_bytes=60<<20,dimension_semantics=("arbitrary",)))(counts,h,tables,dst,neg)


HALF=208

def reduce_kernel(g_ref, gh_ref, src_ref, rid_ref, sc_ref,
                  ge_ref, gr_ref, sco_ref,
                  pr, own, sacc, racc, sa0, sa1, ra0, ra1, sb0, sb1, rb0, rb1, sz, rz, ghb, rp, rsz, rzr, scb,
                  ps, prr, osem, gsem, sas, sar, sbs, sbr, zs, zr, rps, rpr, rzs, rzrr, gxs, gxr, gys, gyr, gds, gdr, css, csr, czs, czr):
    parts,width,ents=g_ref.shape
    nz=4; CK=ents//4; last=nz-1
    cap=src_ref.shape[1]
    nrel=gr_ref.shape[0]
    c,z,k,xn,yn=place()
    e=2*z+k; sib=2*z+1-k
    x=lax.rem(c,2); y=lax.div(c,2); xo=1-x; yo=1-y
    bar=pltpu.get_barrier_semaphore()
    for to in ((c,sib),(xn,e),(yn,e))+tuple((c,lax.rem(e+2*d,parts)) for d in range(1,nz)):
        pl.semaphore_signal(bar,inc=1,device_id=to,device_id_type=MESH)
    order=[lax.rem(z+1+i,nz) for i in range(nz)]
    rows_of=(pl.ds(0,HALF),pl.ds(HALF,width-HALF))
    lo=(0,HALF); num=(HALF,width-HALF)
    def load(i): return pltpu.make_async_copy(g_ref.at[2*order[i]+k],own.at[i%2],osem.at[i%2])
    def gload(b): return pltpu.make_async_copy(gh_ref.at[pl.ds(b*cap,cap),:],ghb.at[b%2],gsem.at[b%2])
    gload(0).start(); load(0).start(); load(1).start()
    pl.semaphore_wait(bar,nz+2)
    def rc(src,dst,s,r,to):
        return pltpu.make_async_remote_copy(src_ref=src,dst_ref=dst,send_sem=s,recv_sem=r,device_id=to,device_id_type=MESH)
    def pair(i,h): return rc(g_ref.at[2*order[i]+1-k,rows_of[h],:],pr.at[i,rows_of[h],:],ps.at[i,h],prr.at[i,h],(c,sib))
    for i in range(2):
        for h in range(2): pair(i,h).start()
    def lane(ck,n=1): return pl.ds(pl.multiple_of(ck*CK,CK),n*CK)
    near=((xn,e),(yn,e)); sa=(sa0,sa1); ra=(ra0,ra1); sb=(sb0,sb1); rb=(rb0,rb1)
    def ac(i,h): return rc(sa[h].at[i],ra[h].at[i],sas.at[i,h],sar.at[i,h],near[h])
    def bc(i,h): return rc(sb[h].at[i],rb[h].at[i],sbs.at[i,h],sbr.at[i,h],near[1-h])
    def zc(i,h): return rc(sz.at[i,rows_of[h],:],rz.at[i,rows_of[h],:],zs.at[i,h],zr.at[i,h],(c,2*order[i]+k))
    gone=((xo,xo+2),(2*yo,2*yo+1))
    kept=((x,x+2),(2*y,2*y+1))
    passed=(x+2*yo,2*y+xo)
    mine=(y,x)
    RB=16
    def strips(h,fn):
        fn(rows_of[h],pl.ds(0,num[h]))
    def st0(i,h):
        if h==0 and i!=last: load(i).wait()
        pair(i,h).wait_recv()
        def one(rows,rel):
            for s in range(2):
                l=lane(gone[h][s])
                sa[h][i,rel,s*CK:(s+1)*CK]=(pr[i,rows,l]+own[i%2,rows,l]).astype(bf16)
                l=lane(kept[h][s])
                pr[i,rows,l]=pr[i,rows,l]+own[i%2,rows,l]
        strips(h,one)
        ac(i,h).start()
        if h==1 and i+2<nz:
            load(i+2).start()
            for g in range(2): pair(i+2,g).start()
    def stB(i,h):
        ac(i,h).wait_recv()
        def one(rows,rel):
            sb[h][i,rel,:]=(pr[i,rows,lane(passed[h])]+ra[h][i,rel,lane(1-mine[h])].astype(f32)).astype(sb0.dtype)
            pr[i,rows,lane(c)]=pr[i,rows,lane(c)]+ra[h][i,rel,lane(mine[h])].astype(f32)
        strips(h,one)
        bc(i,h).start()
    def stZ(i,h):
        bc(i,h).wait_recv()
        def one(rows,rel):
            v=pr[i,rows,lane(c)]+rb[h][i,rel,:].astype(f32)
            if i==last: ge_ref[rows,lane(c)]=v
            else: sz[i,rows,:]=v.astype(sz.dtype)
        strips(h,one)
        if i!=last: zc(i,h).start()
    def both(fn,i):
        fn(i,0); fn(i,1)
    def getblock(b):
        gload(b).wait()
        gload((b+1)%parts).start()
    def slot(ids_ref,acc,b,RC):
        ids=ids_ref[b:b+1,:]
        def chunk(t,_):
            rows=pl.ds(pl.multiple_of(t*RC,8),RC)
            oh=jnp.where(lax.broadcasted_iota(i32,(RC,cap),0)==ids-t*RC,1.0,0.0).astype(bf16)
            d=jnp.dot(oh,ghb[b%2],preferred_element_type=f32)
            if b==0: acc[rows,:]=d
            else: acc[rows,:]=acc[rows,:]+d
            return 0
        lax.fori_loop(0,acc.shape[0]//RC,chunk,0)
    def src(b):
        getblock(b); slot(src_ref,sacc,b,CK)
    def rel(b):
        getblock(b); slot(rid_ref,racc,b,2*nrel)
    def addsrc():
        def it(t,_):
            l=pl.ds(pl.multiple_of(t*128,128),128)
            own[last%2,:,l]=own[last%2,:,l]+sacc[l,:].T
            return 0
        lax.fori_loop(0,ents//128,it,0)
    def grp(g): return pl.ds(pl.multiple_of(g*nrel,8),nrel)
    def relpair(i): return rc(racc.at[grp(2*order[i]+1-k),:],rp.at[i],rps.at[i],rpr.at[i],(c,sib))
    def relz(i): return rc(rsz.at[i],rzr.at[i],rzs.at[i],rzrr.at[i],(c,2*order[i]+k))
    src(0)
    src(1)
    both(st0,0)
    src(2)
    src(3)
    both(st0,1)
    src(4)
    both(stB,0)
    src(5)
    src(6)
    both(st0,2)
    src(7)
    load(last).wait()
    addsrc()
    both(stB,1)
    both(stZ,0)
    rel(0)
    rel(1)
    both(st0,3)
    rel(2)
    both(stB,2)
    both(stZ,1)
    rel(3)
    rel(4)
    rel(5)
    both(stB,3)
    rel(6)
    both(stZ,2)
    rel(7)
    for i in range(nz): relpair(i).start()
    for i in range(last):
        relpair(i).wait_recv()
        rsz[i]=(racc[grp(2*order[i]+k),:]+rp[i]).astype(rsz.dtype)
        relz(i).start()
    both(stZ,3)
    gload(0).wait()
    sq=jnp.zeros((RB,CK),f32)
    def gx(h,l): return rc(ge_ref.at[rows_of[h],l],ge_ref.at[rows_of[h],l],gxs.at[h],gxr.at[h],(xn,e))
    def gy(h,l): return rc(ge_ref.at[rows_of[h],l],ge_ref.at[rows_of[h],l],gys.at[h],gyr.at[h],(yn,e))
    def gd(h,l): return rc(ge_ref.at[rows_of[h],l],ge_ref.at[rows_of[h],l],gds.at[h],gdr.at[h],near[1-h])
    for h in range(2):
        for i in range(last): zc(i,h).wait_recv()
        rows=rows_of[h]
        v=ge_ref[rows,lane(c)]
        for i in range(last): v=v+rz[i,rows,:].astype(f32)
        ge_ref[rows,lane(c)]=v
        v=v*v
        for b in range(0,num[h],RB): sq=sq+v[b:b+RB]
        if h==0: gx(0,lane(c)).start()
        else: gy(1,lane(c)).start()
    gy(0,lane(c)).start(); gx(1,lane(c)).start()
    relpair(last).wait_recv()
    rv=racc[grp(e),:]+rp[last]
    for i in range(last):
        relz(i).wait_recv()
        rv=rv+rzr[i].astype(f32)
    gr_ref[...]=rv
    one=jnp.sum(sq)+3.0*jnp.sum(rv*rv)
    row=lax.broadcasted_iota(i32,(8,128),0)
    v=jnp.where(row==0,one,jnp.where(row==1,jnp.sum(sc_ref[0:8,:]),jnp.where(row==2,jnp.sum(sc_ref[8:16,:]),0.0)))
    def swap(s,v,to):
        scb[s]=v
        cp=rc(scb.at[s],scb.at[3+s],css.at[s],csr.at[s],to)
        cp.start(); cp.wait()
        return v+scb[3+s]
    v=swap(0,v,(c,sib))
    scb[6+z]=v
    def cz(d): return rc(scb.at[6+z],scb.at[6+z],czs.at[d],czr.at[d],(c,lax.rem(e+2*d,parts)))
    for d in range(1,nz): cz(d).start()
    gx(0,lane(xn)).wait_recv(); gd(0,lane(xn)).start()
    gy(1,lane(yn)).wait_recv(); gd(1,lane(yn)).start()
    for d in range(1,nz): cz(d).wait()
    v=(scb[6]+scb[7])+(scb[8]+scb[9])
    v=swap(1,v,(xn,e))
    v=swap(2,v,(yn,e))
    live=v[2:3,:]
    norm=jnp.sqrt(v[0:1,:])/live
    clip=0.01/math.sqrt(4*parts*parts*cap)
    scale=jnp.minimum(1.0,clip/norm)/live
    sco_ref[...]=jnp.where(row==0,norm,jnp.where(row==3,scale,v))
    gx(1,lane(xn)).wait_recv(); gy(0,lane(yn)).wait_recv()
    gd(0,lane(3-c)).wait_recv(); gd(1,lane(3-c)).wait_recv()
    for h in range(2):
        gx(h,lane(c)).wait_send(); gy(h,lane(c)).wait_send()
        for i in range(nz):
            pair(i,h).wait_send(); ac(i,h).wait_send(); bc(i,h).wait_send()
            if i<last: zc(i,h).wait_send()
    gd(0,lane(xn)).wait_send(); gd(1,lane(yn)).wait_send()
    for i in range(nz):
        relpair(i).wait_send()
        if i<last: relz(i).wait_send()

def reduce_call(g,gh,src,rid,sc,nrel,BT=bf16,ZT=bf16,RT=bf16):
    parts,width,ents=g.shape
    cap=src.shape[1]; nz=4; CK=ents//4
    D=pltpu.SemaphoreType.DMA
    V=pl.BlockSpec(memory_space=pltpu.VMEM); A=pl.BlockSpec(memory_space=pl.ANY)
    VM=pltpu.VMEM
    rest=width-HALF
    return pl.pallas_call(reduce_kernel,name="k3_reduce",
        in_specs=[A,A,V,V,V],out_specs=[V,V,V],
        out_shape=[jax.ShapeDtypeStruct((width,ents),f32),jax.ShapeDtypeStruct((nrel,width),f32),jax.ShapeDtypeStruct((8,128),f32)],
        scratch_shapes=[VM((nz,width,ents),f32),VM((2,width,ents),f32),VM((ents,width),f32),VM((parts*nrel,width),f32),
            VM((nz,HALF,2*CK),bf16),VM((nz,rest,2*CK),bf16),VM((nz,HALF,2*CK),bf16),VM((nz,rest,2*CK),bf16),
            VM((nz,HALF,CK),BT),VM((nz,rest,CK),BT),VM((nz,HALF,CK),BT),VM((nz,rest,CK),BT),
            VM((nz-1,width,CK),ZT),VM((nz-1,width,CK),ZT),
            VM((2,cap,width),bf16),VM((nz,nrel,width),f32),VM((nz-1,nrel,width),RT),VM((nz-1,nrel,width),RT),VM((10,8,128),f32),
            D((4,2)),D((4,2)),D((2,)),D((2,)),D((4,2)),D((4,2)),D((4,2)),D((4,2)),D((3,2)),D((3,2)),D((4,)),D((4,)),D((3,)),D((3,)),
            D((2,)),D((2,)),D((2,)),D((2,)),D((2,)),D((2,)),D((3,)),D((3,)),D((4,)),D((4,))],
        compiler_params=pltpu.CompilerParams(collective_id=2,has_side_effects=True,vmem_limit_bytes=62<<20))(g,gh,src,rid,sc)


def cube_body(
    ent_table,
    entity_first_moment,
    ent_v,
    rel_table,
    relation_first_moment,
    rel_v,
    src_ids,
    rel_ids,
    dst_ids,
    neg_ids,
    bucket_counts,
):
    parts = src_ids.shape[2]
    negcount = neg_ids.shape[3]
    nrel = rel_table.shape[1]
    padded = -(-negcount // 1024) * 1024
    negs = jnp.pad(neg_ids[0, 0], ((0, 0), (0, padded - negcount)), constant_values=-1)
    tables, hidden, arrived = gather_call(
        ent_table.T, rel_table, src_ids[0, 0], rel_ids[0, 0], negs.reshape(parts, -1, 128)
    )
    back, partial, sums = run_blocks(
        hidden,
        tables,
        dst_ids[0, 0],
        arrived.reshape(parts, 1, padded),
        bucket_counts[0, 0],
        negcount,
    )
    ent_grad, rel_grad, totals = reduce_call(
        partial, back, src_ids[0, 0], rel_ids[0, 0], sums, nrel
    )
    grad_norm, loss_sum, total, scale = totals[0, 0], totals[1, 0], totals[2, 0], totals[3, 0]
    new_ent, new_ent_m, new_ent_v = adamw(ent_table, entity_first_moment, ent_v, scale * ent_grad.T)
    new_rel, new_rel_m, new_rel_v = adamw(
        rel_table, relation_first_moment, rel_v, scale * rel_grad[None]
    )
    return (
        loss_sum,
        total,
        grad_norm,
        new_ent,
        new_ent_m,
        new_ent_v,
        new_ent.astype(jnp.bfloat16),
        new_rel,
        new_rel_m,
        new_rel_v,
        new_rel.astype(jnp.bfloat16),
    )


def solution(mesh):
    body = cube_body if mesh.shape["rel"] == 4 and mesh.shape["ent"] == 8 else general_body
    return jax.shard_map(
        body,
        mesh=mesh,
        in_specs=(
            P("ent", None),
            P("ent", None),
            P("ent", None),
            P(None, ("rel", "ent"), None),
            P(None, ("rel", "ent"), None),
            P(None, ("rel", "ent"), None),
            P("rel", "ent", None, None),
            P("rel", "ent", None, None),
            P("rel", "ent", None, None),
            P("rel", "ent", None, None),
            P("rel", "ent", None),
        ),
        out_specs=(
            P(),
            P(),
            P(),
            P("ent", None),
            P("ent", None),
            P("ent", None),
            P("ent", None),
            P(None, ("rel", "ent"), None),
            P(None, ("rel", "ent"), None),
            P(None, ("rel", "ent"), None),
            P(None, ("rel", "ent"), None),
        ),
        check_vma=False,
    )
```
